32 devices in a mesh: ha: 8 (over y, x, core), wa: 4 (over z).
Axes of the slice: x: 2, y: 2, z: 4, core: 2. Of those that a mesh axis runs over, the one named last changes fastest.
Arguments:
- hw_plane: bfloat16 [256, 512, 128], P('ha', 'wa'), may hold values from -200 to 200
- zh_plane: bfloat16 [64, 256, 128], P(None, 'ha'), may hold values from -5 to 5
- wz_plane: bfloat16 [512, 64, 128], P('wa'), may hold values from -5 to 5
- w_in: bfloat16 [128, 256], replicated, may hold values from -0.5 to 0.5
- b_in: float32 [256], replicated, may hold values from -3 to 3
- w_out: bfloat16 [256, 18], replicated, may hold values from -0.75 to 0.75
- b_out: float32 [18], replicated, may hold values from -3 to 3
- run_index: int32 [32, 512], P(('ha', 'wa')), may hold values from 0 to 2047, as said below
- run_count: int32 [32], P(('ha', 'wa')), may hold values from 1 to 511, as said below
- labels: int32 [32, 512, 128], P(('ha', 'wa')), may hold values from 0 to 17
Outputs:
- hw_grad: float32 [256, 512, 128], P('ha', 'wa')
- zh_grad: float32 [64, 256, 128], P('wa', 'ha')
- wz_grad: float32 [512, 64, 128], P('wa', 'ha')
- w_in_grad: float32 [128, 256], replicated
- b_in_grad: float32 [256], replicated
- w_out_grad: float32 [256, 18], replicated
- b_out_grad: float32 [18], replicated
The draws below stay inside these ranges and needn't reach their ends.
Inputs may be any that keep to these rules, and one draw needn't show every extreme that they name: `run_index`: each row holds 512 different run positions of one device block. `run_count`: the counts of block k and of block k + 8 * 4 / 2 (ha index differing by 4) sum to exactly 512.
All inputs are finite; a program needn't handle non-finite values.
Results may differ from the reference program's by a relative error of at most 0.00055.
The reference program's roundings to bfloat16 on the way (of `features`, `hidden`, `dlogits` and `dpreact`) count: a program that leaves them out, or rounds other values in their place, can miss the bound.
Values may be sent and summed in bfloat16 or wider, within the bound.
No kernel may reach another device: no remote copies, remote signals or barrier semaphores. Data moves between devices by JAX's collectives and lax.ppermute only.
A program may use at most 192 MiB of HBM per device.

```python
import jax
import jax.numpy as jnp
from jax import lax

C = 128
HID = 256
NCLS = 18
Z = 64
HB = 32
WB = 128
RUN = 128
CAP = 512
H = 256
W = 512
N_HA = 8
N_WA = 4


def draw_hw_plane(key, part):
    key = jax.random.fold_in(key, 11)
    draws = jnp.clip(jax.random.normal(key, (H, W, C), jnp.float32), -4.0, 4.0)
    return draws.astype(jnp.bfloat16)


def draw_run_index(key, part):
    key = jax.random.fold_in(key, 7)
    device_keys = jax.random.split(key, N_HA * N_WA)
    picked = jax.vmap(lambda one_key: jax.random.permutation(one_key, HB * WB // 2)[:CAP])(device_keys)
    return picked.astype(jnp.int32)


def draw_run_count(key, part):
    key = jax.random.fold_in(key, 5)
    lower_counts = jax.random.randint(key, (N_HA * N_WA // 2,), 1, CAP, dtype=jnp.int32)
    lower_counts = lower_counts.at[0].set(CAP - 1)
    return jnp.concatenate([lower_counts, CAP - lower_counts]).astype(jnp.int32)


def set_ends(result, stream_key, low, largest):
    shape = result.shape
    spot = [jax.random.randint(jax.random.fold_in(stream_key, axis), (), 0, shape[axis]) for axis in range(len(shape))]
    result = result.at[tuple(spot)].set(low)
    longest = shape.index(max(shape))
    spot[longest] = (spot[longest] + 1) % shape[longest]
    return result.at[tuple(spot)].set(largest)


def block_levels(key, extent, shards, low, high):
    level = 1.0
    for position, parts in shards:
        steps = jax.random.uniform(jax.random.fold_in(jax.random.fold_in(key, 6), position), (parts,), jnp.float32, low / len(shards), high / len(shards))
        level = level * jnp.repeat(jnp.exp(steps), extent[position] // parts).reshape((-1,) + (1,) * (len(extent) - 1 - position))
    return level


def normal_values(stream_key, shape, width, most, pieces=(), kind=jnp.bfloat16):
    array = jax.random.normal(stream_key, shape, jnp.float32) * width
    if len(pieces) > 0:
        array = block_levels(stream_key, shape, pieces, -0.22, 0.18) * array
    return jnp.clip(array, min=-most, max=most).astype(kind)


def setup_inputs(seed: int = 0) -> dict:
    seeds = jax.random.split(jax.random.key(seed), 11)
    hw_plane = draw_hw_plane(jax.random.fold_in(seeds[10], 71), 0)
    zh_plane = normal_values(seeds[1], (Z, H, C), 1.0, 5.0, ((1, 8),))
    wz_plane = normal_values(seeds[2], (W, Z, C), 1.0, 5.0, ((0, 4),))
    w_in = normal_values(seeds[3], (C, HID), C ** -0.5, 0.5)
    b_in = normal_values(seeds[4], (HID,), 0.5, 3.0, (), jnp.float32)
    w_out = normal_values(seeds[5], (HID, NCLS), (HID // 4) ** -0.5, 0.75)
    b_out = normal_values(seeds[6], (NCLS,), 0.5, 3.0, (), jnp.float32)
    run_index = draw_run_index(jax.random.fold_in(seeds[10], 71), 0)
    run_count = draw_run_count(jax.random.fold_in(seeds[10], 71), 0)
    labels = set_ends(jax.random.randint(seeds[9], (N_HA * N_WA, CAP, RUN), 0, NCLS), jax.random.fold_in(seeds[9], 1), 0, NCLS - 1).astype(jnp.int32)
    return dict(hw_plane=hw_plane, zh_plane=zh_plane, wz_plane=wz_plane, w_in=w_in, b_in=b_in, w_out=w_out, b_out=b_out, run_index=run_index, run_count=run_count, labels=labels)


grad_scale = 0.25


def silu_slope(preact):
    sigmoid_val = jax.nn.sigmoid(preact)
    return sigmoid_val * (1.0 + preact * (1.0 - sigmoid_val))


def contract_rows(left, right):
    return lax.dot_general(left, right, (((0,), (0,)), ((), ())), preferred_element_type=jnp.float32)


def contract_cols(left, right):
    return lax.dot_general(left, right, (((1,), (1,)), ((), ())), preferred_element_type=jnp.float32)


def sample_grads(features, labels_flat, validity, w_in, b_in, w_out, b_out):
    preact = jnp.dot(features, w_in, preferred_element_type=jnp.float32) + b_in
    hidden = jax.nn.silu(preact).astype(jnp.bfloat16)
    logits = jnp.dot(hidden, w_out, preferred_element_type=jnp.float32) + b_out
    row_top = jnp.max(logits, axis=1, keepdims=True)
    scores_exp = jnp.exp(logits - row_top)
    probability = scores_exp / jnp.sum(scores_exp, axis=1, keepdims=True)
    classes = jnp.arange(logits.shape[1], dtype=jnp.int32)
    onehot = (labels_flat[:, None] == classes[None, :]).astype(jnp.float32)
    dlogits = ((probability - onehot) * (grad_scale * validity[:, None])).astype(jnp.bfloat16)
    grad_w_out = contract_rows(hidden, dlogits)
    grad_b_out = jnp.sum(dlogits.astype(jnp.float32), axis=0)
    dhidden = contract_cols(dlogits, w_out)
    dpreact = (dhidden * silu_slope(preact)).astype(jnp.bfloat16)
    grad_w_in = contract_rows(features, dpreact)
    grad_b_in = jnp.sum(dpreact.astype(jnp.float32), axis=0)
    dfeatures = contract_cols(dpreact, w_in)
    return dfeatures, (grad_w_in, grad_b_in, grad_w_out, grad_b_out)


def run_features(hw_block, zh_rows, wz_block, run_ids):
    rows_blk, cols_blk, channels = hw_block.shape
    pair_cols = cols_blk // 2
    depth_z = wz_block.shape[1]
    run_row = run_ids // pair_cols
    run_pair = run_ids % pair_cols
    hw_part = hw_block.reshape(rows_blk * pair_cols, 2, channels)[run_ids].astype(jnp.float32)
    zh_part = zh_rows[run_row].astype(jnp.float32)
    wz_part = wz_block.reshape(pair_cols, 2, depth_z, channels)[run_pair].astype(jnp.float32)
    summed = hw_part[:, :, None, :] + zh_part[:, None, :, :] + wz_part
    return summed.astype(jnp.bfloat16)


def plane_grads(dfeatures, run_ids, rows_blk, cols_blk):
    slot_count, pair_count, depth_z, channels = dfeatures.shape
    pair_cols = cols_blk // 2
    run_row = run_ids // pair_cols
    run_pair = run_ids % pair_cols
    hw_local = jnp.zeros((rows_blk * pair_cols, 2, channels), jnp.float32)
    hw_local = hw_local.at[run_ids].add(jnp.sum(dfeatures, axis=2)).reshape(rows_blk, cols_blk, channels)
    zh_rows_grad = jnp.zeros((rows_blk, depth_z, channels), jnp.float32).at[run_row].add(jnp.sum(dfeatures, axis=1))
    zh_local = jnp.transpose(zh_rows_grad, (1, 0, 2))
    wz_local = jnp.zeros((pair_cols, 2, depth_z, channels), jnp.float32).at[run_pair].add(dfeatures)
    return hw_local, zh_local, wz_local.reshape(cols_blk, depth_z, channels)


def reference(hw_plane, zh_plane, wz_plane, w_in, b_in, w_out, b_out, run_index, run_count, labels):
    channels = hw_plane.shape[2]
    zh_all = jnp.transpose(zh_plane, (1, 0, 2))
    zero_init = (jnp.zeros(hw_plane.shape, jnp.float32), jnp.zeros(zh_plane.shape, jnp.float32),
                 jnp.zeros(wz_plane.shape, jnp.float32), jnp.zeros(w_in.shape, jnp.float32),
                 jnp.zeros(b_in.shape, jnp.float32), jnp.zeros(w_out.shape, jnp.float32),
                 jnp.zeros(b_out.shape, jnp.float32))
    slot_ids = jnp.arange(CAP, dtype=jnp.int32)

    def device_step(totals, device):
        row_start = ((device // N_WA) * HB).astype(jnp.int32)
        col_start = ((device % N_WA) * WB).astype(jnp.int32)
        zero_idx = jnp.zeros((), jnp.int32)
        hw_block = lax.dynamic_slice(hw_plane, (row_start, col_start, zero_idx), (HB, WB, channels))
        zh_rows = lax.dynamic_slice(zh_all, (row_start, zero_idx, zero_idx), (HB, Z, channels))
        wz_block = lax.dynamic_slice(wz_plane, (col_start, zero_idx, zero_idx), (WB, Z, channels))
        run_ids = run_index[device]
        features = run_features(hw_block, zh_rows, wz_block, run_ids)
        validity = jnp.repeat((slot_ids < run_count[device]).astype(jnp.float32), RUN)
        dfeat_flat, weight_grads = sample_grads(features.reshape(CAP * RUN, channels),
                                                labels[device].reshape(CAP * RUN), validity,
                                                w_in, b_in, w_out, b_out)
        hw_local, zh_local, wz_local = plane_grads(dfeat_flat.reshape(CAP, 2, Z, channels), run_ids, HB, WB)
        hw_total = lax.dynamic_update_slice(totals[0], hw_local, (row_start, col_start, zero_idx))
        zh_now = lax.dynamic_slice(totals[1], (zero_idx, row_start, zero_idx), (Z, HB, channels))
        zh_total = lax.dynamic_update_slice(totals[1], zh_now + zh_local, (zero_idx, row_start, zero_idx))
        wz_now = lax.dynamic_slice(totals[2], (col_start, zero_idx, zero_idx), (WB, Z, channels))
        wz_total = lax.dynamic_update_slice(totals[2], wz_now + wz_local, (col_start, zero_idx, zero_idx))
        return (hw_total, zh_total, wz_total, totals[3] + weight_grads[0], totals[4] + weight_grads[1],
                totals[5] + weight_grads[2], totals[6] + weight_grads[3]), None

    totals, ignored = lax.scan(device_step, zero_init, jnp.arange(N_HA * N_WA, dtype=jnp.int32))
    return (totals[0], totals[1], totals[2], totals[3], totals[4], totals[5], totals[6])
```

```python
import functools

import jax
import jax.numpy as jnp
from jax import lax
from jax.experimental import pallas as pl
from jax.experimental.pallas import tpu as pltpu
from jax.sharding import PartitionSpec as P

grad_scale = 0.25
CLS_ROWS = 24
CLS_PAD = 32
CHUNKS = ((0, 3), (1, 2))
ZC = 16
RUNS = 32
GROUP = 4
ROWS = RUNS * 2 * ZC
STRIP = 32
LEVEL_TOPS = tuple(2.0 ** e for e in (4, -7, -18, -29, -40))
LEVEL_BITS = (11, 22, 33, 44, 55)
CODE_ROWS = 16


def ppermute_xor(value, axis, size, mask):
    return lax.ppermute(value, axis, [(i, i ^ mask) for i in range(size)])


def fill_planes(side, refs, bases, zh_full, lab_pad, start, *, half, rows_blk, depth_z, slots):
    n_zh = rows_blk * ZC
    n_lab = slots // GROUP
    lane = lax.rem(lax.broadcasted_iota(jnp.int32, (n_lab, 128), 1), depth_z)
    z0 = side * half
    labs = [lab_pad[pl.ds(start + par, n_lab, stride=GROUP), :] for par in range(GROUP)]
    for chunk, ref, base in zip(CHUNKS, refs, bases):
        if ref is None:
            continue
        for h in range(rows_blk):
            parts = [zh_full[pl.ds((z0 + 8 * o) * rows_blk + h, 8, stride=rows_blk), :] for o in chunk]
            ref[base + h * ZC:base + (h + 1) * ZC, :] = jnp.concatenate(parts, axis=0).astype(jnp.bfloat16)
        merged = jnp.zeros((n_lab, 128), jnp.float32)
        for par in range(GROUP):
            for n, o in enumerate(chunk):
                to = par * ZC + 8 * n
                rolled = pltpu.roll(labs[par], jnp.bitwise_and(256 + to - (z0 + 8 * o), 127), 1)
                merged = jnp.where((lane >= to) & (lane < to + 8), rolled, merged)
        ref[base + n_zh:base + n_zh + n_lab, :] = merged.astype(jnp.bfloat16)


def load_inputs(hw_ref, zh_ref, lab_ref, ids_ref, hw_raw, zh_raw, lab_raw, ids_raw, rid_ref, sems,
                hw_full, zh_full, lab_pad, slots):
    copies = [pltpu.make_async_copy(a, b, sems.at[n]) for n, (a, b) in enumerate(
        ((hw_ref, hw_raw), (ids_ref, rid_ref), (ids_ref, ids_raw), (zh_ref, zh_raw), (lab_ref, lab_raw)))]
    for copy in copies:
        copy.start()
    for copy in copies:
        copy.wait()
    hw_full[...] = hw_raw[...].astype(jnp.float32)
    zh_full[...] = zh_raw[...].astype(jnp.float32)
    lab_pad[0:slots, :] = jnp.zeros((slots, lab_raw.shape[1]), jnp.float32)
    lab_pad[slots:, :] = lab_raw[...].astype(jnp.float32)
    ids = [ids_raw[:, k * 128:(k + 1) * 128] for k in range(slots // 128)]
    return jnp.concatenate(ids + ids, axis=0)


def gather_rows(rid_ref, hw_full, hw_rows, slots, shift):
    def gather_step(i, carry):
        for j in range(8):
            s = i * 8 + j
            r = rid_ref[0, jnp.maximum(s - shift, 0)]
            for p in range(2):
                hw_rows[pl.ds(2 * s + p, 1), :] = hw_full[pl.ds(2 * r + p, 1), :]
        return carry

    lax.fori_loop(0, slots // 8, gather_step, 0)


def put_ids(ref, base, ids, shift_bits, keep):
    padded = jnp.concatenate([ids, jnp.zeros_like(ids)], axis=0)
    high = lax.shift_right_logical(padded, shift_bits)
    low = jnp.bitwise_and(padded, keep)
    row = lax.broadcasted_iota(jnp.int32, padded.shape, 0)
    both = jnp.where(row < 4, high, pltpu.roll(low, 4, 0))
    ref[base:base + 16, :] = both.astype(jnp.float32).astype(jnp.bfloat16)


def pack_send_kernel(meta_ref, hw_ref, zh_ref, lab_ref, ids_ref, send_ref,
                     hw_raw, zh_raw, lab_raw, ids_raw, rid_ref, sems,
                     hw_full, hw_rows, zh_full, lab_pad, *, depth_z, rows_blk, slots, pair_cols):
    half = depth_z // 2
    n_hw = 2 * slots
    count = meta_ref[1]
    ids = load_inputs(hw_ref, zh_ref, lab_ref, ids_ref, hw_raw, zh_raw, lab_raw, ids_raw, rid_ref, sems,
                      hw_full, zh_full, lab_pad, slots)
    gather_rows(rid_ref, hw_full, hw_rows, slots, slots - count)
    send_ref[0:n_hw, :] = hw_rows[...].astype(jnp.bfloat16)
    down = slots - count
    lanes = jnp.bitwise_and(down, 127)
    rows = lax.shift_right_logical(down, 7)
    turned = pltpu.roll(ids, lanes, 1)
    here = pltpu.roll(turned, rows, 0)
    before = pltpu.roll(turned, jnp.bitwise_and(rows + 1, 7), 0)
    lane = lax.broadcasted_iota(jnp.int32, ids.shape, 1)
    put_ids(send_ref, n_hw, jnp.where(lane < lanes, before, here), pair_cols.bit_length() - 1, pair_cols - 1)
    fill_planes(1 - meta_ref[0], (send_ref, None), (n_hw + 16, 0), zh_full, lab_pad, count,
                half=half, rows_blk=rows_blk, depth_z=depth_z, slots=slots)


def pack_own_kernel(meta_ref, hw_ref, zh_ref, lab_ref, ids_ref, wz_ref,
                    own0_ref, own1_ref, send1_ref, wz0_ref, wz1_ref,
                    hw_raw, zh_raw, lab_raw, ids_raw, rid_ref, sems,
                    hw_full, hw_rows, zh_full, lab_pad, wz_raw, wz_sem,
                    *, depth_z, rows_blk, slots, pair_cols):
    half = depth_z // 2
    n_hw = 2 * slots
    z0 = pl.multiple_of(meta_ref[0] * half, half)
    wz_copy = pltpu.make_async_copy(wz_ref.at[:, pl.ds(z0, half), :], wz_raw, wz_sem)
    wz_copy.start()
    ids = load_inputs(hw_ref, zh_ref, lab_ref, ids_ref, hw_raw, zh_raw, lab_raw, ids_raw, rid_ref, sems,
                      hw_full, zh_full, lab_pad, slots)
    gather_rows(rid_ref, hw_full, hw_rows, slots, 0)
    own0_ref[0:n_hw, :] = hw_rows[...].astype(jnp.bfloat16)
    put_ids(own0_ref, n_hw, ids, pair_cols.bit_length() - 1, pair_cols - 1)
    fill_planes(meta_ref[0], (own0_ref, own1_ref), (n_hw + 16, 0), zh_full, lab_pad, slots,
                half=half, rows_blk=rows_blk, depth_z=depth_z, slots=slots)
    fill_planes(1 - meta_ref[0], (None, send1_ref), (0, 0), zh_full, lab_pad, meta_ref[1],
                half=half, rows_blk=rows_blk, depth_z=depth_z, slots=slots)
    wz_copy.wait()

    def widen(w, carry):
        rows = wz_raw[w].astype(jnp.float32)
        for chunk, ref in zip(CHUNKS, (wz0_ref, wz1_ref)):
            for n, o in enumerate(chunk):
                ref[w, 8 * n:8 * n + 8, :] = rows[8 * o:8 * o + 8]
        return carry

    lax.fori_loop(0, 2 * pair_cols, widen, 0, unroll=8)


def run_slices(dfeat_ref, j, base=0):
    g, par = j // GROUP, j % GROUP
    at = [base + g * 128 + p * 64 + par * ZC for p in range(2)]
    return [dfeat_ref[pl.ds(at[p], ZC), :] for p in range(2)]


def add_zh(d, row, zh_accs):
    both = d[0] + d[1]
    now = [acc[row] for acc in zh_accs]
    for n, acc in enumerate(zh_accs):
        acc[row] = now[n] + both[8 * n:8 * n + 8]


def add_wz(d, col, wz_accs):
    now = [[acc[col + p] for p in range(2)] for acc in wz_accs]
    for n, acc in enumerate(wz_accs):
        for p in range(2):
            acc[col + p] = now[n][p] + d[p][8 * n:8 * n + 8]


def pick_level(top):
    level = jnp.zeros(top.shape, jnp.float32)
    for n, bound in enumerate(LEVEL_TOPS):
        level = jnp.where(top < bound, n + 1.0, level)
    return level


def level_scale(level, sign):
    scale = jnp.ones(level.shape, jnp.float32)
    for n in range(len(LEVEL_TOPS)):
        scale = jnp.where(level == n + 1.0, 2.0 ** (sign * LEVEL_BITS[n]), scale)
    return scale


def encode(value):
    level = pick_level(jnp.max(jnp.abs(value), axis=1, keepdims=True))
    code = jnp.broadcast_to(level, (value.shape[0], CODE_ROWS, value.shape[2]))
    return jnp.concatenate([value * level_scale(level, 1), code], axis=1).astype(jnp.float16)


def decode_half(value):
    value = value.astype(jnp.float32)
    n = value.shape[1] - CODE_ROWS
    return value[:, :n] * level_scale(value[:, n:n + 1, :], -1)


def read_runs(ids_ref, first, n):
    row = lax.shift_right_logical(first, 7)
    at = jnp.bitwise_and(first, 127)
    return [(ids_ref[row, at + j], ids_ref[row + 4, at + j]) for j in range(n)]


def decode_kernel(*refs, chunk, first, rows_blk, slots, pair_cols):
    n_hw = 2 * slots
    n_zh = rows_blk * ZC
    n_lab = slots // GROUP
    meta_ref, hw_own, hw_recv = refs[:3]
    refs = refs[3:]
    if first:
        z_own, z_recv, z_base = hw_own, hw_recv, n_hw + 16
    else:
        z_own, z_recv, z_base = refs[0], refs[1], 0
        hw_prev, wgt_prev = refs[2:4]
        refs = refs[4:]
    wz_full, w_in_ref, w_in_t_ref, b_in_ref, w_out_t_ref, w_out_half_ref, b_out_ref, sel_ref = refs[:8]
    refs = refs[8:]
    if first:
        wz_out0, wz_out1, zh_out0, zh_out1, hw_out, wgt_out = refs[:6]
        refs = refs[6:]
    else:
        wz_out0, core_out, zh_out0, zh_out1, hw_out, wgt_keep = refs[:6]
        refs = refs[6:]
    (hw_full, zh_full, lab_full, hw_acc, w_in_acc, w_out_acc, b_out_acc, ids_ref, ids_sem) = refs[:9]
    bufs = (refs[9:14], refs[14:19])
    outs = (refs[19:22], refs[22:25])
    dfeat_ref = refs[25]
    wz_accs, zh_accs, ids_vec, wgt_all = refs[26:28], refs[28:30], refs[30], refs[31]
    count = meta_ref[1]
    rel_own = meta_ref[7]

    spot_row = lax.broadcasted_iota(jnp.int32, (8, 128), 0)
    spot = jnp.bitwise_and(spot_row, 3) * 128 + lax.broadcasted_iota(jnp.int32, (8, 128), 1)
    own_ids = hw_own[n_hw:n_hw + 16, :].astype(jnp.float32).astype(jnp.int32)
    recv_ids = hw_recv[n_hw:n_hw + 16, :].astype(jnp.float32).astype(jnp.int32)
    is_own = spot < count
    ids = jnp.where(is_own, own_ids[0:8], recv_ids[0:8])
    rel = jnp.where(is_own, rel_own, 1 - rel_own)
    ids_vec[...] = jnp.where(spot_row < 4, ids + rel * rows_blk, 2 * ids)
    copy = pltpu.make_async_copy(ids_vec, ids_ref, ids_sem)
    copy.start()
    row = lax.broadcasted_iota(jnp.int32, (n_hw, 128), 0)
    hw_full[...] = jnp.where(row < 2 * count, hw_own[0:n_hw, :].astype(jnp.float32),
                             hw_recv[0:n_hw, :].astype(jnp.float32))
    for k, ref in ((0, z_own), (1, z_recv)):
        base = jnp.bitwise_xor(rel_own, k) * rows_blk
        for h in range(rows_blk):
            zh_full[base + h] = ref[z_base + h * ZC:z_base + (h + 1) * ZC, :].astype(jnp.float32)
    lab_row = lax.broadcasted_iota(jnp.int32, (n_lab, 128), 0)
    lab_lane = lax.broadcasted_iota(jnp.int32, (n_lab, 128), 1)
    place = GROUP * lab_row + lax.rem(lab_lane // ZC, GROUP)
    first_lab = z_base + n_zh
    lab_full[...] = jnp.where(place < count, z_own[first_lab:first_lab + n_lab, :].astype(jnp.float32),
                              z_recv[first_lab:first_lab + n_lab, :].astype(jnp.float32))
    for acc in wz_accs + zh_accs:
        acc[...] = jnp.zeros_like(acc)
    w_in_acc[...] = jnp.zeros_like(w_in_acc)
    w_out_acc[...] = jnp.zeros_like(w_out_acc)
    b_out_acc[...] = jnp.zeros_like(b_out_acc)
    copy.wait()

    groups = RUNS // GROUP
    n_ch = w_in_ref.shape[0]
    for left_ref, dhid_ref, dpre_ref in outs:
        left_ref[n_ch:, :] = sel_ref[...]
    class_ids = lax.broadcasted_iota(jnp.int32, (CLS_ROWS, 128), 0).astype(jnp.float32)
    nt = (((1,), (1,)), ((), ()))

    def front(b, buf):
        feat_ref, hid_ref, slope_ref, logit_ref, pre_ref = buf
        pieces = []
        runs = read_runs(ids_ref, RUNS * b, RUNS)
        for g in range(groups):
            for p in range(2):
                for par in range(GROUP):
                    row, col = runs[GROUP * g + par]
                    at = pl.multiple_of(2 * RUNS * b, 2 * RUNS) + 2 * (GROUP * g + par) + p
                    total = hw_full[pl.ds(at, 1), :] + zh_full[row] + wz_full[col + p]
                    pieces.append(total.astype(jnp.bfloat16))
        feat = jnp.concatenate(pieces, axis=0)
        feat_ref[...] = feat
        pre_ref[...] = jnp.dot(feat, w_in_ref[...], preferred_element_type=jnp.float32)
        for r in range(0, ROWS, STRIP):
            pre = pre_ref[r:r + STRIP, :] + b_in_ref[...]
            t = jnp.tanh(pre)
            a = 1.0 + t
            u = pre * a
            hid_ref[r:r + STRIP, :] = u.astype(jnp.bfloat16)
            slope_ref[r:r + STRIP, :] = a + u * (1.0 - t)
        logits = lax.dot_general(w_out_t_ref[...], hid_ref[...], nt, preferred_element_type=jnp.float32)
        logit_ref[...] = logits[0:CLS_ROWS, :]

    def middle(b, buf, out):
        feat_ref, hid_ref, slope_ref, logit_ref, pre_ref = buf
        left_ref, dhid_ref, dpre_ref = out
        left_ref[0:n_ch, :] = jnp.transpose(feat_ref[...], (1, 0))
        dl_tiles = []
        b_part = None
        for g in range(groups):
            tile = logit_ref[:, g * 128:(g + 1) * 128] + b_out_ref[...]
            top = jnp.max(tile, axis=0, keepdims=True)
            e = jnp.exp(tile - top)
            inv = 1.0 / jnp.sum(e, axis=0, keepdims=True)
            lab_here = lab_full[pl.ds(groups * b + g, 1), :]
            onehot = jnp.where(class_ids == lab_here, 1.0, 0.0)
            dl = ((e * inv - onehot) * grad_scale).astype(jnp.bfloat16).astype(jnp.float32)
            b_part = dl if b_part is None else b_part + dl
            dl_tiles.append(dl)
        b_out_acc[...] += b_part
        dl_all = jnp.concatenate(dl_tiles, axis=1)
        dl_all = jnp.concatenate([dl_all, jnp.zeros((CLS_PAD - CLS_ROWS, ROWS), jnp.float32)], axis=0)
        dl_t = jnp.transpose(dl_all, (1, 0)).astype(jnp.bfloat16)
        w_out_acc[...] += jnp.dot(dl_all.astype(jnp.bfloat16), hid_ref[...], preferred_element_type=jnp.float32)
        dhid_ref[...] = jnp.dot(dl_t, w_out_half_ref[...], preferred_element_type=jnp.float32)
        for r in range(0, ROWS, STRIP):
            dpre_ref[r:r + STRIP, :] = (dhid_ref[r:r + STRIP, :] * slope_ref[r:r + STRIP, :]).astype(jnp.bfloat16)

    def back(b, out):
        left_ref, dhid_ref, dpre_ref = out
        dpre = dpre_ref[...]
        sums = jnp.dot(left_ref[...], dpre, preferred_element_type=jnp.float32)
        w_in_acc[...] += sums[0:n_ch]
        hw_acc[pl.ds(pl.multiple_of(2 * RUNS * b, 2 * RUNS), 2 * RUNS), :] = sums[n_ch:]
        dfeat_ref[...] = jnp.dot(dpre, w_in_t_ref[...], preferred_element_type=jnp.float32)
        runs = read_runs(ids_ref, RUNS * b, RUNS)
        for j in range(RUNS):
            d = run_slices(dfeat_ref, j)
            add_zh(d, runs[j][0], zh_accs)
            add_wz(d, runs[j][1], wz_accs)

    n_batch = slots // RUNS
    front(0, bufs[0])
    front(1, bufs[1])
    middle(0, bufs[0], outs[0])

    def step(k, carry):
        b = 2 * k
        front(b + 2, bufs[0])
        middle(b + 1, bufs[1], outs[1])
        back(b, outs[0])
        front(b + 3, bufs[1])
        middle(b + 2, bufs[0], outs[0])
        back(b + 1, outs[1])
        return carry

    lax.fori_loop(0, n_batch // 2 - 1, step, 0)
    middle(n_batch - 1, bufs[1], outs[1])
    back(n_batch - 2, outs[0])
    back(n_batch - 1, outs[1])
    tail = hw_acc[...]
    total = None
    for n in range(3):
        part = tail.astype(jnp.bfloat16)
        tail = tail - part.astype(jnp.float32)
        term = jnp.dot(part, w_in_t_ref[...], preferred_element_type=jnp.float32)
        total = term if total is None else total + term
    width = w_in_acc.shape[1]
    b_in_sum = jnp.sum(hw_acc[...], axis=0, keepdims=True)
    b_pad = jnp.concatenate([b_out_acc[...], jnp.zeros((128 - CLS_ROWS, 128), jnp.float32)], axis=0)
    b_out_sum = jnp.sum(jnp.transpose(b_pad, (1, 0)), axis=0, keepdims=True)
    b_out_sum = jnp.concatenate([b_out_sum, jnp.zeros((1, width - 128), jnp.float32)], axis=1)
    biases = jnp.concatenate([b_in_sum, b_out_sum, jnp.zeros((6, width), jnp.float32)], axis=0)
    weights = jnp.concatenate([w_in_acc[...], biases, w_out_acc[0:CLS_ROWS, :]], axis=0)
    put_zh(meta_ref, chunk, zh_accs, zh_out0, zh_out1)
    if first:
        hw_out[...] = total
        wgt_out[...] = weights
        put_wz(meta_ref, chunk, wz_accs, wz_out0, wz_out1)
        return
    hw_out[...] = total + hw_prev[...]
    wgt_all[...] = weights + wgt_prev[...]
    put_wz(meta_ref, chunk, wz_accs, wz_out0, core_out.at[0:2 * pair_cols])
    mid = wgt_all.shape[0] // 2
    mine = meta_ref[8] * mid
    wgt_keep[...] = split_lanes(wgt_all[pl.ds(pl.multiple_of(mine, 8), mid), :])
    core_out[2 * pair_cols:] = split_lanes(wgt_all[pl.ds(pl.multiple_of(mid - mine, 8), mid), :])


def split_lanes(value):
    return jnp.concatenate([value[:, :128], value[:, 128:]], axis=0).reshape(value.shape[0] // 4, 8, 128)


def put_zh(meta_ref, chunk, zh_accs, zh_out0, zh_out1):
    same = meta_ref[6] == chunk[0] // 2
    zh_out0[...] = jnp.where(same, zh_accs[0][...], zh_accs[1][...])
    zh_out1[...] = jnp.where(same, zh_accs[1][...], zh_accs[0][...])


def put_wz(meta_ref, chunk, wz_accs, wz_out0, wz_out1):
    same = meta_ref[2 + chunk[0]] == 0
    wz_out0[...] = jnp.where(same, wz_accs[0][...], wz_accs[1][...])
    wz_out1[...] = jnp.where(same, wz_accs[1][...], wz_accs[0][...])


def place_kernel(meta_ref, rid_ref, mine_ref, recv_ref, out_ref, *, slots):
    out_ref[...] = jnp.zeros_like(out_ref)
    count = meta_ref[1]

    def place(s, carry):
        r = rid_ref[0, s]
        for p in range(2):
            out_ref[pl.ds(2 * r + p, 1), :] = (mine_ref[pl.ds(2 * s + p, 1), :]
                                               + recv_ref[pl.ds(2 * (slots - count + s) + p, 1), :])
        return carry

    def place_eight(i, carry):
        for j in range(8):
            place(8 * i + j, carry)
        return carry

    lax.fori_loop(0, count // 8, place_eight, 0)
    lax.fori_loop(count // 8 * 8, count, place, 0)


def finish_kernel(meta_ref, zh0_ref, zh1_ref, w_mine_ref, w_other_ref,
                  zh_out, w_in_out, b_in_out, w_out_out, b_out_out, w_all, *, rows_blk):
    mid = w_all.shape[0] // 2
    mine = meta_ref[8] * mid
    for start, ref in ((mine, w_mine_ref), (mid - mine, w_other_ref)):
        flat = ref[...].reshape(2 * mid, 128)
        w_all[pl.ds(pl.multiple_of(start, 8), mid), :] = jnp.concatenate([flat[:mid], flat[mid:]], axis=1)
    n_ch = w_in_out.shape[0]
    w_in_out[...] = w_all[0:n_ch, :]
    b_in_out[...] = w_all[n_ch:n_ch + 1, :]
    b_out_out[...] = w_all[n_ch + 1:n_ch + 2, 0:b_out_out.shape[1]]
    w_out_out[...] = w_all[n_ch + 8:n_ch + 8 + w_out_out.shape[0], :]
    swapped = meta_ref[6]
    for n, ref in ((0, zh0_ref), (1, zh1_ref)):
        base = jnp.bitwise_xor(swapped, n) * 8
        for z in range(8):
            zh_out[base + z] = ref[pl.ds(z, rows_blk, stride=8), :]


def local(n_ha, n_wa, hw_plane, zh_plane, wz_plane, w_in, b_in, w_out, b_out,
          run_index, run_count, labels):
    rows_blk, cols_blk, channels = hw_plane.shape
    depth_z = zh_plane.shape[0]
    hidden = w_in.shape[1]
    classes = w_out.shape[1]
    slots = run_index.shape[1]
    half = depth_z // 2
    pair_cols = cols_blk // 2
    n_q = n_ha // 2
    n_zl = n_wa // 2
    n_hw = 2 * slots
    n_zh = rows_blk * ZC
    n_lab = slots // GROUP
    smem = pl.BlockSpec(memory_space=pltpu.SMEM)
    vmem = pl.BlockSpec(memory_space=pltpu.VMEM)
    hbm = pl.BlockSpec(memory_space=pltpu.HBM)
    f32 = jnp.float32
    bf16 = jnp.bfloat16

    ha = lax.axis_index("ha")
    wa = lax.axis_index("wa")
    y = ha // n_q
    my_q = ha % n_q
    b1 = wa // n_zl
    my_zl = wa % n_zl
    count = run_count[0]
    direct = n_q == 4 and n_zl == 2
    if direct:
        wz_pos = [(o ^ my_q) % 2 for o in range(4)]
        rest = [my_zl, y ^ b1, ha % 2, my_q]
    else:
        wz_pos = [jnp.int32(o // 2) for o in range(4)]
        rest = [jnp.int32(0), y, ha % 2, my_q]
    meta = jnp.stack([y, count] + wz_pos + rest).astype(jnp.int32)
    swap_y = [(i, (i + n_q) % n_ha) for i in range(n_ha)]

    pack_rows = (n_hw + 16 + n_zh + n_lab, n_zh + n_lab)
    planes = (hw_plane.reshape(rows_blk * cols_blk, channels),
              zh_plane.reshape(depth_z * rows_blk, channels), labels[0], run_index)
    raw = [pltpu.VMEM((rows_blk * cols_blk, channels), bf16), pltpu.VMEM((depth_z * rows_blk, channels), bf16),
           pltpu.VMEM((slots, 2 * depth_z), jnp.int32), pltpu.VMEM((1, slots), jnp.int32),
           pltpu.SMEM((1, slots), jnp.int32), pltpu.SemaphoreType.DMA((5,)),
           pltpu.VMEM((rows_blk * cols_blk, channels), f32), pltpu.VMEM((n_hw, channels), f32),
           pltpu.VMEM((depth_z * rows_blk, channels), f32), pltpu.VMEM((2 * slots, 2 * depth_z), f32)]

    def call(kernel, name, operands, specs, outs, scratch, flops, limit=16):
        return pl.pallas_call(
            kernel,
            out_shape=[jax.ShapeDtypeStruct(shape, kind) for shape, kind in outs],
            in_specs=specs,
            out_specs=[vmem] * len(outs),
            scratch_shapes=scratch,
            compiler_params=pltpu.CompilerParams(vmem_limit_bytes=limit * 2**20),
            cost_estimate=pl.CostEstimate(flops=flops, bytes_accessed=2**20, transcendentals=0),
            name=name,
        )(*operands)

    sizes = dict(depth_z=depth_z, rows_blk=rows_blk, slots=slots, pair_cols=pair_cols)
    send0, = call(functools.partial(pack_send_kernel, **sizes), "pack_send", (meta,) + planes,
                  [smem] + [hbm] * 4, [((pack_rows[0], channels), bf16)], raw, 3 * 10**9, 60)
    recv0 = lax.ppermute(send0, "ha", swap_y)
    later = lax.optimization_barrier((send0, w_in, b_in, w_out, b_out) + planes)
    w_in, b_in, w_out, b_out = later[1:5]
    own0, own1, send1, wzf0, wzf1 = call(
        functools.partial(pack_own_kernel, **sizes), "pack_own", (meta,) + later[5:] + (wz_plane,),
        [smem] + [hbm] * 5,
        [((pack_rows[0], channels), bf16), ((pack_rows[1], channels), bf16), ((pack_rows[1], channels), bf16),
         ((cols_blk, ZC, channels), f32), ((cols_blk, ZC, channels), f32)],
        raw + [pltpu.VMEM((cols_blk, half, channels), bf16), pltpu.SemaphoreType.DMA], 3 * 10**9)
    send1, recv0 = lax.optimization_barrier((send1, recv0))
    recv1 = lax.ppermute(send1, "ha", swap_y)

    w_in_half = (w_in.astype(f32) * 0.5).astype(bf16)
    w_out_half = jnp.pad((w_out.astype(f32) * 0.5).astype(bf16).T, ((0, CLS_PAD - classes), (0, 0)))
    w_out_t = jnp.pad(w_out.T, ((0, CLS_PAD - classes), (0, 0)))
    b_out_rows = jnp.broadcast_to(
        jnp.pad(b_out, (0, CLS_ROWS - classes), constant_values=-1e30)[:, None], (CLS_ROWS, 128))
    spot = jnp.arange(ROWS)
    run_of = (spot // 128) * GROUP + (spot % 64) // ZC
    select = (jnp.arange(2 * RUNS)[:, None] == (2 * run_of + (spot // 64) % 2)[None, :]).astype(bf16)
    w_in_t = w_in.T
    shared = (w_in_half, w_in_t, (b_in * 0.5).reshape(1, hidden), w_out_t, w_out_half, b_out_rows, select)
    wgt_rows = channels + 8 + CLS_ROWS
    mid = wgt_rows // 2
    buf = [pltpu.VMEM((ROWS, channels), bf16), pltpu.VMEM((ROWS, hidden), bf16),
           pltpu.VMEM((ROWS, hidden), f32), pltpu.VMEM((CLS_ROWS, ROWS), f32), pltpu.VMEM((ROWS, hidden), f32)]
    out_buf = [pltpu.VMEM((channels + 2 * RUNS, ROWS), bf16), pltpu.VMEM((ROWS, hidden), f32),
               pltpu.VMEM((ROWS, hidden), bf16)]
    work = [pltpu.VMEM((n_hw, channels), f32), pltpu.VMEM((2 * rows_blk, ZC, channels), f32),
            pltpu.VMEM((n_lab, 128), f32), pltpu.VMEM((n_hw, hidden), f32),
            pltpu.VMEM((channels, hidden), f32), pltpu.VMEM((CLS_PAD, hidden), f32),
            pltpu.VMEM((CLS_ROWS, 128), f32), pltpu.SMEM((8, 128), jnp.int32), pltpu.SemaphoreType.DMA]
    work += buf + buf + out_buf + out_buf + [pltpu.VMEM((ROWS, channels), f32)]
    work += [pltpu.VMEM((cols_blk, 8, channels), f32)] * 2 + [pltpu.VMEM((2 * rows_blk, 8, channels), f32)] * 2
    work += [pltpu.VMEM((8, 128), jnp.int32), pltpu.VMEM((wgt_rows, hidden), f32)]
    sums = [((cols_blk, 8, channels), f32)] * 2 + [((2 * rows_blk, 8, channels), f32)] * 2
    def decode(n, sources, outs):
        return call(
            functools.partial(decode_kernel, chunk=CHUNKS[n], first=n == 0, rows_blk=rows_blk,
                              slots=slots, pair_cols=pair_cols), "decode%d" % n,
            (meta,) + sources + (wzf0, wzf1)[n:n + 1] + shared,
            [smem] + [vmem] * (len(sources) + 8), outs, work, 22 * 10**9, 28)

    wz0a, wz0b, zh0a, zh0b, hw0, wgt0 = decode(
        0, (own0, recv0), sums + [((n_hw, channels), f32), ((wgt_rows, hidden), f32)])
    recv1, wz0a, wz0b, zh0a, zh0b = lax.optimization_barrier((recv1, wz0a, wz0b, zh0a, zh0b))
    wz1a, core_send, zh1a, zh1b, hw1, w_keep = decode(
        1, (own0, recv0, own1, recv1, hw0, wgt0),
        [sums[0], ((cols_blk + mid // 4, 8, channels), f32), sums[2], sums[3],
         ((n_hw, channels), f32), ((mid // 4, 8, channels), f32)])

    def place(mine, recv):
        return call(
            functools.partial(place_kernel, slots=slots), "place", (meta, run_index, mine, recv),
            [smem, smem, vmem, vmem], [((rows_blk * cols_blk, channels), f32)], [],
            3 * 10**9, 4)[0].reshape(rows_blk, cols_blk, channels)

    zpart = half // n_zl
    moves = []
    for a in range(n_ha):
        for b in range(n_wa):
            moves.append((a * n_wa + b, ((b // n_zl) * n_q + a % n_q) * n_wa + (a // n_q) * n_zl + b % n_zl))
    barrier = lax.optimization_barrier

    if direct:
        def ha_perm(pairs):
            return [(top * n_q + a, top * n_q + b) for top in range(2) for a, b in pairs]

        def flat(value):
            return value.reshape(2 * rows_blk * 8, channels)

        n_part = rows_blk * 8
        zh0a, zh0b = flat(zh0a), flat(zh0b)
        zh1a, zh1b = flat(zh1a), flat(zh1b)
        wz0r = ppermute_xor(wz0b, "ha", n_ha, 1)
        zh0 = encode(jnp.concatenate([zh0a, zh0b]).reshape(4, n_part, channels))
        zh0r = []
        for k0 in range(2):
            for k1 in range(2):
                owners = []
                for a in range(n_ha):
                    for b in range(n_wa):
                        dest_a = ((b // 2) ^ k1) * n_q + a % n_q
                        dest_b = (a // n_q) * 2 + ((b % 2) ^ k0)
                        owners.append((a * n_wa + b, dest_a * n_wa + dest_b))
                zh0r.append(lax.ppermute(zh0[2 * k0 + k1], ("ha", "wa"), owners))
        wz0r, zh0r, wz1a, core_send, zh1a, zh1b, hw1, w_keep = barrier(
            (wz0r, zh0r, wz1a, core_send, zh1a, zh1b, hw1, w_keep))
        zh1r = ppermute_xor(encode(zh1b[None]), "wa", n_wa, 1)
        core_recv = ppermute_xor(core_send, "ha", n_ha, 1)
        hw_recv = lax.ppermute(encode(hw1[None]), "ha", swap_y)
        near0 = wz0a + wz0r
        zh_first = sum(decode_half(part[None])[0] for part in zh0r)
        w = w_keep + core_recv[cols_blk:]
        wr = ppermute_xor(w, "wa", n_wa, 2)
        zh1r, wr = barrier((zh1r, wr))
        near1 = wz1a + core_recv[:cols_blk]
        part1 = zh1a + decode_half(zh1r)[0]
        zhf = ppermute_xor(encode(part1[None, n_part:]), "wa", n_wa, 2)
        outer = (my_q == 0) | (my_q == 3)
        far = ppermute_xor(encode(jnp.where(outer, near1, near0).reshape(1, cols_blk * 8, channels)), "ha", n_ha, 2)
        w = w + wr
        w = w + ppermute_xor(w, "ha", n_ha, n_q)
        wr = ppermute_xor(w, "ha", n_ha, 2)
        zhf, wr, hw_recv = barrier((zhf, wr, hw_recv))
        zhm = lax.ppermute(encode(part1[None, :n_part] + decode_half(zhf)), ("ha", "wa"), moves)
        w = w + wr
        w = w + ppermute_xor(w, "wa", n_wa, 1)
        w_other = ppermute_xor(w, "ha", n_ha, 1)
        hw_grad = place(hw1, decode_half(hw_recv)[0])
        wz_grad = jnp.where(outer, near0, near1) + decode_half(far).reshape(near1.shape)
        zh_grad, w_in_grad, b_in_grad, w_out_grad, b_out_grad = call(
            functools.partial(finish_kernel, rows_blk=rows_blk), "finish", (meta, zh_first, decode_half(zhm)[0], w, w_other),
            [smem] + [vmem] * 4,
            [((2 * 8, rows_blk, channels), f32), ((channels, hidden), f32), ((1, hidden), f32),
             ((classes, hidden), f32), ((1, classes), f32)], [pltpu.VMEM((wgt_rows, hidden), f32)], 10**9, 4)
        return hw_grad, zh_grad, wz_grad, w_in_grad, b_in_grad[0], w_out_grad.T, b_out_grad[0]

    wz1b = core_send[:cols_blk]
    hw_grad = place(hw1, lax.ppermute(hw1, "ha", swap_y))
    wz_all = jnp.stack([wz0a, wz1a, wz1b, wz0b])
    wz_all = wz_all.transpose(1, 0, 2, 3).reshape(cols_blk, n_q, half // n_q, channels)
    part = jnp.take(wz_all.transpose(1, 0, 2, 3), jnp.arange(n_q) ^ my_q, axis=0)
    bit = 1
    while bit < n_q:
        part = part.reshape(part.shape[0] // 2, 2, cols_blk, half // n_q, channels)
        part = part[:, 0] + ppermute_xor(part[:, 1], "ha", n_ha, bit)
        bit *= 2
    wz_grad = part[0]
    zh_all = jnp.stack([zh0a, zh1a, zh1b, zh0b], axis=1)
    zh_all = zh_all.reshape(2, rows_blk, n_zl, zpart, channels).transpose(0, 2, 1, 3, 4)
    part = jnp.take(zh_all, jnp.arange(n_zl) ^ my_zl, axis=1)
    part = jnp.take(part, jnp.arange(2) ^ b1, axis=0)
    bit = 1
    while bit < n_zl:
        part = part.reshape(2, part.shape[1] // 2, 2, rows_blk, zpart, channels)
        part = part[:, :, 0] + ppermute_xor(part[:, :, 1], "wa", n_wa, bit)
        bit *= 2
    part = part[:, 0]
    part = part[0] + ppermute_xor(part[1], "wa", n_wa, n_zl)
    zh_grad = lax.ppermute(part, ("ha", "wa"), moves).transpose(1, 0, 2)
    w = w_keep + ppermute_xor(core_send[cols_blk:], "ha", n_ha, 1)
    bit = 2
    while bit < n_ha:
        w = w + ppermute_xor(w, "ha", n_ha, bit)
        bit *= 2
    bit = 1
    while bit < n_wa:
        w = w + ppermute_xor(w, "wa", n_wa, bit)
        bit *= 2
    w_other = ppermute_xor(w, "ha", n_ha, 1)
    w, w_other = [jnp.concatenate(jnp.split(v.reshape(2 * mid, 128), 2), axis=1) for v in (w, w_other)]
    upper = ha % 2 == 1
    wgt = jnp.concatenate([jnp.where(upper, w_other, w), jnp.where(upper, w, w_other)])
    first = channels + 8
    return (hw_grad, zh_grad, wz_grad, wgt[:channels], wgt[channels],
            wgt[first:first + classes].T, wgt[channels + 1, :classes])


def solution(mesh):
    placed = (
        P("ha", "wa", None),
        P(None, "ha", None),
        P("wa", None, None),
        P(),
        P(),
        P(),
        P(),
        P(("ha", "wa"), None),
        P(("ha", "wa")),
        P(("ha", "wa"), None, None),
    )
    return jax.shard_map(
        functools.partial(local, mesh.shape["ha"], mesh.shape["wa"]),
        mesh=mesh,
        in_specs=placed,
        out_specs=(
            P("ha", "wa", None),
            P("wa", "ha", None),
            P("wa", "ha", None),
            P(),
            P(),
            P(),
            P(),
        ),
        check_vma=False,
    )
```

```python
import functools

import jax
import jax.numpy as jnp
from jax import lax
from jax.experimental import pallas as pl
from jax.experimental.pallas import tpu as pltpu
from jax.sharding import PartitionSpec as P

grad_scale = 0.25
CLS_ROWS = 24
CLS_PAD = 32
CHUNKS = ((0, 3), (1, 2))
ZC = 16
RUNS = 32
GROUP = 4
ROWS = RUNS * 2 * ZC
STRIP = 32
LEVEL_TOPS = tuple(2.0 ** e for e in (4, -7, -18, -29, -40))
LEVEL_BITS = (11, 22, 33, 44, 55)
CODE_ROWS = 16


def ppermute_xor(value, axis, size, mask):
    return lax.ppermute(value, axis, [(i, i ^ mask) for i in range(size)])


def fill_planes(side, refs, bases, zh_full, lab_pad, start, *, half, rows_blk, depth_z, slots):
    n_zh = rows_blk * ZC
    n_lab = slots // GROUP
    lane = lax.rem(lax.broadcasted_iota(jnp.int32, (n_lab, 128), 1), depth_z)
    z0 = side * half
    labs = [lab_pad[pl.ds(start + par, n_lab, stride=GROUP), :] for par in range(GROUP)]
    for chunk, ref, base in zip(CHUNKS, refs, bases):
        if ref is None:
            continue
        for h in range(rows_blk):
            parts = [zh_full[pl.ds((z0 + 8 * o) * rows_blk + h, 8, stride=rows_blk), :] for o in chunk]
            ref[base + h * ZC:base + (h + 1) * ZC, :] = jnp.concatenate(parts, axis=0).astype(jnp.bfloat16)
        merged = jnp.zeros((n_lab, 128), jnp.float32)
        for par in range(GROUP):
            for n, o in enumerate(chunk):
                to = par * ZC + 8 * n
                rolled = pltpu.roll(labs[par], jnp.bitwise_and(256 + to - (z0 + 8 * o), 127), 1)
                merged = jnp.where((lane >= to) & (lane < to + 8), rolled, merged)
        ref[base + n_zh:base + n_zh + n_lab, :] = merged.astype(jnp.bfloat16)


def fetch(pairs, sems):
    copies = [pltpu.make_async_copy(src, dst, sems.at[n]) for n, (src, dst) in enumerate(pairs)]
    for copy in copies:
        copy.start()
    for copy in copies:
        copy.wait()


def widen_planes(zh_raw, lab_raw, zh_full, lab_pad, slots):
    zh_full[...] = zh_raw[...].astype(jnp.float32)
    lab_pad[0:slots, :] = jnp.zeros((slots, lab_raw.shape[1]), jnp.float32)
    lab_pad[slots:, :] = lab_raw[...].astype(jnp.float32)


def twice(ids_raw, slots):
    ids = [ids_raw[:, k * 128:(k + 1) * 128] for k in range(slots // 128)]
    return jnp.concatenate(ids + ids, axis=0)


def gather_rows(rid_ref, hw_full, hw_rows, slots, shift):
    def gather_step(i, carry):
        for j in range(8):
            s = i * 8 + j
            r = rid_ref[0, jnp.maximum(s - shift, 0)]
            for p in range(2):
                hw_rows[pl.ds(2 * s + p, 1), :] = hw_full[pl.ds(2 * r + p, 1), :]
        return carry

    lax.fori_loop(0, slots // 8, gather_step, 0)


def put_ids(ref, base, ids, shift_bits, keep):
    padded = jnp.concatenate([ids, jnp.zeros_like(ids)], axis=0)
    high = lax.shift_right_logical(padded, shift_bits)
    low = jnp.bitwise_and(padded, keep)
    row = lax.broadcasted_iota(jnp.int32, padded.shape, 0)
    both = jnp.where(row < 4, high, pltpu.roll(low, 4, 0))
    ref[base:base + 16, :] = both.astype(jnp.float32).astype(jnp.bfloat16)


def pack_plane_kernel(meta_ref, zh_ref, lab_ref, send_ref, zh_raw, lab_raw, sems, zh_full, lab_pad,
                      *, depth_z, rows_blk, slots, pair_cols):
    fetch(((zh_ref, zh_raw), (lab_ref, lab_raw)), sems)
    widen_planes(zh_raw, lab_raw, zh_full, lab_pad, slots)
    fill_planes(1 - meta_ref[0], (send_ref, None), (0, 0), zh_full, lab_pad, meta_ref[1],
                half=depth_z // 2, rows_blk=rows_blk, depth_z=depth_z, slots=slots)


def pack_rows_kernel(meta_ref, hw_ref, ids_ref, send_ref, hw_raw, ids_raw, rid_ref, sems, hw_full, hw_rows,
                     *, depth_z, rows_blk, slots, pair_cols):
    n_hw = 2 * slots
    count = meta_ref[1]
    fetch(((hw_ref, hw_raw), (ids_ref, rid_ref), (ids_ref, ids_raw)), sems)
    hw_full[...] = hw_raw[...].astype(jnp.float32)
    ids = twice(ids_raw, slots)
    gather_rows(rid_ref, hw_full, hw_rows, slots, slots - count)
    send_ref[0:n_hw, :] = hw_rows[...].astype(jnp.bfloat16)
    down = slots - count
    lanes = jnp.bitwise_and(down, 127)
    rows = lax.shift_right_logical(down, 7)
    turned = pltpu.roll(ids, lanes, 1)
    here = pltpu.roll(turned, rows, 0)
    before = pltpu.roll(turned, jnp.bitwise_and(rows + 1, 7), 0)
    lane = lax.broadcasted_iota(jnp.int32, ids.shape, 1)
    put_ids(send_ref, n_hw, jnp.where(lane < lanes, before, here), pair_cols.bit_length() - 1, pair_cols - 1)


def pack_own_kernel(meta_ref, hw_ref, zh_ref, lab_ref, ids_ref, wz_ref,
                    hw_out, own0_ref, own1_ref, send1_ref, wz0_ref, wz1_ref,
                    hw_raw, zh_raw, lab_raw, ids_raw, rid_ref, sems,
                    hw_full, hw_rows, zh_full, lab_pad, wz_raw, wz_sem,
                    *, depth_z, rows_blk, slots, pair_cols):
    half = depth_z // 2
    n_hw = 2 * slots
    z0 = pl.multiple_of(meta_ref[0] * half, half)
    wz_copy = pltpu.make_async_copy(wz_ref.at[:, pl.ds(z0, half), :], wz_raw, wz_sem)
    wz_copy.start()
    fetch(((hw_ref, hw_raw), (ids_ref, rid_ref), (ids_ref, ids_raw), (zh_ref, zh_raw), (lab_ref, lab_raw)), sems)
    hw_full[...] = hw_raw[...].astype(jnp.float32)
    widen_planes(zh_raw, lab_raw, zh_full, lab_pad, slots)
    gather_rows(rid_ref, hw_full, hw_rows, slots, 0)
    hw_out[0:n_hw, :] = hw_rows[...].astype(jnp.bfloat16)
    put_ids(hw_out, n_hw, twice(ids_raw, slots), pair_cols.bit_length() - 1, pair_cols - 1)
    fill_planes(meta_ref[0], (own0_ref, own1_ref), (0, 0), zh_full, lab_pad, slots,
                half=half, rows_blk=rows_blk, depth_z=depth_z, slots=slots)
    fill_planes(1 - meta_ref[0], (None, send1_ref), (0, 0), zh_full, lab_pad, meta_ref[1],
                half=half, rows_blk=rows_blk, depth_z=depth_z, slots=slots)
    wz_copy.wait()

    def widen(w, carry):
        rows = wz_raw[w].astype(jnp.float32)
        for chunk, ref in zip(CHUNKS, (wz0_ref, wz1_ref)):
            for n, o in enumerate(chunk):
                ref[w, 8 * n:8 * n + 8, :] = rows[8 * o:8 * o + 8]
        return carry

    lax.fori_loop(0, 2 * pair_cols, widen, 0, unroll=8)


def add_zh(d, row, zh_accs):
    both = d[0] + d[1]
    now = [acc[row] for acc in zh_accs]
    for n, acc in enumerate(zh_accs):
        acc[row] = now[n] + both[8 * n:8 * n + 8]


def add_wz(d, col, wz_accs):
    now = [[acc[col + p] for p in range(2)] for acc in wz_accs]
    for n, acc in enumerate(wz_accs):
        for p in range(2):
            acc[col + p] = now[n][p] + d[p][8 * n:8 * n + 8]


def pick_level(top):
    level = jnp.zeros(top.shape, jnp.float32)
    for n, bound in enumerate(LEVEL_TOPS):
        level = jnp.where(top < bound, n + 1.0, level)
    return level


def level_scale(level, sign):
    scale = jnp.ones(level.shape, jnp.float32)
    for n in range(len(LEVEL_TOPS)):
        scale = jnp.where(level == n + 1.0, 2.0 ** (sign * LEVEL_BITS[n]), scale)
    return scale


def encode(value):
    level = pick_level(jnp.max(jnp.abs(value), axis=1, keepdims=True))
    code = jnp.broadcast_to(level, (value.shape[0], CODE_ROWS, value.shape[2]))
    return jnp.concatenate([value * level_scale(level, 1), code], axis=1).astype(jnp.float16)


def decode_half(value):
    value = value.astype(jnp.float32)
    n = value.shape[1] - CODE_ROWS
    return value[:, :n] * level_scale(value[:, n:n + 1, :], -1)


def read_runs(ids_ref, first, n):
    row = lax.shift_right_logical(first, 7)
    at = jnp.bitwise_and(first, 127)
    return [(ids_ref[row, at + j], ids_ref[row + 4, at + j]) for j in range(n)]


def decode_kernel(*refs, chunk, first, rows_blk, slots, pair_cols):
    n_hw = 2 * slots
    n_zh = rows_blk * ZC
    n_lab = slots // GROUP
    meta_ref, hw_own, hw_recv, z_own, z_recv = refs[:5]
    refs = refs[5:]
    z_base = 0
    if not first:
        hw_prev, wgt_prev = refs[:2]
        refs = refs[2:]
    wz_full, w_in_ref, w_in_t_ref, b_in_ref, w_out_t_ref, w_out_half_ref, b_out_ref, sel_ref = refs[:8]
    refs = refs[8:]
    if first:
        wz_out0, wz_out1, zh_out0, zh_out1, hw_out, wgt_out = refs[:6]
        refs = refs[6:]
    else:
        wz_out0, core_out, zh_out0, zh_out1, hw_out, wgt_keep = refs[:6]
        refs = refs[6:]
    (hw_full, zh_full, lab_full, hw_acc, w_in_acc, w_out_acc, b_out_acc, ids_ref, ids_sem) = refs[:9]
    bufs = (refs[9:13], refs[13:17])
    outs = (refs[17:19], refs[19:21])
    wz_accs, zh_accs, ids_vec, wgt_all = refs[21:23], refs[23:25], refs[25], refs[26]
    count = meta_ref[1]
    rel_own = meta_ref[7]

    spot_row = lax.broadcasted_iota(jnp.int32, (8, 128), 0)
    spot = jnp.bitwise_and(spot_row, 3) * 128 + lax.broadcasted_iota(jnp.int32, (8, 128), 1)
    own_ids = hw_own[n_hw:n_hw + 16, :].astype(jnp.float32).astype(jnp.int32)
    recv_ids = hw_recv[n_hw:n_hw + 16, :].astype(jnp.float32).astype(jnp.int32)
    is_own = spot < count
    ids = jnp.where(is_own, own_ids[0:8], recv_ids[0:8])
    rel = jnp.where(is_own, rel_own, 1 - rel_own)
    ids_vec[...] = jnp.where(spot_row < 4, ids + rel * rows_blk, 2 * ids)
    copy = pltpu.make_async_copy(ids_vec, ids_ref, ids_sem)
    copy.start()
    row = lax.broadcasted_iota(jnp.int32, (n_hw, 128), 0)
    hw_full[...] = jnp.where(row < 2 * count, hw_own[0:n_hw, :].astype(jnp.float32),
                             hw_recv[0:n_hw, :].astype(jnp.float32))
    for k, ref in ((0, z_own), (1, z_recv)):
        base = jnp.bitwise_xor(rel_own, k) * rows_blk
        for h in range(rows_blk):
            zh_full[base + h] = ref[z_base + h * ZC:z_base + (h + 1) * ZC, :].astype(jnp.float32)
    lab_row = lax.broadcasted_iota(jnp.int32, (n_lab, 128), 0)
    lab_lane = lax.broadcasted_iota(jnp.int32, (n_lab, 128), 1)
    place = GROUP * lab_row + lax.rem(lab_lane // ZC, GROUP)
    first_lab = z_base + n_zh
    lab_full[...] = jnp.where(place < count, z_own[first_lab:first_lab + n_lab, :].astype(jnp.float32),
                              z_recv[first_lab:first_lab + n_lab, :].astype(jnp.float32))
    for acc in wz_accs + zh_accs:
        acc[...] = jnp.zeros_like(acc)
    w_in_acc[...] = jnp.zeros_like(w_in_acc)
    w_out_acc[...] = jnp.zeros_like(w_out_acc)
    b_out_acc[...] = jnp.zeros_like(b_out_acc)
    copy.wait()

    groups = RUNS // GROUP
    n_ch = w_in_ref.shape[0]
    for left_ref, dpre_ref in outs:
        left_ref[n_ch:, :] = sel_ref[...]
    class_ids = lax.broadcasted_iota(jnp.int32, (CLS_ROWS, 128), 0).astype(jnp.float32)
    nt = (((1,), (1,)), ((), ()))

    def front(b, buf):
        feat_ref, hid_ref, slope_ref, logit_ref = buf
        runs = read_runs(ids_ref, RUNS * b, RUNS)
        for g in range(groups):
            pieces = []
            for p in range(2):
                for par in range(GROUP):
                    row, col = runs[GROUP * g + par]
                    at = pl.multiple_of(2 * RUNS * b, 2 * RUNS) + 2 * (GROUP * g + par) + p
                    total = hw_full[pl.ds(at, 1), :] + zh_full[row] + wz_full[col + p]
                    pieces.append(total.astype(jnp.bfloat16))
            feat = jnp.concatenate(pieces, axis=0)
            feat_ref[g * 128:(g + 1) * 128, :] = feat
            pre_all = jnp.dot(feat, w_in_ref[...], preferred_element_type=jnp.float32)
            for r in range(0, 128, STRIP):
                pre = pre_all[r:r + STRIP] + b_in_ref[...]
                t = jnp.tanh(pre)
                a = 1.0 + t
                u = pre * a
                at = g * 128 + r
                hid_ref[at:at + STRIP, :] = u.astype(jnp.bfloat16)
                slope_ref[at:at + STRIP, :] = a + u * (1.0 - t)
        logits = lax.dot_general(w_out_t_ref[...], hid_ref[...], nt, preferred_element_type=jnp.float32)
        logit_ref[...] = logits[0:CLS_ROWS, :]

    def middle(b, buf, out):
        feat_ref, hid_ref, slope_ref, logit_ref = buf
        left_ref, dpre_ref = out
        left_ref[0:n_ch, :] = jnp.transpose(feat_ref[...], (1, 0))
        dl_tiles = []
        b_part = None
        for g in range(groups):
            tile = logit_ref[:, g * 128:(g + 1) * 128] + b_out_ref[...]
            top = jnp.max(tile, axis=0, keepdims=True)
            e = jnp.exp(tile - top)
            inv = 1.0 / jnp.sum(e, axis=0, keepdims=True)
            lab_here = lab_full[pl.ds(groups * b + g, 1), :]
            onehot = jnp.where(class_ids == lab_here, 1.0, 0.0)
            dl = ((e * inv - onehot) * grad_scale).astype(jnp.bfloat16).astype(jnp.float32)
            b_part = dl if b_part is None else b_part + dl
            dl_tiles.append(dl)
        b_out_acc[...] += b_part
        dl_all = jnp.concatenate(dl_tiles, axis=1)
        dl_all = jnp.concatenate([dl_all, jnp.zeros((CLS_PAD - CLS_ROWS, ROWS), jnp.float32)], axis=0)
        dl_t = jnp.transpose(dl_all, (1, 0)).astype(jnp.bfloat16)
        w_out_acc[...] += jnp.dot(dl_all.astype(jnp.bfloat16), hid_ref[...], preferred_element_type=jnp.float32)
        for g in range(groups):
            dhid = jnp.dot(dl_t[g * 128:(g + 1) * 128], w_out_half_ref[...], preferred_element_type=jnp.float32)
            for r in range(0, 128, STRIP):
                at = g * 128 + r
                dpre_ref[at:at + STRIP, :] = (dhid[r:r + STRIP] * slope_ref[at:at + STRIP, :]).astype(jnp.bfloat16)

    def back(b, out):
        left_ref, dpre_ref = out
        dpre = dpre_ref[...]
        sums = jnp.dot(left_ref[...], dpre, preferred_element_type=jnp.float32)
        w_in_acc[...] += sums[0:n_ch]
        hw_acc[pl.ds(pl.multiple_of(2 * RUNS * b, 2 * RUNS), 2 * RUNS), :] = sums[n_ch:]
        runs = read_runs(ids_ref, RUNS * b, RUNS)
        for g in range(groups):
            dfeat = jnp.dot(dpre_ref[g * 128:(g + 1) * 128, :], w_in_t_ref[...], preferred_element_type=jnp.float32)
            for par in range(GROUP):
                d = [dfeat[p * 64 + par * ZC:p * 64 + (par + 1) * ZC] for p in range(2)]
                row, col = runs[GROUP * g + par]
                add_zh(d, row, zh_accs)
                add_wz(d, col, wz_accs)

    n_batch = slots // RUNS
    front(0, bufs[0])
    front(1, bufs[1])
    middle(0, bufs[0], outs[0])

    def step(k, carry):
        b = 2 * k
        front(b + 2, bufs[0])
        middle(b + 1, bufs[1], outs[1])
        back(b, outs[0])
        front(b + 3, bufs[1])
        middle(b + 2, bufs[0], outs[0])
        back(b + 1, outs[1])
        return carry

    lax.fori_loop(0, n_batch // 2 - 1, step, 0)
    middle(n_batch - 1, bufs[1], outs[1])
    back(n_batch - 2, outs[0])
    back(n_batch - 1, outs[1])
    tail = hw_acc[...]
    total = None
    for n in range(3):
        part = tail.astype(jnp.bfloat16)
        tail = tail - part.astype(jnp.float32)
        term = jnp.dot(part, w_in_t_ref[...], preferred_element_type=jnp.float32)
        total = term if total is None else total + term
    width = w_in_acc.shape[1]
    b_in_sum = jnp.sum(hw_acc[...], axis=0, keepdims=True)
    b_pad = jnp.concatenate([b_out_acc[...], jnp.zeros((128 - CLS_ROWS, 128), jnp.float32)], axis=0)
    b_out_sum = jnp.sum(jnp.transpose(b_pad, (1, 0)), axis=0, keepdims=True)
    b_out_sum = jnp.concatenate([b_out_sum, jnp.zeros((1, width - 128), jnp.float32)], axis=1)
    biases = jnp.concatenate([b_in_sum, b_out_sum, jnp.zeros((6, width), jnp.float32)], axis=0)
    weights = jnp.concatenate([w_in_acc[...], biases, w_out_acc[0:CLS_ROWS, :]], axis=0)
    put_zh(meta_ref, chunk, zh_accs, zh_out0, zh_out1)
    if first:
        hw_out[...] = total
        wgt_out[...] = weights
        put_wz(meta_ref, chunk, wz_accs, wz_out0, wz_out1)
        return
    hw_out[...] = total + hw_prev[...]
    wgt_all[...] = weights + wgt_prev[...]
    put_wz(meta_ref, chunk, wz_accs, wz_out0, core_out.at[0:2 * pair_cols])
    mid = wgt_all.shape[0] // 2
    mine = meta_ref[8] * mid
    wgt_keep[...] = split_lanes(wgt_all[pl.ds(pl.multiple_of(mine, 8), mid), :])
    core_out[2 * pair_cols:] = split_lanes(wgt_all[pl.ds(pl.multiple_of(mid - mine, 8), mid), :])


def split_lanes(value):
    return jnp.concatenate([value[:, :128], value[:, 128:]], axis=0).reshape(value.shape[0] // 4, 8, 128)


def put_zh(meta_ref, chunk, zh_accs, zh_out0, zh_out1):
    same = meta_ref[6] == chunk[0] // 2
    zh_out0[...] = jnp.where(same, zh_accs[0][...], zh_accs[1][...])
    zh_out1[...] = jnp.where(same, zh_accs[1][...], zh_accs[0][...])


def put_wz(meta_ref, chunk, wz_accs, wz_out0, wz_out1):
    same = meta_ref[2 + chunk[0]] == 0
    wz_out0[...] = jnp.where(same, wz_accs[0][...], wz_accs[1][...])
    wz_out1[...] = jnp.where(same, wz_accs[1][...], wz_accs[0][...])


def place_kernel(meta_ref, rid_ref, mine_ref, recv_ref, out_ref, *, slots):
    out_ref[...] = jnp.zeros_like(out_ref)
    count = meta_ref[1]

    def place(s, carry):
        r = rid_ref[0, s]
        for p in range(2):
            out_ref[pl.ds(2 * r + p, 1), :] = (mine_ref[pl.ds(2 * s + p, 1), :]
                                               + recv_ref[pl.ds(2 * (slots - count + s) + p, 1), :])
        return carry

    def place_eight(i, carry):
        for j in range(8):
            place(8 * i + j, carry)
        return carry

    lax.fori_loop(0, count // 8, place_eight, 0)
    lax.fori_loop(count // 8 * 8, count, place, 0)


def finish_kernel(meta_ref, zh_ref, w_mine_ref, w_other_ref,
                  zh_out, w_in_out, b_in_out, w_out_out, b_out_out, w_all, *, rows_blk):
    mid = w_all.shape[0] // 2
    mine = meta_ref[8] * mid
    for start, ref in ((mine, w_mine_ref), (mid - mine, w_other_ref)):
        flat = ref[...].reshape(2 * mid, 128)
        w_all[pl.ds(pl.multiple_of(start, 8), mid), :] = jnp.concatenate([flat[:mid], flat[mid:]], axis=1)
    n_ch = w_in_out.shape[0]
    w_in_out[...] = w_all[0:n_ch, :]
    b_in_out[...] = w_all[n_ch:n_ch + 1, :]
    b_out_out[...] = w_all[n_ch + 1:n_ch + 2, 0:b_out_out.shape[1]]
    w_out_out[...] = w_all[n_ch + 8:n_ch + 8 + w_out_out.shape[0], :]
    swapped = meta_ref[6]
    for n in range(2):
        base = jnp.bitwise_xor(swapped, n) * 8
        for z in range(8):
            zh_out[base + z] = zh_ref[n, pl.ds(z, rows_blk, stride=8), :]


def local(n_ha, n_wa, hw_plane, zh_plane, wz_plane, w_in, b_in, w_out, b_out,
          run_index, run_count, labels):
    rows_blk, cols_blk, channels = hw_plane.shape
    depth_z = zh_plane.shape[0]
    hidden = w_in.shape[1]
    classes = w_out.shape[1]
    slots = run_index.shape[1]
    half = depth_z // 2
    pair_cols = cols_blk // 2
    n_q = n_ha // 2
    n_zl = n_wa // 2
    n_hw = 2 * slots
    n_zh = rows_blk * ZC
    n_lab = slots // GROUP
    smem = pl.BlockSpec(memory_space=pltpu.SMEM)
    vmem = pl.BlockSpec(memory_space=pltpu.VMEM)
    hbm = pl.BlockSpec(memory_space=pltpu.HBM)
    f32 = jnp.float32
    bf16 = jnp.bfloat16

    ha = lax.axis_index("ha")
    wa = lax.axis_index("wa")
    y = ha // n_q
    my_q = ha % n_q
    b1 = wa // n_zl
    my_zl = wa % n_zl
    count = run_count[0]
    direct = n_q == 4 and n_zl == 2
    if direct:
        wz_pos = [(o ^ my_q) % 2 for o in range(4)]
        rest = [my_zl, y ^ b1, ha % 2, my_q]
    else:
        wz_pos = [jnp.int32(o // 2) for o in range(4)]
        rest = [jnp.int32(0), y, ha % 2, my_q]
    meta = jnp.stack([y, count] + wz_pos + rest).astype(jnp.int32)
    swap_y = [(i, (i + n_q) % n_ha) for i in range(n_ha)]

    n_rows, n_plane = n_hw + 16, n_zh + n_lab
    planes = (hw_plane.reshape(rows_blk * cols_blk, channels),
              zh_plane.reshape(depth_z * rows_blk, channels), labels[0], run_index)
    hw_raw = pltpu.VMEM((rows_blk * cols_blk, channels), bf16)
    plane_raw = [pltpu.VMEM((depth_z * rows_blk, channels), bf16), pltpu.VMEM((slots, 2 * depth_z), jnp.int32)]
    ids_raw = [pltpu.VMEM((1, slots), jnp.int32), pltpu.SMEM((1, slots), jnp.int32)]
    hw_wide = [pltpu.VMEM((rows_blk * cols_blk, channels), f32), pltpu.VMEM((n_hw, channels), f32)]
    plane_wide = [pltpu.VMEM((depth_z * rows_blk, channels), f32), pltpu.VMEM((2 * slots, 2 * depth_z), f32)]

    def call(kernel, name, operands, specs, outs, scratch, flops, limit=16):
        return pl.pallas_call(
            kernel,
            out_shape=[jax.ShapeDtypeStruct(shape, kind) for shape, kind in outs],
            in_specs=specs,
            out_specs=[vmem] * len(outs),
            scratch_shapes=scratch,
            compiler_params=pltpu.CompilerParams(vmem_limit_bytes=limit * 2**20),
            cost_estimate=pl.CostEstimate(flops=flops, bytes_accessed=2**20, transcendentals=0),
            name=name,
        )(*operands)

    sizes = dict(depth_z=depth_z, rows_blk=rows_blk, slots=slots, pair_cols=pair_cols)
    send0, = call(functools.partial(pack_plane_kernel, **sizes), "pack_plane", (meta, planes[1], planes[2]),
                  [smem] + [hbm] * 2, [((n_plane, channels), bf16)],
                  plane_raw + [pltpu.SemaphoreType.DMA((2,))] + plane_wide, 2 * 10**9, 60)
    recv0 = lax.ppermute(send0, "ha", swap_y)
    send0, hw_late, ids_late = lax.optimization_barrier((send0, planes[0], planes[3]))
    send_hw, = call(functools.partial(pack_rows_kernel, **sizes), "pack_rows", (meta, hw_late, ids_late),
                    [smem] + [hbm] * 2, [((n_rows, channels), bf16)],
                    [hw_raw] + ids_raw + [pltpu.SemaphoreType.DMA((3,))] + hw_wide, 3 * 10**9, 12)
    recv_hw = lax.ppermute(send_hw, "ha", swap_y)
    later = lax.optimization_barrier((send_hw, w_in, b_in, w_out, b_out) + planes)
    w_in, b_in, w_out, b_out = later[1:5]
    own_hw, own0, own1, send1, wzf0, wzf1 = call(
        functools.partial(pack_own_kernel, **sizes), "pack_own", (meta,) + later[5:] + (wz_plane,),
        [smem] + [hbm] * 5,
        [((n_rows, channels), bf16)] + [((n_plane, channels), bf16)] * 3 + [((cols_blk, ZC, channels), f32)] * 2,
        [hw_raw] + plane_raw + ids_raw + [pltpu.SemaphoreType.DMA((5,))] + hw_wide + plane_wide
        + [pltpu.VMEM((cols_blk, half, channels), bf16), pltpu.SemaphoreType.DMA], 3 * 10**9, 16)
    send1, recv0, recv_hw = lax.optimization_barrier((send1, recv0, recv_hw))
    recv1 = lax.ppermute(send1, "ha", swap_y)

    w_in_half = (w_in.astype(f32) * 0.5).astype(bf16)
    w_out_half = jnp.pad((w_out.astype(f32) * 0.5).astype(bf16).T, ((0, CLS_PAD - classes), (0, 0)))
    w_out_t = jnp.pad(w_out.T, ((0, CLS_PAD - classes), (0, 0)))
    b_out_rows = jnp.broadcast_to(
        jnp.pad(b_out, (0, CLS_ROWS - classes), constant_values=-1e30)[:, None], (CLS_ROWS, 128))
    spot = jnp.arange(ROWS)
    run_of = (spot // 128) * GROUP + (spot % 64) // ZC
    select = (jnp.arange(2 * RUNS)[:, None] == (2 * run_of + (spot // 64) % 2)[None, :]).astype(bf16)
    w_in_t = w_in.T
    shared = (w_in_half, w_in_t, (b_in * 0.5).reshape(1, hidden), w_out_t, w_out_half, b_out_rows, select)
    wgt_rows = channels + 8 + CLS_ROWS
    mid = wgt_rows // 2
    buf = [pltpu.VMEM((ROWS, channels), bf16), pltpu.VMEM((ROWS, hidden), bf16),
           pltpu.VMEM((ROWS, hidden), f32), pltpu.VMEM((CLS_ROWS, ROWS), f32)]
    out_buf = [pltpu.VMEM((channels + 2 * RUNS, ROWS), bf16), pltpu.VMEM((ROWS, hidden), bf16)]
    work = [pltpu.VMEM((n_hw, channels), f32), pltpu.VMEM((2 * rows_blk, ZC, channels), f32),
            pltpu.VMEM((n_lab, 128), f32), pltpu.VMEM((n_hw, hidden), f32),
            pltpu.VMEM((channels, hidden), f32), pltpu.VMEM((CLS_PAD, hidden), f32),
            pltpu.VMEM((CLS_ROWS, 128), f32), pltpu.SMEM((8, 128), jnp.int32), pltpu.SemaphoreType.DMA]
    work += buf + buf + out_buf + out_buf
    work += [pltpu.VMEM((cols_blk, 8, channels), f32)] * 2 + [pltpu.VMEM((2 * rows_blk, 8, channels), f32)] * 2
    work += [pltpu.VMEM((8, 128), jnp.int32), pltpu.VMEM((wgt_rows, hidden), f32)]
    sums = [((cols_blk, 8, channels), f32)] * 2 + [((2 * rows_blk, 8, channels), f32)] * 2
    def decode(n, sources, outs):
        return call(
            functools.partial(decode_kernel, chunk=CHUNKS[n], first=n == 0, rows_blk=rows_blk,
                              slots=slots, pair_cols=pair_cols), "decode%d" % n,
            (meta,) + sources + (wzf0, wzf1)[n:n + 1] + shared,
            [smem] + [vmem] * (len(sources) + 8), outs, work, 22 * 10**9, 28)

    wz0a, wz0b, zh0a, zh0b, hw0, wgt0 = decode(
        0, (own_hw, recv_hw, own0, recv0), sums + [((n_hw, channels), f32), ((wgt_rows, hidden), f32)])
    recv1, wz0a, wz0b, zh0a, zh0b = lax.optimization_barrier((recv1, wz0a, wz0b, zh0a, zh0b))
    wz1a, core_send, zh1a, zh1b, hw1, w_keep = decode(
        1, (own_hw, recv_hw, own1, recv1, hw0, wgt0),
        [sums[0], ((cols_blk + mid // 4, 8, channels), f32), sums[2], sums[3],
         ((n_hw, channels), f32), ((mid // 4, 8, channels), f32)])

    def place(mine, recv):
        return call(
            functools.partial(place_kernel, slots=slots), "place", (meta, run_index, mine, recv),
            [smem, smem, vmem, vmem], [((rows_blk * cols_blk, channels), f32)], [],
            3 * 10**9, 4)[0].reshape(rows_blk, cols_blk, channels)

    zpart = half // n_zl
    moves = []
    for a in range(n_ha):
        for b in range(n_wa):
            moves.append((a * n_wa + b, ((b // n_zl) * n_q + a % n_q) * n_wa + (a // n_q) * n_zl + b % n_zl))
    barrier = lax.optimization_barrier

    if direct:
        def ha_perm(pairs):
            return [(top * n_q + a, top * n_q + b) for top in range(2) for a, b in pairs]

        def flat(value):
            return value.reshape(2 * rows_blk * 8, channels)

        n_part = rows_blk * 8
        zh0a, zh0b = flat(zh0a), flat(zh0b)
        zh1a, zh1b = flat(zh1a), flat(zh1b)
        wz0r = ppermute_xor(wz0b, "ha", n_ha, 1)
        zh0r = ppermute_xor(zh0b, "wa", n_wa, 1)
        stays = y == b1
        wz0r, zh0r, wz1a, core_send, zh1a, zh1b, hw1, w_keep = barrier(
            (wz0r, zh0r, wz1a, core_send, zh1a, zh1b, hw1, w_keep))
        def corner(value, ha_mask, wa_mask):
            pairs = [(a * n_wa + b, (a ^ ha_mask) * n_wa + (b ^ wa_mask)) for a in range(n_ha) for b in range(n_wa)]
            return lax.ppermute(value, ("ha", "wa"), pairs)

        zh1r = ppermute_xor(encode(zh1b[None]), "wa", n_wa, 1)
        core_recv = ppermute_xor(core_send, "ha", n_ha, 1)
        hw_recv = lax.ppermute(encode(hw1[None]), "ha", swap_y)
        near0 = wz0a + wz0r
        near1 = wz1a + core_recv[:cols_blk]
        outer = (my_q == 0) | (my_q == 3)
        far = ppermute_xor(encode(jnp.where(outer, near1, near0).reshape(1, cols_blk * 8, channels)), "ha", n_ha, 2)
        part0 = zh0a + zh0r
        w = w_keep + core_recv[cols_blk:]
        wr = ppermute_xor(w, "wa", n_wa, 2)
        zh1r, wr, hw_recv = barrier((zh1r, wr, hw_recv))
        both = jnp.stack([part0, zh1a + decode_half(zh1r)[0]])
        zhf = ppermute_xor(encode(both[:, n_part:]), "wa", n_wa, 2)
        w = w + wr
        wr = [ppermute_xor(w, "ha", n_ha, mask) for mask in (n_q, 2, n_q + 2)]
        zhf, wr, far, hw_recv = barrier((zhf, wr, far, hw_recv))
        zh_code = encode(both[:, :n_part] + decode_half(zhf))
        zhm = jnp.where(stays, zh_code, corner(zh_code, n_q, 2))
        w = (w + wr[0]) + (wr[1] + wr[2])
        w_mine = w + ppermute_xor(w, "wa", n_wa, 1)
        w_other = ppermute_xor(w, "ha", n_ha, 1) + corner(w, 1, 1)
        hw_grad = place(hw1, decode_half(hw_recv)[0])
        wz_grad = jnp.where(outer, near0, near1) + decode_half(far).reshape(near1.shape)
        zh_grad, w_in_grad, b_in_grad, w_out_grad, b_out_grad = call(
            functools.partial(finish_kernel, rows_blk=rows_blk), "finish", (meta, decode_half(zhm), w_mine, w_other),
            [smem] + [vmem] * 3,
            [((2 * 8, rows_blk, channels), f32), ((channels, hidden), f32), ((1, hidden), f32),
             ((classes, hidden), f32), ((1, classes), f32)], [pltpu.VMEM((wgt_rows, hidden), f32)], 10**9, 4)
        return hw_grad, zh_grad, wz_grad, w_in_grad, b_in_grad[0], w_out_grad.T, b_out_grad[0]

    wz1b = core_send[:cols_blk]
    hw_grad = place(hw1, lax.ppermute(hw1, "ha", swap_y))
    wz_all = jnp.stack([wz0a, wz1a, wz1b, wz0b])
    wz_all = wz_all.transpose(1, 0, 2, 3).reshape(cols_blk, n_q, half // n_q, channels)
    part = jnp.take(wz_all.transpose(1, 0, 2, 3), jnp.arange(n_q) ^ my_q, axis=0)
    bit = 1
    while bit < n_q:
        part = part.reshape(part.shape[0] // 2, 2, cols_blk, half // n_q, channels)
        part = part[:, 0] + ppermute_xor(part[:, 1], "ha", n_ha, bit)
        bit *= 2
    wz_grad = part[0]
    zh_all = jnp.stack([zh0a, zh1a, zh1b, zh0b], axis=1)
    zh_all = zh_all.reshape(2, rows_blk, n_zl, zpart, channels).transpose(0, 2, 1, 3, 4)
    part = jnp.take(zh_all, jnp.arange(n_zl) ^ my_zl, axis=1)
    part = jnp.take(part, jnp.arange(2) ^ b1, axis=0)
    bit = 1
    while bit < n_zl:
        part = part.reshape(2, part.shape[1] // 2, 2, rows_blk, zpart, channels)
        part = part[:, :, 0] + ppermute_xor(part[:, :, 1], "wa", n_wa, bit)
        bit *= 2
    part = part[:, 0]
    part = part[0] + ppermute_xor(part[1], "wa", n_wa, n_zl)
    zh_grad = lax.ppermute(part, ("ha", "wa"), moves).transpose(1, 0, 2)
    w = w_keep + ppermute_xor(core_send[cols_blk:], "ha", n_ha, 1)
    bit = 2
    while bit < n_ha:
        w = w + ppermute_xor(w, "ha", n_ha, bit)
        bit *= 2
    bit = 1
    while bit < n_wa:
        w = w + ppermute_xor(w, "wa", n_wa, bit)
        bit *= 2
    w_other = ppermute_xor(w, "ha", n_ha, 1)
    w, w_other = [jnp.concatenate(jnp.split(v.reshape(2 * mid, 128), 2), axis=1) for v in (w, w_other)]
    upper = ha % 2 == 1
    wgt = jnp.concatenate([jnp.where(upper, w_other, w), jnp.where(upper, w, w_other)])
    first = channels + 8
    return (hw_grad, zh_grad, wz_grad, wgt[:channels], wgt[channels],
            wgt[first:first + classes].T, wgt[channels + 1, :classes])


def solution(mesh):
    placed = (
        P("ha", "wa", None),
        P(None, "ha", None),
        P("wa", None, None),
        P(),
        P(),
        P(),
        P(),
        P(("ha", "wa"), None),
        P(("ha", "wa")),
        P(("ha", "wa"), None, None),
    )
    return jax.shard_map(
        functools.partial(local, mesh.shape["ha"], mesh.shape["wa"]),
        mesh=mesh,
        in_specs=placed,
        out_specs=(
            P("ha", "wa", None),
            P("wa", "ha", None),
            P("wa", "ha", None),
            P(),
            P(),
            P(),
            P(),
        ),
        check_vma=False,
    )
```

```python
import functools

import jax
import jax.numpy as jnp
from jax import lax
from jax.experimental import pallas as pl
from jax.experimental.pallas import tpu as pltpu
from jax.sharding import PartitionSpec as P

grad_scale = 0.25
CLS_ROWS = 24
CLS_PAD = 32
CHUNKS = ((0, 3), (1, 2))
ZC = 16
RUNS = 32
GROUP = 4
ROWS = RUNS * 2 * ZC
STRIP = 32
LEVEL_TOPS = tuple(2.0 ** e for e in (4, -7, -18, -29, -40))
LEVEL_BITS = (11, 22, 33, 44, 55)
CODE_ROWS = 16


def ppermute_xor(value, axis, size, mask):
    return lax.ppermute(value, axis, [(i, i ^ mask) for i in range(size)])


def fill_planes(side, refs, bases, zh_full, lab_pad, start, *, half, rows_blk, depth_z, slots):
    n_zh = rows_blk * ZC
    n_lab = slots // GROUP
    lane = lax.rem(lax.broadcasted_iota(jnp.int32, (n_lab, 128), 1), depth_z)
    z0 = side * half
    labs = [lab_pad[pl.ds(start + par, n_lab, stride=GROUP), :] for par in range(GROUP)]
    for chunk, ref, base in zip(CHUNKS, refs, bases):
        if ref is None:
            continue
        for h in range(rows_blk):
            parts = [zh_full[pl.ds((z0 + 8 * o) * rows_blk + h, 8, stride=rows_blk), :] for o in chunk]
            ref[base + h * ZC:base + (h + 1) * ZC, :] = jnp.concatenate(parts, axis=0).astype(jnp.bfloat16)
        merged = jnp.zeros((n_lab, 128), jnp.float32)
        for par in range(GROUP):
            for n, o in enumerate(chunk):
                to = par * ZC + 8 * n
                rolled = pltpu.roll(labs[par], jnp.bitwise_and(256 + to - (z0 + 8 * o), 127), 1)
                merged = jnp.where((lane >= to) & (lane < to + 8), rolled, merged)
        ref[base + n_zh:base + n_zh + n_lab, :] = merged.astype(jnp.bfloat16)


def fetch(pairs, sems):
    copies = [pltpu.make_async_copy(src, dst, sems.at[n]) for n, (src, dst) in enumerate(pairs)]
    for copy in copies:
        copy.start()
    for copy in copies:
        copy.wait()


def widen_planes(zh_raw, lab_raw, zh_full, lab_pad, slots):
    zh_full[...] = zh_raw[...].astype(jnp.float32)
    lab_pad[0:slots, :] = jnp.zeros((slots, lab_raw.shape[1]), jnp.float32)
    lab_pad[slots:, :] = lab_raw[...].astype(jnp.float32)


def twice(ids_raw, slots):
    ids = [ids_raw[:, k * 128:(k + 1) * 128] for k in range(slots // 128)]
    return jnp.concatenate(ids + ids, axis=0)


def gather_rows(rid_ref, hw_full, hw_rows, slots, shift):
    def gather_step(i, carry):
        for j in range(8):
            s = i * 8 + j
            r = rid_ref[0, jnp.maximum(s - shift, 0)]
            for p in range(2):
                hw_rows[pl.ds(2 * s + p, 1), :] = hw_full[pl.ds(2 * r + p, 1), :]
        return carry

    lax.fori_loop(0, slots // 8, gather_step, 0)


def put_ids(ref, base, ids, shift_bits, keep):
    padded = jnp.concatenate([ids, jnp.zeros_like(ids)], axis=0)
    high = lax.shift_right_logical(padded, shift_bits)
    low = jnp.bitwise_and(padded, keep)
    row = lax.broadcasted_iota(jnp.int32, padded.shape, 0)
    both = jnp.where(row < 4, high, pltpu.roll(low, 4, 0))
    ref[base:base + 16, :] = both.astype(jnp.float32).astype(jnp.bfloat16)


def pack_plane_kernel(meta_ref, zh_ref, lab_ref, send_ref, zh_raw, lab_raw, sems, zh_full, lab_pad,
                      *, depth_z, rows_blk, slots, pair_cols):
    fetch(((zh_ref, zh_raw), (lab_ref, lab_raw)), sems)
    widen_planes(zh_raw, lab_raw, zh_full, lab_pad, slots)
    fill_planes(1 - meta_ref[0], (send_ref, None), (0, 0), zh_full, lab_pad, meta_ref[1],
                half=depth_z // 2, rows_blk=rows_blk, depth_z=depth_z, slots=slots)


def pack_rows_kernel(meta_ref, hw_ref, ids_ref, send_ref, hw_raw, ids_raw, rid_ref, sems, hw_full, hw_rows,
                     *, depth_z, rows_blk, slots, pair_cols):
    n_hw = 2 * slots
    count = meta_ref[1]
    fetch(((hw_ref, hw_raw), (ids_ref, rid_ref), (ids_ref, ids_raw)), sems)
    hw_full[...] = hw_raw[...].astype(jnp.float32)
    ids = twice(ids_raw, slots)
    gather_rows(rid_ref, hw_full, hw_rows, slots, slots - count)
    send_ref[0:n_hw, :] = hw_rows[...].astype(jnp.bfloat16)
    down = slots - count
    lanes = jnp.bitwise_and(down, 127)
    rows = lax.shift_right_logical(down, 7)
    turned = pltpu.roll(ids, lanes, 1)
    here = pltpu.roll(turned, rows, 0)
    before = pltpu.roll(turned, jnp.bitwise_and(rows + 1, 7), 0)
    lane = lax.broadcasted_iota(jnp.int32, ids.shape, 1)
    put_ids(send_ref, n_hw, jnp.where(lane < lanes, before, here), pair_cols.bit_length() - 1, pair_cols - 1)


def prepare_weights(w_in_ref, b_in_ref, w_out_ref, b_out_ref,
                    w_in_half, w_in_t, b_in_half, w_out_t, w_out_half, b_out_rows, w_wide, b_wide):
    w_in = w_in_ref[...].astype(jnp.float32)
    w_in_half[...] = (w_in * 0.5).astype(jnp.bfloat16)
    w_in_t[...] = jnp.transpose(w_in, (1, 0)).astype(jnp.bfloat16)
    b_in_half[...] = b_in_ref[...] * 0.5
    classes = w_out_ref.shape[0]
    w_wide[...] = jnp.zeros_like(w_wide)
    w_wide[0:classes, :] = w_out_ref[...].astype(jnp.float32)
    turned = w_wide[...]
    w_out_t[...] = turned.astype(jnp.bfloat16)
    w_out_half[...] = (turned * 0.5).astype(jnp.bfloat16)
    b_wide[...] = jnp.full_like(b_wide, -1e30)
    b_wide[0:1, 0:classes] = b_out_ref[...]
    b_out_rows[...] = jnp.broadcast_to(jnp.transpose(b_wide[...], (1, 0))[0:CLS_ROWS, 0:1], (CLS_ROWS, 128))


def pack_own_kernel(meta_ref, hw_ref, zh_ref, lab_ref, ids_ref, wz_ref, w_in_ref, b_in_ref, w_out_ref, b_out_ref,
                    hw_out, own0_ref, own1_ref, send1_ref, wz0_ref, wz1_ref,
                    w_in_half, w_in_t, b_in_half, w_out_t, w_out_half, b_out_rows,
                    hw_raw, zh_raw, lab_raw, ids_raw, rid_ref, sems,
                    hw_full, hw_rows, zh_full, lab_pad, wz_raw, wz_sem, w_wide, b_wide,
                    *, depth_z, rows_blk, slots, pair_cols):
    half = depth_z // 2
    n_hw = 2 * slots
    z0 = pl.multiple_of(meta_ref[0] * half, half)
    wz_copy = pltpu.make_async_copy(wz_ref.at[:, pl.ds(z0, half), :], wz_raw, wz_sem)
    wz_copy.start()
    prepare_weights(w_in_ref, b_in_ref, w_out_ref, b_out_ref,
                    w_in_half, w_in_t, b_in_half, w_out_t, w_out_half, b_out_rows, w_wide, b_wide)
    fetch(((hw_ref, hw_raw), (ids_ref, rid_ref), (ids_ref, ids_raw), (zh_ref, zh_raw), (lab_ref, lab_raw)), sems)
    hw_full[...] = hw_raw[...].astype(jnp.float32)
    widen_planes(zh_raw, lab_raw, zh_full, lab_pad, slots)
    gather_rows(rid_ref, hw_full, hw_rows, slots, 0)
    hw_out[0:n_hw, :] = hw_rows[...].astype(jnp.bfloat16)
    put_ids(hw_out, n_hw, twice(ids_raw, slots), pair_cols.bit_length() - 1, pair_cols - 1)
    fill_planes(meta_ref[0], (own0_ref, own1_ref), (0, 0), zh_full, lab_pad, slots,
                half=half, rows_blk=rows_blk, depth_z=depth_z, slots=slots)
    fill_planes(1 - meta_ref[0], (None, send1_ref), (0, 0), zh_full, lab_pad, meta_ref[1],
                half=half, rows_blk=rows_blk, depth_z=depth_z, slots=slots)
    wz_copy.wait()

    def widen(w, carry):
        rows = wz_raw[w].astype(jnp.float32)
        for chunk, ref in zip(CHUNKS, (wz0_ref, wz1_ref)):
            for n, o in enumerate(chunk):
                ref[w, 8 * n:8 * n + 8, :] = rows[8 * o:8 * o + 8]
        return carry

    lax.fori_loop(0, 2 * pair_cols, widen, 0, unroll=8)


def add_zh(d, row, zh_accs):
    both = d[0] + d[1]
    now = [acc[row] for acc in zh_accs]
    for n, acc in enumerate(zh_accs):
        acc[row] = now[n] + both[8 * n:8 * n + 8]


def add_wz(d, col, wz_accs):
    now = [[acc[col + p] for p in range(2)] for acc in wz_accs]
    for n, acc in enumerate(wz_accs):
        for p in range(2):
            acc[col + p] = now[n][p] + d[p][8 * n:8 * n + 8]


def pick_level(top):
    level = jnp.zeros(top.shape, jnp.float32)
    for n, bound in enumerate(LEVEL_TOPS):
        level = jnp.where(top < bound, n + 1.0, level)
    return level


def level_scale(level, sign):
    scale = jnp.ones(level.shape, jnp.float32)
    for n in range(len(LEVEL_TOPS)):
        scale = jnp.where(level == n + 1.0, 2.0 ** (sign * LEVEL_BITS[n]), scale)
    return scale


def encode(value):
    level = pick_level(jnp.max(jnp.abs(value), axis=1, keepdims=True))
    code = jnp.broadcast_to(level, (value.shape[0], CODE_ROWS, value.shape[2]))
    return jnp.concatenate([value * level_scale(level, 1), code], axis=1).astype(jnp.float16)


def decode_half(value):
    value = value.astype(jnp.float32)
    n = value.shape[1] - CODE_ROWS
    return value[:, :n] * level_scale(value[:, n:n + 1, :], -1)


def read_runs(ids_ref, first, n):
    row = lax.shift_right_logical(first, 7)
    at = jnp.bitwise_and(first, 127)
    return [(ids_ref[row, at + j], ids_ref[row + 4, at + j]) for j in range(n)]


def decode_kernel(*refs, chunk, first, rows_blk, slots, pair_cols):
    n_hw = 2 * slots
    n_zh = rows_blk * ZC
    n_lab = slots // GROUP
    meta_ref, hw_own, hw_recv, z_own, z_recv = refs[:5]
    refs = refs[5:]
    z_base = 0
    if not first:
        hw_prev, wgt_prev = refs[:2]
        refs = refs[2:]
    wz_full, w_in_ref, w_in_t_ref, b_in_ref, w_out_t_ref, w_out_half_ref, b_out_ref = refs[:7]
    refs = refs[7:]
    if first:
        wz_out0, wz_out1, zh_out0, zh_out1, hw_out, wgt_out = refs[:6]
        refs = refs[6:]
    else:
        wz_out0, core_out, zh_out0, zh_out1, hw_out, wgt_keep = refs[:6]
        refs = refs[6:]
    (hw_full, zh_full, lab_full, hw_acc, w_in_acc, w_out_acc, b_out_acc, ids_ref, ids_sem) = refs[:9]
    bufs = (refs[9:13], refs[13:17])
    outs = (refs[17:19], refs[19:21])
    wz_accs, zh_accs, ids_vec, wgt_all = refs[21:23], refs[23:25], refs[25], refs[26]
    count = meta_ref[1]
    rel_own = meta_ref[7]

    spot_row = lax.broadcasted_iota(jnp.int32, (8, 128), 0)
    spot = jnp.bitwise_and(spot_row, 3) * 128 + lax.broadcasted_iota(jnp.int32, (8, 128), 1)
    own_ids = hw_own[n_hw:n_hw + 16, :].astype(jnp.float32).astype(jnp.int32)
    recv_ids = hw_recv[n_hw:n_hw + 16, :].astype(jnp.float32).astype(jnp.int32)
    is_own = spot < count
    ids = jnp.where(is_own, own_ids[0:8], recv_ids[0:8])
    rel = jnp.where(is_own, rel_own, 1 - rel_own)
    ids_vec[...] = jnp.where(spot_row < 4, ids + rel * rows_blk, 2 * ids)
    copy = pltpu.make_async_copy(ids_vec, ids_ref, ids_sem)
    copy.start()
    row = lax.broadcasted_iota(jnp.int32, (n_hw, 128), 0)
    hw_full[...] = jnp.where(row < 2 * count, hw_own[0:n_hw, :].astype(jnp.float32),
                             hw_recv[0:n_hw, :].astype(jnp.float32))
    for k, ref in ((0, z_own), (1, z_recv)):
        base = jnp.bitwise_xor(rel_own, k) * rows_blk
        for h in range(rows_blk):
            zh_full[base + h] = ref[z_base + h * ZC:z_base + (h + 1) * ZC, :].astype(jnp.float32)
    lab_row = lax.broadcasted_iota(jnp.int32, (n_lab, 128), 0)
    lab_lane = lax.broadcasted_iota(jnp.int32, (n_lab, 128), 1)
    place = GROUP * lab_row + lax.rem(lab_lane // ZC, GROUP)
    first_lab = z_base + n_zh
    lab_full[...] = jnp.where(place < count, z_own[first_lab:first_lab + n_lab, :].astype(jnp.float32),
                              z_recv[first_lab:first_lab + n_lab, :].astype(jnp.float32))
    for acc in wz_accs + zh_accs:
        acc[...] = jnp.zeros_like(acc)
    w_in_acc[...] = jnp.zeros_like(w_in_acc)
    w_out_acc[...] = jnp.zeros_like(w_out_acc)
    b_out_acc[...] = jnp.zeros_like(b_out_acc)
    copy.wait()

    groups = RUNS // GROUP
    n_ch = w_in_ref.shape[0]
    sel_row = lax.broadcasted_iota(jnp.int32, (2 * RUNS, ROWS), 0)
    sample = lax.broadcasted_iota(jnp.int32, (2 * RUNS, ROWS), 1)
    sample_run = lax.shift_right_logical(sample, 7) * GROUP + lax.shift_right_logical(jnp.bitwise_and(sample, 63), 4)
    sample_row = 2 * sample_run + jnp.bitwise_and(lax.shift_right_logical(sample, 6), 1)
    select = jnp.where(sel_row == sample_row, 1.0, 0.0).astype(jnp.bfloat16)
    for left_ref, dpre_ref in outs:
        left_ref[n_ch:, :] = select
    class_ids = lax.broadcasted_iota(jnp.int32, (CLS_ROWS, 128), 0).astype(jnp.float32)
    nt = (((1,), (1,)), ((), ()))

    def front(b, buf):
        feat_ref, hid_ref, slope_ref, logit_ref = buf
        runs = read_runs(ids_ref, RUNS * b, RUNS)
        for g in range(groups):
            pieces = []
            for p in range(2):
                for par in range(GROUP):
                    row, col = runs[GROUP * g + par]
                    at = pl.multiple_of(2 * RUNS * b, 2 * RUNS) + 2 * (GROUP * g + par) + p
                    total = hw_full[pl.ds(at, 1), :] + zh_full[row] + wz_full[col + p]
                    pieces.append(total.astype(jnp.bfloat16))
            feat = jnp.concatenate(pieces, axis=0)
            feat_ref[g * 128:(g + 1) * 128, :] = feat
            pre_all = jnp.dot(feat, w_in_ref[...], preferred_element_type=jnp.float32)
            for r in range(0, 128, STRIP):
                pre = pre_all[r:r + STRIP] + b_in_ref[...]
                t = jnp.tanh(pre)
                a = 1.0 + t
                u = pre * a
                at = g * 128 + r
                hid_ref[at:at + STRIP, :] = u.astype(jnp.bfloat16)
                slope_ref[at:at + STRIP, :] = a + u * (1.0 - t)
        logits = lax.dot_general(w_out_t_ref[...], hid_ref[...], nt, preferred_element_type=jnp.float32)
        logit_ref[...] = logits[0:CLS_ROWS, :]

    def middle(b, buf, out):
        feat_ref, hid_ref, slope_ref, logit_ref = buf
        left_ref, dpre_ref = out
        left_ref[0:n_ch, :] = jnp.transpose(feat_ref[...], (1, 0))
        dl_tiles = []
        b_part = None
        for g in range(groups):
            tile = logit_ref[:, g * 128:(g + 1) * 128] + b_out_ref[...]
            top = jnp.max(tile, axis=0, keepdims=True)
            e = jnp.exp(tile - top)
            inv = 1.0 / jnp.sum(e, axis=0, keepdims=True)
            lab_here = lab_full[pl.ds(groups * b + g, 1), :]
            onehot = jnp.where(class_ids == lab_here, 1.0, 0.0)
            dl = ((e * inv - onehot) * grad_scale).astype(jnp.bfloat16).astype(jnp.float32)
            b_part = dl if b_part is None else b_part + dl
            dl_tiles.append(dl)
        b_out_acc[...] += b_part
        dl_all = jnp.concatenate(dl_tiles, axis=1)
        dl_all = jnp.concatenate([dl_all, jnp.zeros((CLS_PAD - CLS_ROWS, ROWS), jnp.float32)], axis=0)
        dl_t = jnp.transpose(dl_all, (1, 0)).astype(jnp.bfloat16)
        w_out_acc[...] += jnp.dot(dl_all.astype(jnp.bfloat16), hid_ref[...], preferred_element_type=jnp.float32)
        for g in range(groups):
            dhid = jnp.dot(dl_t[g * 128:(g + 1) * 128], w_out_half_ref[...], preferred_element_type=jnp.float32)
            for r in range(0, 128, STRIP):
                at = g * 128 + r
                dpre_ref[at:at + STRIP, :] = (dhid[r:r + STRIP] * slope_ref[at:at + STRIP, :]).astype(jnp.bfloat16)

    def back(b, out):
        left_ref, dpre_ref = out
        dpre = dpre_ref[...]
        sums = jnp.dot(left_ref[...], dpre, preferred_element_type=jnp.float32)
        w_in_acc[...] += sums[0:n_ch]
        hw_acc[pl.ds(pl.multiple_of(2 * RUNS * b, 2 * RUNS), 2 * RUNS), :] = sums[n_ch:]
        runs = read_runs(ids_ref, RUNS * b, RUNS)
        for g in range(groups):
            dfeat = jnp.dot(dpre_ref[g * 128:(g + 1) * 128, :], w_in_t_ref[...], preferred_element_type=jnp.float32)
            for par in range(GROUP):
                d = [dfeat[p * 64 + par * ZC:p * 64 + (par + 1) * ZC] for p in range(2)]
                row, col = runs[GROUP * g + par]
                add_zh(d, row, zh_accs)
                add_wz(d, col, wz_accs)

    n_batch = slots // RUNS
    front(0, bufs[0])
    front(1, bufs[1])
    middle(0, bufs[0], outs[0])

    def step(k, carry):
        b = 2 * k
        front(b + 2, bufs[0])
        middle(b + 1, bufs[1], outs[1])
        back(b, outs[0])
        front(b + 3, bufs[1])
        middle(b + 2, bufs[0], outs[0])
        back(b + 1, outs[1])
        return carry

    lax.fori_loop(0, n_batch // 2 - 1, step, 0)
    middle(n_batch - 1, bufs[1], outs[1])
    back(n_batch - 2, outs[0])
    back(n_batch - 1, outs[1])
    tail = hw_acc[...]
    total = None
    for n in range(3):
        part = tail.astype(jnp.bfloat16)
        tail = tail - part.astype(jnp.float32)
        term = jnp.dot(part, w_in_t_ref[...], preferred_element_type=jnp.float32)
        total = term if total is None else total + term
    width = w_in_acc.shape[1]
    b_in_sum = jnp.sum(hw_acc[...], axis=0, keepdims=True)
    b_pad = jnp.concatenate([b_out_acc[...], jnp.zeros((128 - CLS_ROWS, 128), jnp.float32)], axis=0)
    b_out_sum = jnp.sum(jnp.transpose(b_pad, (1, 0)), axis=0, keepdims=True)
    b_out_sum = jnp.concatenate([b_out_sum, jnp.zeros((1, width - 128), jnp.float32)], axis=1)
    biases = jnp.concatenate([b_in_sum, b_out_sum, jnp.zeros((6, width), jnp.float32)], axis=0)
    weights = jnp.concatenate([w_in_acc[...], biases, w_out_acc[0:CLS_ROWS, :]], axis=0)
    put_zh(meta_ref, chunk, zh_accs, zh_out0, zh_out1)
    if first:
        hw_out[...] = total
        wgt_out[...] = weights
        put_wz(meta_ref, chunk, wz_accs, wz_out0, wz_out1)
        return
    hw_out[...] = total + hw_prev[...]
    wgt_all[...] = weights + wgt_prev[...]
    put_wz(meta_ref, chunk, wz_accs, wz_out0, core_out.at[0:2 * pair_cols])
    mid = wgt_all.shape[0] // 2
    mine = meta_ref[8] * mid
    wgt_keep[...] = split_lanes(wgt_all[pl.ds(pl.multiple_of(mine, 8), mid), :])
    core_out[2 * pair_cols:] = split_lanes(wgt_all[pl.ds(pl.multiple_of(mid - mine, 8), mid), :])


def split_lanes(value):
    return jnp.concatenate([value[:, :128], value[:, 128:]], axis=0).reshape(value.shape[0] // 4, 8, 128)


def put_zh(meta_ref, chunk, zh_accs, zh_out0, zh_out1):
    same = meta_ref[6] == chunk[0] // 2
    zh_out0[...] = jnp.where(same, zh_accs[0][...], zh_accs[1][...])
    zh_out1[...] = jnp.where(same, zh_accs[1][...], zh_accs[0][...])


def put_wz(meta_ref, chunk, wz_accs, wz_out0, wz_out1):
    same = meta_ref[2 + chunk[0]] == 0
    wz_out0[...] = jnp.where(same, wz_accs[0][...], wz_accs[1][...])
    wz_out1[...] = jnp.where(same, wz_accs[1][...], wz_accs[0][...])


def place_kernel(meta_ref, rid_ref, mine_ref, recv_ref, out_ref, *, slots):
    out_ref[...] = jnp.zeros_like(out_ref)
    count = meta_ref[1]

    def place(s, carry):
        r = rid_ref[0, s]
        for p in range(2):
            out_ref[pl.ds(2 * r + p, 1), :] = (mine_ref[pl.ds(2 * s + p, 1), :]
                                               + recv_ref[pl.ds(2 * (slots - count + s) + p, 1), :])
        return carry

    def place_eight(i, carry):
        for j in range(8):
            place(8 * i + j, carry)
        return carry

    lax.fori_loop(0, count // 8, place_eight, 0)
    lax.fori_loop(count // 8 * 8, count, place, 0)


def finish_kernel(meta_ref, zh_ref, w_mine_ref, w_other_ref,
                  zh_out, w_in_out, b_in_out, w_out_out, b_out_out, w_all, *, rows_blk):
    mid = w_all.shape[0] // 2
    mine = meta_ref[8] * mid
    for start, ref in ((mine, w_mine_ref), (mid - mine, w_other_ref)):
        flat = ref[...].reshape(2 * mid, 128)
        w_all[pl.ds(pl.multiple_of(start, 8), mid), :] = jnp.concatenate([flat[:mid], flat[mid:]], axis=1)
    n_ch = w_in_out.shape[0]
    w_in_out[...] = w_all[0:n_ch, :]
    b_in_out[...] = w_all[n_ch:n_ch + 1, :]
    b_out_out[...] = w_all[n_ch + 1:n_ch + 2, 0:b_out_out.shape[1]]
    w_out_out[...] = w_all[n_ch + 8:n_ch + 8 + w_out_out.shape[0], :]
    swapped = meta_ref[6]
    for n in range(2):
        base = jnp.bitwise_xor(swapped, n) * 8
        for z in range(8):
            zh_out[base + z] = zh_ref[n, pl.ds(z, rows_blk, stride=8), :]


def local(n_ha, n_wa, hw_plane, zh_plane, wz_plane, w_in, b_in, w_out, b_out,
          run_index, run_count, labels):
    rows_blk, cols_blk, channels = hw_plane.shape
    depth_z = zh_plane.shape[0]
    hidden = w_in.shape[1]
    classes = w_out.shape[1]
    slots = run_index.shape[1]
    half = depth_z // 2
    pair_cols = cols_blk // 2
    n_q = n_ha // 2
    n_zl = n_wa // 2
    n_hw = 2 * slots
    n_zh = rows_blk * ZC
    n_lab = slots // GROUP
    smem = pl.BlockSpec(memory_space=pltpu.SMEM)
    vmem = pl.BlockSpec(memory_space=pltpu.VMEM)
    hbm = pl.BlockSpec(memory_space=pltpu.HBM)
    f32 = jnp.float32
    bf16 = jnp.bfloat16

    ha = lax.axis_index("ha")
    wa = lax.axis_index("wa")
    y = ha // n_q
    my_q = ha % n_q
    b1 = wa // n_zl
    my_zl = wa % n_zl
    count = run_count[0]
    direct = n_q == 4 and n_zl == 2
    if direct:
        wz_pos = [(o ^ my_q) % 2 for o in range(4)]
        rest = [my_zl, y ^ b1, ha % 2, my_q]
    else:
        wz_pos = [jnp.int32(o // 2) for o in range(4)]
        rest = [jnp.int32(0), y, ha % 2, my_q]
    meta = jnp.stack([y, count] + wz_pos + rest).astype(jnp.int32)
    swap_y = [(i, (i + n_q) % n_ha) for i in range(n_ha)]

    n_rows, n_plane = n_hw + 16, n_zh + n_lab
    planes = (hw_plane.reshape(rows_blk * cols_blk, channels),
              zh_plane.reshape(depth_z * rows_blk, channels), labels[0], run_index)
    hw_raw = pltpu.VMEM((rows_blk * cols_blk, channels), bf16)
    plane_raw = [pltpu.VMEM((depth_z * rows_blk, channels), bf16), pltpu.VMEM((slots, 2 * depth_z), jnp.int32)]
    ids_raw = [pltpu.VMEM((1, slots), jnp.int32), pltpu.SMEM((1, slots), jnp.int32)]
    hw_wide = [pltpu.VMEM((rows_blk * cols_blk, channels), f32), pltpu.VMEM((n_hw, channels), f32)]
    plane_wide = [pltpu.VMEM((depth_z * rows_blk, channels), f32), pltpu.VMEM((2 * slots, 2 * depth_z), f32)]

    def call(kernel, name, operands, specs, outs, scratch, flops, limit=16):
        return pl.pallas_call(
            kernel,
            out_shape=[jax.ShapeDtypeStruct(shape, kind) for shape, kind in outs],
            in_specs=specs,
            out_specs=[vmem] * len(outs),
            scratch_shapes=scratch,
            compiler_params=pltpu.CompilerParams(vmem_limit_bytes=limit * 2**20),
            cost_estimate=pl.CostEstimate(flops=flops, bytes_accessed=2**20, transcendentals=0),
            name=name,
        )(*operands)

    sizes = dict(depth_z=depth_z, rows_blk=rows_blk, slots=slots, pair_cols=pair_cols)
    send0, = call(functools.partial(pack_plane_kernel, **sizes), "pack_plane", (meta, planes[1], planes[2]),
                  [smem] + [hbm] * 2, [((n_plane, channels), bf16)],
                  plane_raw + [pltpu.SemaphoreType.DMA((2,))] + plane_wide, 2 * 10**9, 60)
    recv0 = lax.ppermute(send0, "ha", swap_y)
    send0, hw_late, ids_late = lax.optimization_barrier((send0, planes[0], planes[3]))
    send_hw, = call(functools.partial(pack_rows_kernel, **sizes), "pack_rows", (meta, hw_late, ids_late),
                    [smem] + [hbm] * 2, [((n_rows, channels), bf16)],
                    [hw_raw] + ids_raw + [pltpu.SemaphoreType.DMA((3,))] + hw_wide, 3 * 10**9, 12)
    recv_hw = lax.ppermute(send_hw, "ha", swap_y)
    later = lax.optimization_barrier((send_hw,) + planes)
    own_hw, own0, own1, send1, wzf0, wzf1, *shared = call(
        functools.partial(pack_own_kernel, **sizes), "pack_own",
        (meta,) + later[1:] + (wz_plane, w_in, b_in.reshape(1, hidden), w_out.T, b_out.reshape(1, classes)),
        [smem] + [hbm] * 5 + [vmem] * 4,
        [((n_rows, channels), bf16)] + [((n_plane, channels), bf16)] * 3 + [((cols_blk, ZC, channels), f32)] * 2
        + [((channels, hidden), bf16), ((hidden, channels), bf16), ((1, hidden), f32), ((CLS_PAD, hidden), bf16),
           ((CLS_PAD, hidden), bf16), ((CLS_ROWS, 128), f32)],
        [hw_raw] + plane_raw + ids_raw + [pltpu.SemaphoreType.DMA((5,))] + hw_wide + plane_wide
        + [pltpu.VMEM((cols_blk, half, channels), bf16), pltpu.SemaphoreType.DMA,
           pltpu.VMEM((CLS_PAD, hidden), f32), pltpu.VMEM((8, 128), f32)], 3 * 10**9, 16)
    send1, recv0, recv_hw = lax.optimization_barrier((send1, recv0, recv_hw))
    recv1 = lax.ppermute(send1, "ha", swap_y)

    shared = tuple(shared)
    wgt_rows = channels + 8 + CLS_ROWS
    mid = wgt_rows // 2
    buf = [pltpu.VMEM((ROWS, channels), bf16), pltpu.VMEM((ROWS, hidden), bf16),
           pltpu.VMEM((ROWS, hidden), f32), pltpu.VMEM((CLS_ROWS, ROWS), f32)]
    out_buf = [pltpu.VMEM((channels + 2 * RUNS, ROWS), bf16), pltpu.VMEM((ROWS, hidden), bf16)]
    work = [pltpu.VMEM((n_hw, channels), f32), pltpu.VMEM((2 * rows_blk, ZC, channels), f32),
            pltpu.VMEM((n_lab, 128), f32), pltpu.VMEM((n_hw, hidden), f32),
            pltpu.VMEM((channels, hidden), f32), pltpu.VMEM((CLS_PAD, hidden), f32),
            pltpu.VMEM((CLS_ROWS, 128), f32), pltpu.SMEM((8, 128), jnp.int32), pltpu.SemaphoreType.DMA]
    work += buf + buf + out_buf + out_buf
    work += [pltpu.VMEM((cols_blk, 8, channels), f32)] * 2 + [pltpu.VMEM((2 * rows_blk, 8, channels), f32)] * 2
    work += [pltpu.VMEM((8, 128), jnp.int32), pltpu.VMEM((wgt_rows, hidden), f32)]
    sums = [((cols_blk, 8, channels), f32)] * 2 + [((2 * rows_blk, 8, channels), f32)] * 2
    def decode(n, sources, outs):
        return call(
            functools.partial(decode_kernel, chunk=CHUNKS[n], first=n == 0, rows_blk=rows_blk,
                              slots=slots, pair_cols=pair_cols), "decode%d" % n,
            (meta,) + sources + (wzf0, wzf1)[n:n + 1] + shared,
            [smem] + [vmem] * (len(sources) + 8 - 1), outs, work, 22 * 10**9, 20)

    wz0a, wz0b, zh0a, zh0b, hw0, wgt0 = decode(
        0, (own_hw, recv_hw, own0, recv0), sums + [((n_hw, channels), f32), ((wgt_rows, hidden), f32)])
    recv1, wz0a, wz0b, zh0a, zh0b = lax.optimization_barrier((recv1, wz0a, wz0b, zh0a, zh0b))
    wz1a, core_send, zh1a, zh1b, hw1, w_keep = decode(
        1, (own_hw, recv_hw, own1, recv1, hw0, wgt0),
        [sums[0], ((cols_blk + mid // 4, 8, channels), f32), sums[2], sums[3],
         ((n_hw, channels), f32), ((mid // 4, 8, channels), f32)])

    def place(mine, recv):
        return call(
            functools.partial(place_kernel, slots=slots), "place", (meta, run_index, mine, recv),
            [smem, smem, vmem, vmem], [((rows_blk * cols_blk, channels), f32)], [],
            3 * 10**9, 4)[0].reshape(rows_blk, cols_blk, channels)

    zpart = half // n_zl
    moves = []
    for a in range(n_ha):
        for b in range(n_wa):
            moves.append((a * n_wa + b, ((b // n_zl) * n_q + a % n_q) * n_wa + (a // n_q) * n_zl + b % n_zl))
    barrier = lax.optimization_barrier

    if direct:
        def ha_perm(pairs):
            return [(top * n_q + a, top * n_q + b) for top in range(2) for a, b in pairs]

        def flat(value):
            return value.reshape(2 * rows_blk * 8, channels)

        n_part = rows_blk * 8
        zh0a, zh0b = flat(zh0a), flat(zh0b)
        zh1a, zh1b = flat(zh1a), flat(zh1b)
        wz0r = ppermute_xor(wz0b, "ha", n_ha, 1)
        zh0r = ppermute_xor(zh0b, "wa", n_wa, 1)
        stays = y == b1
        wz0r, zh0r, wz1a, core_send, zh1a, zh1b, hw1, w_keep = barrier(
            (wz0r, zh0r, wz1a, core_send, zh1a, zh1b, hw1, w_keep))
        def corner(value, ha_mask, wa_mask):
            pairs = [(a * n_wa + b, (a ^ ha_mask) * n_wa + (b ^ wa_mask)) for a in range(n_ha) for b in range(n_wa)]
            return lax.ppermute(value, ("ha", "wa"), pairs)

        zh1r = ppermute_xor(encode(zh1b[None]), "wa", n_wa, 1)
        core_recv = ppermute_xor(core_send, "ha", n_ha, 1)
        hw_recv = lax.ppermute(encode(hw1[None]), "ha", swap_y)
        near0 = wz0a + wz0r
        near1 = wz1a + core_recv[:cols_blk]
        outer = (my_q == 0) | (my_q == 3)
        far = ppermute_xor(encode(jnp.where(outer, near1, near0).reshape(1, cols_blk * 8, channels)), "ha", n_ha, 2)
        part0 = zh0a + zh0r
        w = w_keep + core_recv[cols_blk:]
        wr = ppermute_xor(w, "wa", n_wa, 2)
        zh1r, wr, hw_recv = barrier((zh1r, wr, hw_recv))
        both = jnp.stack([part0, zh1a + decode_half(zh1r)[0]])
        zhf = ppermute_xor(encode(both[:, n_part:]), "wa", n_wa, 2)
        w = w + wr
        wr = [ppermute_xor(w, "ha", n_ha, mask) for mask in (n_q, 2, n_q + 2)]
        zhf, wr, far, hw_recv = barrier((zhf, wr, far, hw_recv))
        zh_code = encode(both[:, :n_part] + decode_half(zhf))
        zhm = jnp.where(stays, zh_code, corner(zh_code, n_q, 2))
        w = (w + wr[0]) + (wr[1] + wr[2])
        w_mine = w + ppermute_xor(w, "wa", n_wa, 1)
        w_other = ppermute_xor(w, "ha", n_ha, 1) + corner(w, 1, 1)
        hw_grad = place(hw1, decode_half(hw_recv)[0])
        wz_grad = jnp.where(outer, near0, near1) + decode_half(far).reshape(near1.shape)
        zh_grad, w_in_grad, b_in_grad, w_out_grad, b_out_grad = call(
            functools.partial(finish_kernel, rows_blk=rows_blk), "finish", (meta, decode_half(zhm), w_mine, w_other),
            [smem] + [vmem] * 3,
            [((2 * 8, rows_blk, channels), f32), ((channels, hidden), f32), ((1, hidden), f32),
             ((classes, hidden), f32), ((1, classes), f32)], [pltpu.VMEM((wgt_rows, hidden), f32)], 10**9, 4)
        return hw_grad, zh_grad, wz_grad, w_in_grad, b_in_grad[0], w_out_grad.T, b_out_grad[0]

    wz1b = core_send[:cols_blk]
    hw_grad = place(hw1, lax.ppermute(hw1, "ha", swap_y))
    wz_all = jnp.stack([wz0a, wz1a, wz1b, wz0b])
    wz_all = wz_all.transpose(1, 0, 2, 3).reshape(cols_blk, n_q, half // n_q, channels)
    part = jnp.take(wz_all.transpose(1, 0, 2, 3), jnp.arange(n_q) ^ my_q, axis=0)
    bit = 1
    while bit < n_q:
        part = part.reshape(part.shape[0] // 2, 2, cols_blk, half // n_q, channels)
        part = part[:, 0] + ppermute_xor(part[:, 1], "ha", n_ha, bit)
        bit *= 2
    wz_grad = part[0]
    zh_all = jnp.stack([zh0a, zh1a, zh1b, zh0b], axis=1)
    zh_all = zh_all.reshape(2, rows_blk, n_zl, zpart, channels).transpose(0, 2, 1, 3, 4)
    part = jnp.take(zh_all, jnp.arange(n_zl) ^ my_zl, axis=1)
    part = jnp.take(part, jnp.arange(2) ^ b1, axis=0)
    bit = 1
    while bit < n_zl:
        part = part.reshape(2, part.shape[1] // 2, 2, rows_blk, zpart, channels)
        part = part[:, :, 0] + ppermute_xor(part[:, :, 1], "wa", n_wa, bit)
        bit *= 2
    part = part[:, 0]
    part = part[0] + ppermute_xor(part[1], "wa", n_wa, n_zl)
    zh_grad = lax.ppermute(part, ("ha", "wa"), moves).transpose(1, 0, 2)
    w = w_keep + ppermute_xor(core_send[cols_blk:], "ha", n_ha, 1)
    bit = 2
    while bit < n_ha:
        w = w + ppermute_xor(w, "ha", n_ha, bit)
        bit *= 2
    bit = 1
    while bit < n_wa:
        w = w + ppermute_xor(w, "wa", n_wa, bit)
        bit *= 2
    w_other = ppermute_xor(w, "ha", n_ha, 1)
    w, w_other = [jnp.concatenate(jnp.split(v.reshape(2 * mid, 128), 2), axis=1) for v in (w, w_other)]
    upper = ha % 2 == 1
    wgt = jnp.concatenate([jnp.where(upper, w_other, w), jnp.where(upper, w, w_other)])
    first = channels + 8
    return (hw_grad, zh_grad, wz_grad, wgt[:channels], wgt[channels],
            wgt[first:first + classes].T, wgt[channels + 1, :classes])


def solution(mesh):
    placed = (
        P("ha", "wa", None),
        P(None, "ha", None),
        P("wa", None, None),
        P(),
        P(),
        P(),
        P(),
        P(("ha", "wa"), None),
        P(("ha", "wa")),
        P(("ha", "wa"), None, None),
    )
    return jax.shard_map(
        functools.partial(local, mesh.shape["ha"], mesh.shape["wa"]),
        mesh=mesh,
        in_specs=placed,
        out_specs=(
            P("ha", "wa", None),
            P("wa", "ha", None),
            P("wa", "ha", None),
            P(),
            P(),
            P(),
            P(),
        ),
        check_vma=False,
    )
```

```python
import functools

import jax
import jax.numpy as jnp
from jax import lax
from jax.experimental import pallas as pl
from jax.experimental.pallas import tpu as pltpu
from jax.sharding import PartitionSpec as P

grad_scale = 0.25
CLS_ROWS = 24
CLS_PAD = 32
CHUNKS = ((0, 3), (1, 2))
ZC = 16
RUNS = 16
GROUP = 4
ROWS = RUNS * 2 * ZC
STRIP = 32
LEVEL_TOPS = tuple(2.0 ** e for e in (4, -7, -18, -29, -40))
LEVEL_BITS = (11, 22, 33, 44, 55)
CODE_ROWS = 16


def ppermute_xor(value, axis, size, mask):
    return lax.ppermute(value, axis, [(i, i ^ mask) for i in range(size)])


def fill_planes(side, refs, bases, zh_full, lab_pad, start, *, half, rows_blk, depth_z, slots):
    n_zh = rows_blk * ZC
    n_lab = slots // GROUP
    lane = lax.rem(lax.broadcasted_iota(jnp.int32, (n_lab, 128), 1), depth_z)
    z0 = side * half
    labs = [lab_pad[pl.ds(start + par, n_lab, stride=GROUP), :] for par in range(GROUP)]
    for chunk, ref, base in zip(CHUNKS, refs, bases):
        if ref is None:
            continue
        for h in range(rows_blk):
            parts = [zh_full[pl.ds((z0 + 8 * o) * rows_blk + h, 8, stride=rows_blk), :] for o in chunk]
            ref[base + h * ZC:base + (h + 1) * ZC, :] = jnp.concatenate(parts, axis=0).astype(jnp.bfloat16)
        merged = jnp.zeros((n_lab, 128), jnp.float32)
        for par in range(GROUP):
            for n, o in enumerate(chunk):
                to = par * ZC + 8 * n
                rolled = pltpu.roll(labs[par], jnp.bitwise_and(256 + to - (z0 + 8 * o), 127), 1)
                merged = jnp.where((lane >= to) & (lane < to + 8), rolled, merged)
        ref[base + n_zh:base + n_zh + n_lab, :] = merged.astype(jnp.bfloat16)


def fetch(pairs, sems):
    copies = [pltpu.make_async_copy(src, dst, sems.at[n]) for n, (src, dst) in enumerate(pairs)]
    for copy in copies:
        copy.start()
    for copy in copies:
        copy.wait()


def widen_planes(zh_raw, lab_raw, zh_full, lab_pad, slots):
    zh_full[...] = zh_raw[...].astype(jnp.float32)
    lab_pad[0:slots, :] = jnp.zeros((slots, lab_raw.shape[1]), jnp.float32)
    lab_pad[slots:, :] = lab_raw[...].astype(jnp.float32)


def twice(ids_raw, slots):
    ids = [ids_raw[:, k * 128:(k + 1) * 128] for k in range(slots // 128)]
    return jnp.concatenate(ids + ids, axis=0)


def gather_rows(rid_ref, hw_full, hw_rows, slots, shift):
    def gather_step(i, carry):
        for j in range(8):
            s = i * 8 + j
            r = rid_ref[0, jnp.maximum(s - shift, 0)]
            for p in range(2):
                hw_rows[pl.ds(2 * s + p, 1), :] = hw_full[pl.ds(2 * r + p, 1), :]
        return carry

    lax.fori_loop(0, slots // 8, gather_step, 0)


def put_ids(ref, base, ids, shift_bits, keep):
    padded = jnp.concatenate([ids, jnp.zeros_like(ids)], axis=0)
    high = lax.shift_right_logical(padded, shift_bits)
    low = jnp.bitwise_and(padded, keep)
    row = lax.broadcasted_iota(jnp.int32, padded.shape, 0)
    both = jnp.where(row < 4, high, pltpu.roll(low, 4, 0))
    ref[base:base + 16, :] = both.astype(jnp.float32).astype(jnp.bfloat16)


def pack_plane_kernel(meta_ref, zh_ref, lab_ref, send_ref, zh_raw, lab_raw, sems, zh_full, lab_pad,
                      *, depth_z, rows_blk, slots, pair_cols):
    fetch(((zh_ref, zh_raw), (lab_ref, lab_raw)), sems)
    widen_planes(zh_raw, lab_raw, zh_full, lab_pad, slots)
    fill_planes(1 - meta_ref[0], (send_ref, None), (0, 0), zh_full, lab_pad, meta_ref[1],
                half=depth_z // 2, rows_blk=rows_blk, depth_z=depth_z, slots=slots)


def pack_rows_kernel(meta_ref, hw_ref, ids_ref, send_ref, hw_raw, ids_raw, rid_ref, sems, hw_full, hw_rows,
                     *, depth_z, rows_blk, slots, pair_cols):
    n_hw = 2 * slots
    count = meta_ref[1]
    fetch(((hw_ref, hw_raw), (ids_ref, rid_ref), (ids_ref, ids_raw)), sems)
    hw_full[...] = hw_raw[...].astype(jnp.float32)
    ids = twice(ids_raw, slots)
    gather_rows(rid_ref, hw_full, hw_rows, slots, slots - count)
    send_ref[0:n_hw, :] = hw_rows[...].astype(jnp.bfloat16)
    down = slots - count
    lanes = jnp.bitwise_and(down, 127)
    rows = lax.shift_right_logical(down, 7)
    turned = pltpu.roll(ids, lanes, 1)
    here = pltpu.roll(turned, rows, 0)
    before = pltpu.roll(turned, jnp.bitwise_and(rows + 1, 7), 0)
    lane = lax.broadcasted_iota(jnp.int32, ids.shape, 1)
    put_ids(send_ref, n_hw, jnp.where(lane < lanes, before, here), pair_cols.bit_length() - 1, pair_cols - 1)


def prepare_weights(w_in_ref, b_in_ref, w_out_ref, b_out_ref,
                    w_in_half, w_in_t, b_in_half, w_out_t, w_out_half, b_out_rows, w_wide, b_wide):
    w_in = w_in_ref[...].astype(jnp.float32)
    w_in_half[...] = (w_in * 0.5).astype(jnp.bfloat16)
    w_in_t[...] = jnp.transpose(w_in, (1, 0)).astype(jnp.bfloat16)
    b_in_half[...] = b_in_ref[...] * 0.5
    classes = w_out_ref.shape[0]
    w_wide[...] = jnp.zeros_like(w_wide)
    w_wide[0:classes, :] = w_out_ref[...].astype(jnp.float32)
    turned = w_wide[...]
    w_out_t[...] = turned.astype(jnp.bfloat16)
    w_out_half[...] = (turned * 0.5).astype(jnp.bfloat16)
    b_wide[...] = jnp.full_like(b_wide, -1e30)
    b_wide[0:1, 0:classes] = b_out_ref[...]
    b_out_rows[...] = jnp.broadcast_to(jnp.transpose(b_wide[...], (1, 0))[0:CLS_ROWS, 0:1], (CLS_ROWS, 128))


def pack_own_kernel(meta_ref, hw_ref, zh_ref, lab_ref, ids_ref, wz_ref, w_in_ref, b_in_ref, w_out_ref, b_out_ref,
                    hw_out, own0_ref, own1_ref, send1_ref, wz0_ref, wz1_ref,
                    w_in_half, w_in_t, b_in_half, w_out_t, w_out_half, b_out_rows,
                    hw_raw, zh_raw, lab_raw, ids_raw, rid_ref, sems,
                    hw_full, hw_rows, zh_full, lab_pad, wz_raw, wz_sem, w_wide, b_wide,
                    *, depth_z, rows_blk, slots, pair_cols):
    half = depth_z // 2
    n_hw = 2 * slots
    z0 = pl.multiple_of(meta_ref[0] * half, half)
    wz_copy = pltpu.make_async_copy(wz_ref.at[:, pl.ds(z0, half), :], wz_raw, wz_sem)
    wz_copy.start()
    prepare_weights(w_in_ref, b_in_ref, w_out_ref, b_out_ref,
                    w_in_half, w_in_t, b_in_half, w_out_t, w_out_half, b_out_rows, w_wide, b_wide)
    fetch(((hw_ref, hw_raw), (ids_ref, rid_ref), (ids_ref, ids_raw), (zh_ref, zh_raw), (lab_ref, lab_raw)), sems)
    hw_full[...] = hw_raw[...].astype(jnp.float32)
    widen_planes(zh_raw, lab_raw, zh_full, lab_pad, slots)
    gather_rows(rid_ref, hw_full, hw_rows, slots, 0)
    hw_out[0:n_hw, :] = hw_rows[...].astype(jnp.bfloat16)
    put_ids(hw_out, n_hw, twice(ids_raw, slots), pair_cols.bit_length() - 1, pair_cols - 1)
    fill_planes(meta_ref[0], (own0_ref, own1_ref), (0, 0), zh_full, lab_pad, slots,
                half=half, rows_blk=rows_blk, depth_z=depth_z, slots=slots)
    fill_planes(1 - meta_ref[0], (None, send1_ref), (0, 0), zh_full, lab_pad, meta_ref[1],
                half=half, rows_blk=rows_blk, depth_z=depth_z, slots=slots)
    wz_copy.wait()

    def widen(w, carry):
        rows = wz_raw[w].astype(jnp.float32)
        for chunk, ref in zip(CHUNKS, (wz0_ref, wz1_ref)):
            for n, o in enumerate(chunk):
                ref[w, 8 * n:8 * n + 8, :] = rows[8 * o:8 * o + 8]
        return carry

    lax.fori_loop(0, 2 * pair_cols, widen, 0, unroll=8)


def add_zh(d, row, zh_accs):
    both = d[0] + d[1]
    now = [acc[row] for acc in zh_accs]
    for n, acc in enumerate(zh_accs):
        acc[row] = now[n] + both[8 * n:8 * n + 8]


def add_wz(d, col, wz_accs):
    now = [[acc[col + p] for p in range(2)] for acc in wz_accs]
    for n, acc in enumerate(wz_accs):
        for p in range(2):
            acc[col + p] = now[n][p] + d[p][8 * n:8 * n + 8]


def pick_level(top):
    level = jnp.zeros(top.shape, jnp.float32)
    for n, bound in enumerate(LEVEL_TOPS):
        level = jnp.where(top < bound, n + 1.0, level)
    return level


def level_scale(level, sign):
    scale = jnp.ones(level.shape, jnp.float32)
    for n in range(len(LEVEL_TOPS)):
        scale = jnp.where(level == n + 1.0, 2.0 ** (sign * LEVEL_BITS[n]), scale)
    return scale


def encode(value):
    level = pick_level(jnp.max(jnp.abs(value), axis=1, keepdims=True))
    code = jnp.broadcast_to(level, (value.shape[0], CODE_ROWS, value.shape[2]))
    return jnp.concatenate([value * level_scale(level, 1), code], axis=1).astype(jnp.float16)


def decode_half(value):
    value = value.astype(jnp.float32)
    n = value.shape[1] - CODE_ROWS
    return value[:, :n] * level_scale(value[:, n:n + 1, :], -1)


def read_runs(ids_ref, first, n):
    row = lax.shift_right_logical(first, 7)
    at = jnp.bitwise_and(first, 127)
    return [(ids_ref[row, at + j], ids_ref[row + 4, at + j]) for j in range(n)]


def decode_kernel(*refs, chunk, first, rows_blk, slots, pair_cols):
    n_hw = 2 * slots
    n_zh = rows_blk * ZC
    n_lab = slots // GROUP
    meta_ref, hw_own, hw_recv, z_own, z_recv = refs[:5]
    refs = refs[5:]
    z_base = 0
    if not first:
        hw_prev, wgt_prev = refs[:2]
        refs = refs[2:]
    wz_full, w_in_ref, w_in_t_ref, b_in_ref, w_out_t_ref, w_out_half_ref, b_out_ref = refs[:7]
    refs = refs[7:]
    if first:
        wz_out0, wz_out1, zh_out0, zh_out1, hw_out, wgt_out = refs[:6]
        refs = refs[6:]
    else:
        wz_out0, core_out, zh_out0, zh_out1, hw_out, wgt_keep = refs[:6]
        refs = refs[6:]
    (hw_full, zh_full, lab_full, hw_acc, w_in_acc, w_out_acc, b_out_acc, ids_ref, ids_sem) = refs[:9]
    bufs = (refs[9:13], refs[13:17])
    outs = (refs[17:19], refs[19:21])
    wz_accs, zh_accs, ids_vec, wgt_all = refs[21:23], refs[23:25], refs[25], refs[26]
    count = meta_ref[1]
    rel_own = meta_ref[7]

    spot_row = lax.broadcasted_iota(jnp.int32, (8, 128), 0)
    spot = jnp.bitwise_and(spot_row, 3) * 128 + lax.broadcasted_iota(jnp.int32, (8, 128), 1)
    own_ids = hw_own[n_hw:n_hw + 16, :].astype(jnp.float32).astype(jnp.int32)
    recv_ids = hw_recv[n_hw:n_hw + 16, :].astype(jnp.float32).astype(jnp.int32)
    is_own = spot < count
    ids = jnp.where(is_own, own_ids[0:8], recv_ids[0:8])
    rel = jnp.where(is_own, rel_own, 1 - rel_own)
    ids_vec[...] = jnp.where(spot_row < 4, ids + rel * rows_blk, 2 * ids)
    copy = pltpu.make_async_copy(ids_vec, ids_ref, ids_sem)
    copy.start()
    row = lax.broadcasted_iota(jnp.int32, (n_hw, 128), 0)
    hw_full[...] = jnp.where(row < 2 * count, hw_own[0:n_hw, :].astype(jnp.float32),
                             hw_recv[0:n_hw, :].astype(jnp.float32))
    for k, ref in ((0, z_own), (1, z_recv)):
        base = jnp.bitwise_xor(rel_own, k) * rows_blk
        for h in range(rows_blk):
            zh_full[base + h] = ref[z_base + h * ZC:z_base + (h + 1) * ZC, :].astype(jnp.float32)
    lab_row = lax.broadcasted_iota(jnp.int32, (n_lab, 128), 0)
    lab_lane = lax.broadcasted_iota(jnp.int32, (n_lab, 128), 1)
    place = GROUP * lab_row + lax.rem(lab_lane // ZC, GROUP)
    first_lab = z_base + n_zh
    lab_full[...] = jnp.where(place < count, z_own[first_lab:first_lab + n_lab, :].astype(jnp.float32),
                              z_recv[first_lab:first_lab + n_lab, :].astype(jnp.float32))
    for acc in wz_accs + zh_accs:
        acc[...] = jnp.zeros_like(acc)
    w_in_acc[...] = jnp.zeros_like(w_in_acc)
    w_out_acc[...] = jnp.zeros_like(w_out_acc)
    b_out_acc[...] = jnp.zeros_like(b_out_acc)
    copy.wait()

    groups = RUNS // GROUP
    n_ch = w_in_ref.shape[0]
    sel_row = lax.broadcasted_iota(jnp.int32, (2 * RUNS, ROWS), 0)
    sample = lax.broadcasted_iota(jnp.int32, (2 * RUNS, ROWS), 1)
    sample_run = lax.shift_right_logical(sample, 7) * GROUP + lax.shift_right_logical(jnp.bitwise_and(sample, 63), 4)
    sample_row = 2 * sample_run + jnp.bitwise_and(lax.shift_right_logical(sample, 6), 1)
    select = jnp.where(sel_row == sample_row, 1.0, 0.0).astype(jnp.bfloat16)
    for left_ref, dpre_ref in outs:
        left_ref[n_ch:, :] = select
    class_ids = lax.broadcasted_iota(jnp.int32, (CLS_ROWS, 128), 0).astype(jnp.float32)
    nt = (((1,), (1,)), ((), ()))

    def front(b, buf):
        feat_ref, hid_ref, slope_ref, logit_ref = buf
        runs = read_runs(ids_ref, RUNS * b, RUNS)
        for g in range(groups):
            pieces = []
            for p in range(2):
                for par in range(GROUP):
                    row, col = runs[GROUP * g + par]
                    at = pl.multiple_of(2 * RUNS * b, 2 * RUNS) + 2 * (GROUP * g + par) + p
                    total = hw_full[pl.ds(at, 1), :] + zh_full[row] + wz_full[col + p]
                    pieces.append(total.astype(jnp.bfloat16))
            feat = jnp.concatenate(pieces, axis=0)
            feat_ref[g * 128:(g + 1) * 128, :] = feat
            pre_all = jnp.dot(feat, w_in_ref[...], preferred_element_type=jnp.float32)
            for r in range(0, 128, STRIP):
                pre = pre_all[r:r + STRIP] + b_in_ref[...]
                t = jnp.tanh(pre)
                a = 1.0 + t
                u = pre * a
                at = g * 128 + r
                hid_ref[at:at + STRIP, :] = u.astype(jnp.bfloat16)
                slope_ref[at:at + STRIP, :] = a + u * (1.0 - t)
        logits = lax.dot_general(w_out_t_ref[...], hid_ref[...], nt, preferred_element_type=jnp.float32)
        logit_ref[...] = logits[0:CLS_ROWS, :]

    def middle(b, buf, out):
        feat_ref, hid_ref, slope_ref, logit_ref = buf
        left_ref, dpre_ref = out
        left_ref[0:n_ch, :] = jnp.transpose(feat_ref[...], (1, 0))
        dl_tiles = []
        b_part = None
        for g in range(groups):
            tile = logit_ref[:, g * 128:(g + 1) * 128] + b_out_ref[...]
            top = jnp.max(tile, axis=0, keepdims=True)
            e = jnp.exp(tile - top)
            inv = 1.0 / jnp.sum(e, axis=0, keepdims=True)
            lab_here = lab_full[pl.ds(groups * b + g, 1), :]
            onehot = jnp.where(class_ids == lab_here, 1.0, 0.0)
            dl = ((e * inv - onehot) * grad_scale).astype(jnp.bfloat16).astype(jnp.float32)
            b_part = dl if b_part is None else b_part + dl
            dl_tiles.append(dl)
        b_out_acc[...] += b_part
        dl_all = jnp.concatenate(dl_tiles, axis=1)
        dl_all = jnp.concatenate([dl_all, jnp.zeros((CLS_PAD - CLS_ROWS, ROWS), jnp.float32)], axis=0)
        dl_t = jnp.transpose(dl_all, (1, 0)).astype(jnp.bfloat16)
        w_out_acc[...] += jnp.dot(dl_all.astype(jnp.bfloat16), hid_ref[...], preferred_element_type=jnp.float32)
        for g in range(groups):
            dhid = jnp.dot(dl_t[g * 128:(g + 1) * 128], w_out_half_ref[...], preferred_element_type=jnp.float32)
            for r in range(0, 128, STRIP):
                at = g * 128 + r
                dpre_ref[at:at + STRIP, :] = (dhid[r:r + STRIP] * slope_ref[at:at + STRIP, :]).astype(jnp.bfloat16)

    def back(b, out):
        left_ref, dpre_ref = out
        dpre = dpre_ref[...]
        sums = jnp.dot(left_ref[...], dpre, preferred_element_type=jnp.float32)
        w_in_acc[...] += sums[0:n_ch]
        hw_acc[pl.ds(pl.multiple_of(2 * RUNS * b, 2 * RUNS), 2 * RUNS), :] = sums[n_ch:]
        runs = read_runs(ids_ref, RUNS * b, RUNS)
        for g in range(groups):
            dfeat = jnp.dot(dpre_ref[g * 128:(g + 1) * 128, :], w_in_t_ref[...], preferred_element_type=jnp.float32)
            for par in range(GROUP):
                d = [dfeat[p * 64 + par * ZC:p * 64 + (par + 1) * ZC] for p in range(2)]
                row, col = runs[GROUP * g + par]
                add_zh(d, row, zh_accs)
                add_wz(d, col, wz_accs)

    n_batch = slots // RUNS
    front(0, bufs[0])
    front(1, bufs[1])
    middle(0, bufs[0], outs[0])

    def step(k, carry):
        b = 2 * k
        front(b + 2, bufs[0])
        middle(b + 1, bufs[1], outs[1])
        back(b, outs[0])
        front(b + 3, bufs[1])
        middle(b + 2, bufs[0], outs[0])
        back(b + 1, outs[1])
        return carry

    lax.fori_loop(0, n_batch // 2 - 1, step, 0)
    middle(n_batch - 1, bufs[1], outs[1])
    back(n_batch - 2, outs[0])
    back(n_batch - 1, outs[1])
    tail = hw_acc[...]
    total = None
    for n in range(3):
        part = tail.astype(jnp.bfloat16)
        tail = tail - part.astype(jnp.float32)
        term = jnp.dot(part, w_in_t_ref[...], preferred_element_type=jnp.float32)
        total = term if total is None else total + term
    width = w_in_acc.shape[1]
    b_in_sum = jnp.sum(hw_acc[...], axis=0, keepdims=True)
    b_pad = jnp.concatenate([b_out_acc[...], jnp.zeros((128 - CLS_ROWS, 128), jnp.float32)], axis=0)
    b_out_sum = jnp.sum(jnp.transpose(b_pad, (1, 0)), axis=0, keepdims=True)
    b_out_sum = jnp.concatenate([b_out_sum, jnp.zeros((1, width - 128), jnp.float32)], axis=1)
    biases = jnp.concatenate([b_in_sum, b_out_sum, jnp.zeros((6, width), jnp.float32)], axis=0)
    weights = jnp.concatenate([w_in_acc[...], biases, w_out_acc[0:CLS_ROWS, :]], axis=0)
    put_zh(meta_ref, chunk, zh_accs, zh_out0, zh_out1)
    if first:
        hw_out[...] = total
        wgt_out[...] = weights
        put_wz(meta_ref, chunk, wz_accs, wz_out0, wz_out1)
        return
    hw_out[...] = total + hw_prev[...]
    wgt_all[...] = weights + wgt_prev[...]
    put_wz(meta_ref, chunk, wz_accs, wz_out0, core_out.at[0:2 * pair_cols])
    mid = wgt_all.shape[0] // 2
    mine = meta_ref[8] * mid
    wgt_keep[...] = split_lanes(wgt_all[pl.ds(pl.multiple_of(mine, 8), mid), :])
    core_out[2 * pair_cols:] = split_lanes(wgt_all[pl.ds(pl.multiple_of(mid - mine, 8), mid), :])


def split_lanes(value):
    return jnp.concatenate([value[:, :128], value[:, 128:]], axis=0).reshape(value.shape[0] // 4, 8, 128)


def put_zh(meta_ref, chunk, zh_accs, zh_out0, zh_out1):
    same = meta_ref[6] == chunk[0] // 2
    zh_out0[...] = jnp.where(same, zh_accs[0][...], zh_accs[1][...])
    zh_out1[...] = jnp.where(same, zh_accs[1][...], zh_accs[0][...])


def put_wz(meta_ref, chunk, wz_accs, wz_out0, wz_out1):
    same = meta_ref[2 + chunk[0]] == 0
    wz_out0[...] = jnp.where(same, wz_accs[0][...], wz_accs[1][...])
    wz_out1[...] = jnp.where(same, wz_accs[1][...], wz_accs[0][...])


def place_kernel(meta_ref, rid_ref, mine_ref, recv_ref, out_ref, *, slots):
    out_ref[...] = jnp.zeros_like(out_ref)
    count = meta_ref[1]

    def place(s, carry):
        r = rid_ref[0, s]
        for p in range(2):
            out_ref[pl.ds(2 * r + p, 1), :] = (mine_ref[pl.ds(2 * s + p, 1), :]
                                               + recv_ref[pl.ds(2 * (slots - count + s) + p, 1), :])
        return carry

    def place_eight(i, carry):
        for j in range(8):
            place(8 * i + j, carry)
        return carry

    lax.fori_loop(0, count // 8, place_eight, 0)
    lax.fori_loop(count // 8 * 8, count, place, 0)


def finish_kernel(meta_ref, zh_ref, w_mine_ref, w_other_ref,
                  zh_out, w_in_out, b_in_out, w_out_out, b_out_out, w_all, *, rows_blk):
    mid = w_all.shape[0] // 2
    mine = meta_ref[8] * mid
    for start, ref in ((mine, w_mine_ref), (mid - mine, w_other_ref)):
        flat = ref[...].reshape(2 * mid, 128)
        w_all[pl.ds(pl.multiple_of(start, 8), mid), :] = jnp.concatenate([flat[:mid], flat[mid:]], axis=1)
    n_ch = w_in_out.shape[0]
    w_in_out[...] = w_all[0:n_ch, :]
    b_in_out[...] = w_all[n_ch:n_ch + 1, :]
    b_out_out[...] = w_all[n_ch + 1:n_ch + 2, 0:b_out_out.shape[1]]
    w_out_out[...] = w_all[n_ch + 8:n_ch + 8 + w_out_out.shape[0], :]
    swapped = meta_ref[6]
    for n in range(2):
        base = jnp.bitwise_xor(swapped, n) * 8
        for z in range(8):
            zh_out[base + z] = zh_ref[n, pl.ds(z, rows_blk, stride=8), :]


def local(n_ha, n_wa, hw_plane, zh_plane, wz_plane, w_in, b_in, w_out, b_out,
          run_index, run_count, labels):
    rows_blk, cols_blk, channels = hw_plane.shape
    depth_z = zh_plane.shape[0]
    hidden = w_in.shape[1]
    classes = w_out.shape[1]
    slots = run_index.shape[1]
    half = depth_z // 2
    pair_cols = cols_blk // 2
    n_q = n_ha // 2
    n_zl = n_wa // 2
    n_hw = 2 * slots
    n_zh = rows_blk * ZC
    n_lab = slots // GROUP
    smem = pl.BlockSpec(memory_space=pltpu.SMEM)
    vmem = pl.BlockSpec(memory_space=pltpu.VMEM)
    hbm = pl.BlockSpec(memory_space=pltpu.HBM)
    f32 = jnp.float32
    bf16 = jnp.bfloat16

    ha = lax.axis_index("ha")
    wa = lax.axis_index("wa")
    y = ha // n_q
    my_q = ha % n_q
    b1 = wa // n_zl
    my_zl = wa % n_zl
    count = run_count[0]
    direct = n_q == 4 and n_zl == 2
    if direct:
        wz_pos = [(o ^ my_q) % 2 for o in range(4)]
        rest = [my_zl, y ^ b1, ha % 2, my_q]
    else:
        wz_pos = [jnp.int32(o // 2) for o in range(4)]
        rest = [jnp.int32(0), y, ha % 2, my_q]
    meta = jnp.stack([y, count] + wz_pos + rest).astype(jnp.int32)
    swap_y = [(i, (i + n_q) % n_ha) for i in range(n_ha)]

    n_rows, n_plane = n_hw + 16, n_zh + n_lab
    planes = (hw_plane.reshape(rows_blk * cols_blk, channels),
              zh_plane.reshape(depth_z * rows_blk, channels), labels[0], run_index)
    hw_raw = pltpu.VMEM((rows_blk * cols_blk, channels), bf16)
    plane_raw = [pltpu.VMEM((depth_z * rows_blk, channels), bf16), pltpu.VMEM((slots, 2 * depth_z), jnp.int32)]
    ids_raw = [pltpu.VMEM((1, slots), jnp.int32), pltpu.SMEM((1, slots), jnp.int32)]
    hw_wide = [pltpu.VMEM((rows_blk * cols_blk, channels), f32), pltpu.VMEM((n_hw, channels), f32)]
    plane_wide = [pltpu.VMEM((depth_z * rows_blk, channels), f32), pltpu.VMEM((2 * slots, 2 * depth_z), f32)]

    def call(kernel, name, operands, specs, outs, scratch, flops, limit=16):
        return pl.pallas_call(
            kernel,
            out_shape=[jax.ShapeDtypeStruct(shape, kind) for shape, kind in outs],
            in_specs=specs,
            out_specs=[vmem] * len(outs),
            scratch_shapes=scratch,
            compiler_params=pltpu.CompilerParams(vmem_limit_bytes=limit * 2**20),
            cost_estimate=pl.CostEstimate(flops=flops, bytes_accessed=2**20, transcendentals=0),
            name=name,
        )(*operands)

    sizes = dict(depth_z=depth_z, rows_blk=rows_blk, slots=slots, pair_cols=pair_cols)
    send0, = call(functools.partial(pack_plane_kernel, **sizes), "pack_plane", (meta, planes[1], planes[2]),
                  [smem] + [hbm] * 2, [((n_plane, channels), bf16)],
                  plane_raw + [pltpu.SemaphoreType.DMA((2,))] + plane_wide, 2 * 10**9, 60)
    recv0 = lax.ppermute(send0, "ha", swap_y)
    send0, hw_late, ids_late = lax.optimization_barrier((send0, planes[0], planes[3]))
    send_hw, = call(functools.partial(pack_rows_kernel, **sizes), "pack_rows", (meta, hw_late, ids_late),
                    [smem] + [hbm] * 2, [((n_rows, channels), bf16)],
                    [hw_raw] + ids_raw + [pltpu.SemaphoreType.DMA((3,))] + hw_wide, 3 * 10**9, 12)
    recv_hw = lax.ppermute(send_hw, "ha", swap_y)
    later = lax.optimization_barrier((send_hw,) + planes)
    own_hw, own0, own1, send1, wzf0, wzf1, *shared = call(
        functools.partial(pack_own_kernel, **sizes), "pack_own",
        (meta,) + later[1:] + (wz_plane, w_in, b_in.reshape(1, hidden), w_out.T, b_out.reshape(1, classes)),
        [smem] + [hbm] * 5 + [vmem] * 4,
        [((n_rows, channels), bf16)] + [((n_plane, channels), bf16)] * 3 + [((cols_blk, ZC, channels), f32)] * 2
        + [((channels, hidden), bf16), ((hidden, channels), bf16), ((1, hidden), f32), ((CLS_PAD, hidden), bf16),
           ((CLS_PAD, hidden), bf16), ((CLS_ROWS, 128), f32)],
        [hw_raw] + plane_raw + ids_raw + [pltpu.SemaphoreType.DMA((5,))] + hw_wide + plane_wide
        + [pltpu.VMEM((cols_blk, half, channels), bf16), pltpu.SemaphoreType.DMA,
           pltpu.VMEM((CLS_PAD, hidden), f32), pltpu.VMEM((8, 128), f32)], 3 * 10**9, 16)
    send1, recv0, recv_hw = lax.optimization_barrier((send1, recv0, recv_hw))
    recv1 = lax.ppermute(send1, "ha", swap_y)

    shared = tuple(shared)
    wgt_rows = channels + 8 + CLS_ROWS
    mid = wgt_rows // 2
    buf = [pltpu.VMEM((ROWS, channels), bf16), pltpu.VMEM((ROWS, hidden), bf16),
           pltpu.VMEM((ROWS, hidden), f32), pltpu.VMEM((CLS_ROWS, ROWS), f32)]
    out_buf = [pltpu.VMEM((channels + 2 * RUNS, ROWS), bf16), pltpu.VMEM((ROWS, hidden), bf16)]
    work = [pltpu.VMEM((n_hw, channels), f32), pltpu.VMEM((2 * rows_blk, ZC, channels), f32),
            pltpu.VMEM((n_lab, 128), f32), pltpu.VMEM((n_hw, hidden), f32),
            pltpu.VMEM((channels, hidden), f32), pltpu.VMEM((CLS_PAD, hidden), f32),
            pltpu.VMEM((CLS_ROWS, 128), f32), pltpu.SMEM((8, 128), jnp.int32), pltpu.SemaphoreType.DMA]
    work += buf + buf + out_buf + out_buf
    work += [pltpu.VMEM((cols_blk, 8, channels), f32)] * 2 + [pltpu.VMEM((2 * rows_blk, 8, channels), f32)] * 2
    work += [pltpu.VMEM((8, 128), jnp.int32), pltpu.VMEM((wgt_rows, hidden), f32)]
    sums = [((cols_blk, 8, channels), f32)] * 2 + [((2 * rows_blk, 8, channels), f32)] * 2
    def decode(n, sources, outs):
        return call(
            functools.partial(decode_kernel, chunk=CHUNKS[n], first=n == 0, rows_blk=rows_blk,
                              slots=slots, pair_cols=pair_cols), "decode%d" % n,
            (meta,) + sources + (wzf0, wzf1)[n:n + 1] + shared,
            [smem] + [vmem] * (len(sources) + 8 - 1), outs, work, 22 * 10**9, 20)

    wz0a, wz0b, zh0a, zh0b, hw0, wgt0 = decode(
        0, (own_hw, recv_hw, own0, recv0), sums + [((n_hw, channels), f32), ((wgt_rows, hidden), f32)])
    recv1, wz0a, wz0b, zh0a, zh0b = lax.optimization_barrier((recv1, wz0a, wz0b, zh0a, zh0b))
    wz1a, core_send, zh1a, zh1b, hw1, w_keep = decode(
        1, (own_hw, recv_hw, own1, recv1, hw0, wgt0),
        [sums[0], ((cols_blk + mid // 4, 8, channels), f32), sums[2], sums[3],
         ((n_hw, channels), f32), ((mid // 4, 8, channels), f32)])

    def place(mine, recv):
        return call(
            functools.partial(place_kernel, slots=slots), "place", (meta, run_index, mine, recv),
            [smem, smem, vmem, vmem], [((rows_blk * cols_blk, channels), f32)], [],
            3 * 10**9, 4)[0].reshape(rows_blk, cols_blk, channels)

    zpart = half // n_zl
    moves = []
    for a in range(n_ha):
        for b in range(n_wa):
            moves.append((a * n_wa + b, ((b // n_zl) * n_q + a % n_q) * n_wa + (a // n_q) * n_zl + b % n_zl))
    barrier = lax.optimization_barrier

    if direct:
        def ha_perm(pairs):
            return [(top * n_q + a, top * n_q + b) for top in range(2) for a, b in pairs]

        def flat(value):
            return value.reshape(2 * rows_blk * 8, channels)

        n_part = rows_blk * 8
        zh0a, zh0b = flat(zh0a), flat(zh0b)
        zh1a, zh1b = flat(zh1a), flat(zh1b)
        wz0r = ppermute_xor(wz0b, "ha", n_ha, 1)
        zh0r = ppermute_xor(zh0b, "wa", n_wa, 1)
        stays = y == b1
        wz0r, zh0r, wz1a, core_send, zh1a, zh1b, hw1, w_keep = barrier(
            (wz0r, zh0r, wz1a, core_send, zh1a, zh1b, hw1, w_keep))
        def corner(value, ha_mask, wa_mask):
            pairs = [(a * n_wa + b, (a ^ ha_mask) * n_wa + (b ^ wa_mask)) for a in range(n_ha) for b in range(n_wa)]
            return lax.ppermute(value, ("ha", "wa"), pairs)

        zh1r = ppermute_xor(encode(zh1b[None]), "wa", n_wa, 1)
        core_recv = ppermute_xor(core_send, "ha", n_ha, 1)
        hw_recv = lax.ppermute(encode(hw1[None]), "ha", swap_y)
        near0 = wz0a + wz0r
        near1 = wz1a + core_recv[:cols_blk]
        outer = (my_q == 0) | (my_q == 3)
        far = ppermute_xor(encode(jnp.where(outer, near1, near0).reshape(1, cols_blk * 8, channels)), "ha", n_ha, 2)
        part0 = zh0a + zh0r
        w = w_keep + core_recv[cols_blk:]
        wr = ppermute_xor(w, "wa", n_wa, 2)
        zh1r, wr = barrier((zh1r, wr))
        both = jnp.stack([part0, zh1a + decode_half(zh1r)[0]])
        zhf = ppermute_xor(encode(both[:, n_part:]), "wa", n_wa, 2)
        w = w + wr
        wr = [ppermute_xor(w, "ha", n_ha, mask) for mask in (n_q, 2, n_q + 2)]
        zhf, wr, far, hw_recv = barrier((zhf, wr, far, hw_recv))
        zh_code = encode(both[:, :n_part] + decode_half(zhf))
        zhm = jnp.where(stays, zh_code, corner(zh_code, n_q, 2))
        w = (w + wr[0]) + (wr[1] + wr[2])
        w_mine = w + ppermute_xor(w, "wa", n_wa, 1)
        w_other = ppermute_xor(w, "ha", n_ha, 1) + corner(w, 1, 1)
        hw_grad = place(hw1, decode_half(hw_recv)[0])
        wz_grad = jnp.where(outer, near0, near1) + decode_half(far).reshape(near1.shape)
        zh_grad, w_in_grad, b_in_grad, w_out_grad, b_out_grad = call(
            functools.partial(finish_kernel, rows_blk=rows_blk), "finish", (meta, decode_half(zhm), w_mine, w_other),
            [smem] + [vmem] * 3,
            [((2 * 8, rows_blk, channels), f32), ((channels, hidden), f32), ((1, hidden), f32),
             ((classes, hidden), f32), ((1, classes), f32)], [pltpu.VMEM((wgt_rows, hidden), f32)], 10**9, 4)
        return hw_grad, zh_grad, wz_grad, w_in_grad, b_in_grad[0], w_out_grad.T, b_out_grad[0]

    wz1b = core_send[:cols_blk]
    hw_grad = place(hw1, lax.ppermute(hw1, "ha", swap_y))
    wz_all = jnp.stack([wz0a, wz1a, wz1b, wz0b])
    wz_all = wz_all.transpose(1, 0, 2, 3).reshape(cols_blk, n_q, half // n_q, channels)
    part = jnp.take(wz_all.transpose(1, 0, 2, 3), jnp.arange(n_q) ^ my_q, axis=0)
    bit = 1
    while bit < n_q:
        part = part.reshape(part.shape[0] // 2, 2, cols_blk, half // n_q, channels)
        part = part[:, 0] + ppermute_xor(part[:, 1], "ha", n_ha, bit)
        bit *= 2
    wz_grad = part[0]
    zh_all = jnp.stack([zh0a, zh1a, zh1b, zh0b], axis=1)
    zh_all = zh_all.reshape(2, rows_blk, n_zl, zpart, channels).transpose(0, 2, 1, 3, 4)
    part = jnp.take(zh_all, jnp.arange(n_zl) ^ my_zl, axis=1)
    part = jnp.take(part, jnp.arange(2) ^ b1, axis=0)
    bit = 1
    while bit < n_zl:
        part = part.reshape(2, part.shape[1] // 2, 2, rows_blk, zpart, channels)
        part = part[:, :, 0] + ppermute_xor(part[:, :, 1], "wa", n_wa, bit)
        bit *= 2
    part = part[:, 0]
    part = part[0] + ppermute_xor(part[1], "wa", n_wa, n_zl)
    zh_grad = lax.ppermute(part, ("ha", "wa"), moves).transpose(1, 0, 2)
    w = w_keep + ppermute_xor(core_send[cols_blk:], "ha", n_ha, 1)
    bit = 2
    while bit < n_ha:
        w = w + ppermute_xor(w, "ha", n_ha, bit)
        bit *= 2
    bit = 1
    while bit < n_wa:
        w = w + ppermute_xor(w, "wa", n_wa, bit)
        bit *= 2
    w_other = ppermute_xor(w, "ha", n_ha, 1)
    w, w_other = [jnp.concatenate(jnp.split(v.reshape(2 * mid, 128), 2), axis=1) for v in (w, w_other)]
    upper = ha % 2 == 1
    wgt = jnp.concatenate([jnp.where(upper, w_other, w), jnp.where(upper, w, w_other)])
    first = channels + 8
    return (hw_grad, zh_grad, wz_grad, wgt[:channels], wgt[channels],
            wgt[first:first + classes].T, wgt[channels + 1, :classes])


def solution(mesh):
    placed = (
        P("ha", "wa", None),
        P(None, "ha", None),
        P("wa", None, None),
        P(),
        P(),
        P(),
        P(),
        P(("ha", "wa"), None),
        P(("ha", "wa")),
        P(("ha", "wa"), None, None),
    )
    return jax.shard_map(
        functools.partial(local, mesh.shape["ha"], mesh.shape["wa"]),
        mesh=mesh,
        in_specs=placed,
        out_specs=(
            P("ha", "wa", None),
            P("wa", "ha", None),
            P("wa", "ha", None),
            P(),
            P(),
            P(),
            P(),
        ),
        check_vma=False,
    )
```

```python
import functools

import jax
import jax.numpy as jnp
from jax import lax
from jax.experimental import pallas as pl
from jax.experimental.pallas import tpu as pltpu
from jax.sharding import PartitionSpec as P

grad_scale = 0.25
CLS_ROWS = 24
CLS_PAD = 32
CHUNKS = ((0, 3), (1, 2))
ZC = 16
RUNS = 64
GROUP = 4
ROWS = RUNS * 2 * ZC
SPAN = 1024
SEL_ROWS = SPAN // ZC
STRIP = 32
LEVEL_TOPS = tuple(2.0 ** e for e in (4, -7, -18, -29, -40))
LEVEL_BITS = (11, 22, 33, 44, 55)
CODE_ROWS = 16


def ppermute_xor(value, axis, size, mask):
    return lax.ppermute(value, axis, [(i, i ^ mask) for i in range(size)])


def fill_planes(side, refs, bases, zh_full, lab_pad, start, *, half, rows_blk, depth_z, slots):
    n_zh = rows_blk * ZC
    n_lab = slots // GROUP
    lane = lax.rem(lax.broadcasted_iota(jnp.int32, (n_lab, 128), 1), depth_z)
    z0 = side * half
    labs = [lab_pad[pl.ds(start + par, n_lab, stride=GROUP), :] for par in range(GROUP)]
    for chunk, ref, base in zip(CHUNKS, refs, bases):
        if ref is None:
            continue
        for h in range(rows_blk):
            parts = [zh_full[pl.ds((z0 + 8 * o) * rows_blk + h, 8, stride=rows_blk), :] for o in chunk]
            ref[base + h * ZC:base + (h + 1) * ZC, :] = jnp.concatenate(parts, axis=0).astype(jnp.bfloat16)
        merged = jnp.zeros((n_lab, 128), jnp.float32)
        for par in range(GROUP):
            for n, o in enumerate(chunk):
                to = par * ZC + 8 * n
                rolled = pltpu.roll(labs[par], jnp.bitwise_and(256 + to - (z0 + 8 * o), 127), 1)
                merged = jnp.where((lane >= to) & (lane < to + 8), rolled, merged)
        ref[base + n_zh:base + n_zh + n_lab, :] = merged.astype(jnp.bfloat16)


def fetch(pairs, sems):
    copies = [pltpu.make_async_copy(src, dst, sems.at[n]) for n, (src, dst) in enumerate(pairs)]
    for copy in copies:
        copy.start()
    for copy in copies:
        copy.wait()


def widen_planes(zh_raw, lab_raw, zh_full, lab_pad, slots):
    zh_full[...] = zh_raw[...].astype(jnp.float32)
    lab_pad[0:slots, :] = jnp.zeros((slots, lab_raw.shape[1]), jnp.float32)
    lab_pad[slots:, :] = lab_raw[...].astype(jnp.float32)


def twice(ids_raw, slots):
    ids = [ids_raw[:, k * 128:(k + 1) * 128] for k in range(slots // 128)]
    return jnp.concatenate(ids + ids, axis=0)


def gather_rows(rid_ref, hw_full, hw_rows, slots, shift):
    def gather_step(i, carry):
        for j in range(8):
            s = i * 8 + j
            r = rid_ref[0, jnp.maximum(s - shift, 0)]
            for p in range(2):
                hw_rows[pl.ds(2 * s + p, 1), :] = hw_full[pl.ds(2 * r + p, 1), :]
        return carry

    lax.fori_loop(0, slots // 8, gather_step, 0)


def put_ids(ref, base, ids, shift_bits, keep):
    padded = jnp.concatenate([ids, jnp.zeros_like(ids)], axis=0)
    high = lax.shift_right_logical(padded, shift_bits)
    low = jnp.bitwise_and(padded, keep)
    row = lax.broadcasted_iota(jnp.int32, padded.shape, 0)
    both = jnp.where(row < 4, high, pltpu.roll(low, 4, 0))
    ref[base:base + 16, :] = both.astype(jnp.float32).astype(jnp.bfloat16)


def pack_plane_kernel(meta_ref, zh_ref, lab_ref, send_ref, zh_raw, lab_raw, sems, zh_full, lab_pad,
                      *, depth_z, rows_blk, slots, pair_cols):
    fetch(((zh_ref, zh_raw), (lab_ref, lab_raw)), sems)
    widen_planes(zh_raw, lab_raw, zh_full, lab_pad, slots)
    fill_planes(1 - meta_ref[0], (send_ref, None), (0, 0), zh_full, lab_pad, meta_ref[1],
                half=depth_z // 2, rows_blk=rows_blk, depth_z=depth_z, slots=slots)


def pack_rows_kernel(meta_ref, hw_ref, ids_ref, send_ref, hw_raw, ids_raw, rid_ref, sems, hw_full, hw_rows,
                     *, depth_z, rows_blk, slots, pair_cols):
    n_hw = 2 * slots
    count = meta_ref[1]
    fetch(((hw_ref, hw_raw), (ids_ref, rid_ref), (ids_ref, ids_raw)), sems)
    hw_full[...] = hw_raw[...].astype(jnp.float32)
    ids = twice(ids_raw, slots)
    gather_rows(rid_ref, hw_full, hw_rows, slots, slots - count)
    send_ref[0:n_hw, :] = hw_rows[...].astype(jnp.bfloat16)
    down = slots - count
    lanes = jnp.bitwise_and(down, 127)
    rows = lax.shift_right_logical(down, 7)
    turned = pltpu.roll(ids, lanes, 1)
    here = pltpu.roll(turned, rows, 0)
    before = pltpu.roll(turned, jnp.bitwise_and(rows + 1, 7), 0)
    lane = lax.broadcasted_iota(jnp.int32, ids.shape, 1)
    put_ids(send_ref, n_hw, jnp.where(lane < lanes, before, here), pair_cols.bit_length() - 1, pair_cols - 1)


def prepare_weights(w_in_ref, b_in_ref, w_out_ref, b_out_ref,
                    w_in_half, w_in_t, b_in_half, w_out_t, w_out_half, b_out_rows, w_wide, b_wide):
    w_in = w_in_ref[...].astype(jnp.float32)
    w_in_half[...] = (w_in * 0.5).astype(jnp.bfloat16)
    w_in_t[...] = jnp.transpose(w_in, (1, 0)).astype(jnp.bfloat16)
    b_in_half[...] = b_in_ref[...] * 0.5
    classes = w_out_ref.shape[0]
    w_wide[...] = jnp.zeros_like(w_wide)
    w_wide[0:classes, :] = w_out_ref[...].astype(jnp.float32)
    turned = w_wide[...]
    w_out_t[...] = turned.astype(jnp.bfloat16)
    w_out_half[...] = (turned * 0.5).astype(jnp.bfloat16)
    b_wide[...] = jnp.full_like(b_wide, -1e30)
    b_wide[0:1, 0:classes] = b_out_ref[...]
    b_out_rows[...] = jnp.broadcast_to(jnp.transpose(b_wide[...], (1, 0))[0:CLS_ROWS, 0:1], (CLS_ROWS, 128))


def pack_own_kernel(meta_ref, hw_ref, zh_ref, lab_ref, ids_ref, wz_ref, w_in_ref, b_in_ref, w_out_ref, b_out_ref,
                    hw_out, own0_ref, own1_ref, send1_ref, wz0_ref, wz1_ref,
                    w_in_half, w_in_t, b_in_half, w_out_t, w_out_half, b_out_rows,
                    hw_raw, zh_raw, lab_raw, ids_raw, rid_ref, sems,
                    hw_full, hw_rows, zh_full, lab_pad, wz_raw, wz_sem, w_wide, b_wide,
                    *, depth_z, rows_blk, slots, pair_cols):
    half = depth_z // 2
    n_hw = 2 * slots
    z0 = pl.multiple_of(meta_ref[0] * half, half)
    wz_copy = pltpu.make_async_copy(wz_ref.at[:, pl.ds(z0, half), :], wz_raw, wz_sem)
    wz_copy.start()
    prepare_weights(w_in_ref, b_in_ref, w_out_ref, b_out_ref,
                    w_in_half, w_in_t, b_in_half, w_out_t, w_out_half, b_out_rows, w_wide, b_wide)
    fetch(((hw_ref, hw_raw), (ids_ref, rid_ref), (ids_ref, ids_raw), (zh_ref, zh_raw), (lab_ref, lab_raw)), sems)
    hw_full[...] = hw_raw[...].astype(jnp.float32)
    widen_planes(zh_raw, lab_raw, zh_full, lab_pad, slots)
    gather_rows(rid_ref, hw_full, hw_rows, slots, 0)
    hw_out[0:n_hw, :] = hw_rows[...].astype(jnp.bfloat16)
    put_ids(hw_out, n_hw, twice(ids_raw, slots), pair_cols.bit_length() - 1, pair_cols - 1)
    fill_planes(meta_ref[0], (own0_ref, own1_ref), (0, 0), zh_full, lab_pad, slots,
                half=half, rows_blk=rows_blk, depth_z=depth_z, slots=slots)
    fill_planes(1 - meta_ref[0], (None, send1_ref), (0, 0), zh_full, lab_pad, meta_ref[1],
                half=half, rows_blk=rows_blk, depth_z=depth_z, slots=slots)
    wz_copy.wait()

    def widen(w, carry):
        rows = wz_raw[w].astype(jnp.float32)
        for chunk, ref in zip(CHUNKS, (wz0_ref, wz1_ref)):
            for n, o in enumerate(chunk):
                ref[w, 8 * n:8 * n + 8, :] = rows[8 * o:8 * o + 8]
        return carry

    lax.fori_loop(0, 2 * pair_cols, widen, 0, unroll=8)


def add_zh(d, row, zh_accs):
    both = d[0] + d[1]
    now = [acc[row] for acc in zh_accs]
    for n, acc in enumerate(zh_accs):
        acc[row] = now[n] + both[8 * n:8 * n + 8]


def add_wz(d, col, wz_accs):
    now = [[acc[col + p] for p in range(2)] for acc in wz_accs]
    for n, acc in enumerate(wz_accs):
        for p in range(2):
            acc[col + p] = now[n][p] + d[p][8 * n:8 * n + 8]


def pick_level(top):
    level = jnp.zeros(top.shape, jnp.float32)
    for n, bound in enumerate(LEVEL_TOPS):
        level = jnp.where(top < bound, n + 1.0, level)
    return level


def level_scale(level, sign):
    scale = jnp.ones(level.shape, jnp.float32)
    for n in range(len(LEVEL_TOPS)):
        scale = jnp.where(level == n + 1.0, 2.0 ** (sign * LEVEL_BITS[n]), scale)
    return scale


def encode(value):
    level = pick_level(jnp.max(jnp.abs(value), axis=1, keepdims=True))
    code = jnp.broadcast_to(level, (value.shape[0], CODE_ROWS, value.shape[2]))
    return jnp.concatenate([value * level_scale(level, 1), code], axis=1).astype(jnp.float16)


def decode_half(value):
    value = value.astype(jnp.float32)
    n = value.shape[1] - CODE_ROWS
    return value[:, :n] * level_scale(value[:, n:n + 1, :], -1)


def read_runs(ids_ref, first, n):
    row = lax.shift_right_logical(first, 7)
    at = jnp.bitwise_and(first, 127)
    return [(ids_ref[row, at + j], ids_ref[row + 4, at + j]) for j in range(n)]


def decode_kernel(*refs, chunk, first, rows_blk, slots, pair_cols):
    n_hw = 2 * slots
    n_zh = rows_blk * ZC
    n_lab = slots // GROUP
    meta_ref, hw_own, hw_recv, z_own, z_recv = refs[:5]
    refs = refs[5:]
    z_base = 0
    if not first:
        hw_prev, wgt_prev = refs[:2]
        refs = refs[2:]
    wz_full, w_in_ref, w_in_t_ref, b_in_ref, w_out_t_ref, w_out_half_ref, b_out_ref = refs[:7]
    refs = refs[7:]
    if first:
        wz_out0, wz_out1, zh_out0, zh_out1, hw_out, wgt_out = refs[:6]
        refs = refs[6:]
    else:
        wz_out0, core_out, zh_out0, zh_out1, hw_out, wgt_keep = refs[:6]
        refs = refs[6:]
    (hw_full, zh_full, lab_full, hw_acc, w_in_acc, w_out_acc, b_out_acc, ids_ref, ids_sem) = refs[:9]
    bufs = (refs[9:13], refs[13:17])
    outs = (refs[17:19], refs[19:21])
    wz_accs, zh_accs, ids_vec, wgt_all = refs[21:23], refs[23:25], refs[25], refs[26]
    count = meta_ref[1]
    rel_own = meta_ref[7]

    spot_row = lax.broadcasted_iota(jnp.int32, (8, 128), 0)
    spot = jnp.bitwise_and(spot_row, 3) * 128 + lax.broadcasted_iota(jnp.int32, (8, 128), 1)
    own_ids = hw_own[n_hw:n_hw + 16, :].astype(jnp.float32).astype(jnp.int32)
    recv_ids = hw_recv[n_hw:n_hw + 16, :].astype(jnp.float32).astype(jnp.int32)
    is_own = spot < count
    ids = jnp.where(is_own, own_ids[0:8], recv_ids[0:8])
    rel = jnp.where(is_own, rel_own, 1 - rel_own)
    ids_vec[...] = jnp.where(spot_row < 4, ids + rel * rows_blk, 2 * ids)
    copy = pltpu.make_async_copy(ids_vec, ids_ref, ids_sem)
    copy.start()
    row = lax.broadcasted_iota(jnp.int32, (n_hw, 128), 0)
    hw_full[...] = jnp.where(row < 2 * count, hw_own[0:n_hw, :].astype(jnp.float32),
                             hw_recv[0:n_hw, :].astype(jnp.float32))
    for k, ref in ((0, z_own), (1, z_recv)):
        base = jnp.bitwise_xor(rel_own, k) * rows_blk
        for h in range(rows_blk):
            zh_full[base + h] = ref[z_base + h * ZC:z_base + (h + 1) * ZC, :].astype(jnp.float32)
    lab_row = lax.broadcasted_iota(jnp.int32, (n_lab, 128), 0)
    lab_lane = lax.broadcasted_iota(jnp.int32, (n_lab, 128), 1)
    place = GROUP * lab_row + lax.rem(lab_lane // ZC, GROUP)
    first_lab = z_base + n_zh
    lab_full[...] = jnp.where(place < count, z_own[first_lab:first_lab + n_lab, :].astype(jnp.float32),
                              z_recv[first_lab:first_lab + n_lab, :].astype(jnp.float32))
    for acc in wz_accs + zh_accs:
        acc[...] = jnp.zeros_like(acc)
    w_in_acc[...] = jnp.zeros_like(w_in_acc)
    w_out_acc[...] = jnp.zeros_like(w_out_acc)
    b_out_acc[...] = jnp.zeros_like(b_out_acc)
    copy.wait()

    groups = RUNS // GROUP
    n_ch = w_in_ref.shape[0]
    sel_row = lax.broadcasted_iota(jnp.int32, (SEL_ROWS, ROWS), 0)
    sample = jnp.bitwise_and(lax.broadcasted_iota(jnp.int32, (SEL_ROWS, ROWS), 1), SPAN - 1)
    sample_run = lax.shift_right_logical(sample, 7) * GROUP + lax.shift_right_logical(jnp.bitwise_and(sample, 63), 4)
    sample_row = 2 * sample_run + jnp.bitwise_and(lax.shift_right_logical(sample, 6), 1)
    select = jnp.where(sel_row == sample_row, 1.0, 0.0).astype(jnp.bfloat16)
    for left_ref, dpre_ref in outs:
        left_ref[n_ch:, :] = select
    class_ids = lax.broadcasted_iota(jnp.int32, (CLS_ROWS, 128), 0).astype(jnp.float32)
    nt = (((1,), (1,)), ((), ()))

    def front(b, buf):
        feat_ref, hid_ref, slope_ref, logit_ref = buf
        runs = read_runs(ids_ref, RUNS * b, RUNS)
        for g in range(groups):
            pieces = []
            for p in range(2):
                for par in range(GROUP):
                    row, col = runs[GROUP * g + par]
                    at = pl.multiple_of(2 * RUNS * b, 2 * RUNS) + 2 * (GROUP * g + par) + p
                    total = hw_full[pl.ds(at, 1), :] + zh_full[row] + wz_full[col + p]
                    pieces.append(total.astype(jnp.bfloat16))
            feat = jnp.concatenate(pieces, axis=0)
            feat_ref[g * 128:(g + 1) * 128, :] = feat
            pre_all = jnp.dot(feat, w_in_ref[...], preferred_element_type=jnp.float32)
            for r in range(0, 128, STRIP):
                pre = pre_all[r:r + STRIP] + b_in_ref[...]
                t = jnp.tanh(pre)
                a = 1.0 + t
                u = pre * a
                at = g * 128 + r
                hid_ref[at:at + STRIP, :] = u.astype(jnp.bfloat16)
                slope_ref[at:at + STRIP, :] = a + u * (1.0 - t)
        logits = lax.dot_general(w_out_t_ref[...], hid_ref[...], nt, preferred_element_type=jnp.float32)
        logit_ref[...] = logits[0:CLS_ROWS, :]

    def middle(b, buf, out):
        feat_ref, hid_ref, slope_ref, logit_ref = buf
        left_ref, dpre_ref = out
        left_ref[0:n_ch, :] = jnp.transpose(feat_ref[...], (1, 0))
        dl_tiles = []
        b_part = None
        for g in range(groups):
            tile = logit_ref[:, g * 128:(g + 1) * 128] + b_out_ref[...]
            top = jnp.max(tile, axis=0, keepdims=True)
            e = jnp.exp(tile - top)
            inv = 1.0 / jnp.sum(e, axis=0, keepdims=True)
            lab_here = lab_full[pl.ds(groups * b + g, 1), :]
            onehot = jnp.where(class_ids == lab_here, 1.0, 0.0)
            dl = ((e * inv - onehot) * grad_scale).astype(jnp.bfloat16).astype(jnp.float32)
            b_part = dl if b_part is None else b_part + dl
            dl_tiles.append(dl)
        b_out_acc[...] += b_part
        dl_all = jnp.concatenate(dl_tiles, axis=1)
        dl_all = jnp.concatenate([dl_all, jnp.zeros((CLS_PAD - CLS_ROWS, ROWS), jnp.float32)], axis=0)
        dl_t = jnp.transpose(dl_all, (1, 0)).astype(jnp.bfloat16)
        w_out_acc[...] += jnp.dot(dl_all.astype(jnp.bfloat16), hid_ref[...], preferred_element_type=jnp.float32)
        for g in range(groups):
            dhid = jnp.dot(dl_t[g * 128:(g + 1) * 128], w_out_half_ref[...], preferred_element_type=jnp.float32)
            for r in range(0, 128, STRIP):
                at = g * 128 + r
                dpre_ref[at:at + STRIP, :] = (dhid[r:r + STRIP] * slope_ref[at:at + STRIP, :]).astype(jnp.bfloat16)

    def back(b, out):
        left_ref, dpre_ref = out
        for k in range(ROWS // SPAN):
            cut = slice(SPAN * k, SPAN * (k + 1))
            sums = jnp.dot(left_ref[:, cut], dpre_ref[cut, :], preferred_element_type=jnp.float32)
            w_in_acc[...] += sums[0:n_ch]
            at = pl.multiple_of(2 * RUNS * b, 2 * RUNS) + SEL_ROWS * k
            hw_acc[pl.ds(at, SEL_ROWS), :] = sums[n_ch:]
        runs = read_runs(ids_ref, RUNS * b, RUNS)
        for g in range(groups):
            dfeat = jnp.dot(dpre_ref[g * 128:(g + 1) * 128, :], w_in_t_ref[...], preferred_element_type=jnp.float32)
            for par in range(GROUP):
                d = [dfeat[p * 64 + par * ZC:p * 64 + (par + 1) * ZC] for p in range(2)]
                row, col = runs[GROUP * g + par]
                add_zh(d, row, zh_accs)
                add_wz(d, col, wz_accs)

    n_batch = slots // RUNS
    front(0, bufs[0])
    front(1, bufs[1])
    middle(0, bufs[0], outs[0])

    def step(k, carry):
        b = 2 * k
        front(b + 2, bufs[0])
        middle(b + 1, bufs[1], outs[1])
        back(b, outs[0])
        front(b + 3, bufs[1])
        middle(b + 2, bufs[0], outs[0])
        back(b + 1, outs[1])
        return carry

    lax.fori_loop(0, n_batch // 2 - 1, step, 0)
    middle(n_batch - 1, bufs[1], outs[1])
    back(n_batch - 2, outs[0])
    back(n_batch - 1, outs[1])
    tail = hw_acc[...]
    total = None
    for n in range(3):
        part = tail.astype(jnp.bfloat16)
        tail = tail - part.astype(jnp.float32)
        term = jnp.dot(part, w_in_t_ref[...], preferred_element_type=jnp.float32)
        total = term if total is None else total + term
    width = w_in_acc.shape[1]
    b_in_sum = jnp.sum(hw_acc[...], axis=0, keepdims=True)
    b_pad = jnp.concatenate([b_out_acc[...], jnp.zeros((128 - CLS_ROWS, 128), jnp.float32)], axis=0)
    b_out_sum = jnp.sum(jnp.transpose(b_pad, (1, 0)), axis=0, keepdims=True)
    b_out_sum = jnp.concatenate([b_out_sum, jnp.zeros((1, width - 128), jnp.float32)], axis=1)
    biases = jnp.concatenate([b_in_sum, b_out_sum, jnp.zeros((6, width), jnp.float32)], axis=0)
    weights = jnp.concatenate([w_in_acc[...], biases, w_out_acc[0:CLS_ROWS, :]], axis=0)
    put_zh(meta_ref, chunk, zh_accs, zh_out0, zh_out1)
    if first:
        hw_out[...] = total
        wgt_out[...] = weights
        put_wz(meta_ref, chunk, wz_accs, wz_out0, wz_out1)
        return
    hw_out[...] = total + hw_prev[...]
    wgt_all[...] = weights + wgt_prev[...]
    put_wz(meta_ref, chunk, wz_accs, wz_out0, core_out.at[0:2 * pair_cols])
    mid = wgt_all.shape[0] // 2
    mine = meta_ref[8] * mid
    wgt_keep[...] = split_lanes(wgt_all[pl.ds(pl.multiple_of(mine, 8), mid), :])
    core_out[2 * pair_cols:] = split_lanes(wgt_all[pl.ds(pl.multiple_of(mid - mine, 8), mid), :])


def split_lanes(value):
    return jnp.concatenate([value[:, :128], value[:, 128:]], axis=0).reshape(value.shape[0] // 4, 8, 128)


def put_zh(meta_ref, chunk, zh_accs, zh_out0, zh_out1):
    same = meta_ref[6] == chunk[0] // 2
    zh_out0[...] = jnp.where(same, zh_accs[0][...], zh_accs[1][...])
    zh_out1[...] = jnp.where(same, zh_accs[1][...], zh_accs[0][...])


def put_wz(meta_ref, chunk, wz_accs, wz_out0, wz_out1):
    same = meta_ref[2 + chunk[0]] == 0
    wz_out0[...] = jnp.where(same, wz_accs[0][...], wz_accs[1][...])
    wz_out1[...] = jnp.where(same, wz_accs[1][...], wz_accs[0][...])


def place_kernel(meta_ref, rid_ref, mine_ref, recv_ref, out_ref, *, slots):
    out_ref[...] = jnp.zeros_like(out_ref)
    count = meta_ref[1]

    def place(s, carry):
        r = rid_ref[0, s]
        for p in range(2):
            out_ref[pl.ds(2 * r + p, 1), :] = (mine_ref[pl.ds(2 * s + p, 1), :]
                                               + recv_ref[pl.ds(2 * (slots - count + s) + p, 1), :])
        return carry

    def place_eight(i, carry):
        for j in range(8):
            place(8 * i + j, carry)
        return carry

    lax.fori_loop(0, count // 8, place_eight, 0)
    lax.fori_loop(count // 8 * 8, count, place, 0)


def finish_kernel(meta_ref, zh_ref, w_mine_ref, w_other_ref,
                  zh_out, w_in_out, b_in_out, w_out_out, b_out_out, w_all, *, rows_blk):
    mid = w_all.shape[0] // 2
    mine = meta_ref[8] * mid
    for start, ref in ((mine, w_mine_ref), (mid - mine, w_other_ref)):
        flat = ref[...].reshape(2 * mid, 128)
        w_all[pl.ds(pl.multiple_of(start, 8), mid), :] = jnp.concatenate([flat[:mid], flat[mid:]], axis=1)
    n_ch = w_in_out.shape[0]
    w_in_out[...] = w_all[0:n_ch, :]
    b_in_out[...] = w_all[n_ch:n_ch + 1, :]
    b_out_out[...] = w_all[n_ch + 1:n_ch + 2, 0:b_out_out.shape[1]]
    w_out_out[...] = w_all[n_ch + 8:n_ch + 8 + w_out_out.shape[0], :]
    swapped = meta_ref[6]
    for n in range(2):
        base = jnp.bitwise_xor(swapped, n) * 8
        for z in range(8):
            zh_out[base + z] = zh_ref[n, pl.ds(z, rows_blk, stride=8), :]


def local(n_ha, n_wa, hw_plane, zh_plane, wz_plane, w_in, b_in, w_out, b_out,
          run_index, run_count, labels):
    rows_blk, cols_blk, channels = hw_plane.shape
    depth_z = zh_plane.shape[0]
    hidden = w_in.shape[1]
    classes = w_out.shape[1]
    slots = run_index.shape[1]
    half = depth_z // 2
    pair_cols = cols_blk // 2
    n_q = n_ha // 2
    n_zl = n_wa // 2
    n_hw = 2 * slots
    n_zh = rows_blk * ZC
    n_lab = slots // GROUP
    smem = pl.BlockSpec(memory_space=pltpu.SMEM)
    vmem = pl.BlockSpec(memory_space=pltpu.VMEM)
    hbm = pl.BlockSpec(memory_space=pltpu.HBM)
    f32 = jnp.float32
    bf16 = jnp.bfloat16

    ha = lax.axis_index("ha")
    wa = lax.axis_index("wa")
    y = ha // n_q
    my_q = ha % n_q
    b1 = wa // n_zl
    my_zl = wa % n_zl
    count = run_count[0]
    direct = n_q == 4 and n_zl == 2
    if direct:
        wz_pos = [(o ^ my_q) % 2 for o in range(4)]
        rest = [my_zl, y ^ b1, ha % 2, my_q]
    else:
        wz_pos = [jnp.int32(o // 2) for o in range(4)]
        rest = [jnp.int32(0), y, ha % 2, my_q]
    meta = jnp.stack([y, count] + wz_pos + rest).astype(jnp.int32)
    swap_y = [(i, (i + n_q) % n_ha) for i in range(n_ha)]

    n_rows, n_plane = n_hw + 16, n_zh + n_lab
    planes = (hw_plane.reshape(rows_blk * cols_blk, channels),
              zh_plane.reshape(depth_z * rows_blk, channels), labels[0], run_index)
    hw_raw = pltpu.VMEM((rows_blk * cols_blk, channels), bf16)
    plane_raw = [pltpu.VMEM((depth_z * rows_blk, channels), bf16), pltpu.VMEM((slots, 2 * depth_z), jnp.int32)]
    ids_raw = [pltpu.VMEM((1, slots), jnp.int32), pltpu.SMEM((1, slots), jnp.int32)]
    hw_wide = [pltpu.VMEM((rows_blk * cols_blk, channels), f32), pltpu.VMEM((n_hw, channels), f32)]
    plane_wide = [pltpu.VMEM((depth_z * rows_blk, channels), f32), pltpu.VMEM((2 * slots, 2 * depth_z), f32)]

    def call(kernel, name, operands, specs, outs, scratch, flops, limit=16):
        return pl.pallas_call(
            kernel,
            out_shape=[jax.ShapeDtypeStruct(shape, kind) for shape, kind in outs],
            in_specs=specs,
            out_specs=[vmem] * len(outs),
            scratch_shapes=scratch,
            compiler_params=pltpu.CompilerParams(vmem_limit_bytes=limit * 2**20),
            cost_estimate=pl.CostEstimate(flops=flops, bytes_accessed=2**20, transcendentals=0),
            name=name,
        )(*operands)

    sizes = dict(depth_z=depth_z, rows_blk=rows_blk, slots=slots, pair_cols=pair_cols)
    send0, = call(functools.partial(pack_plane_kernel, **sizes), "pack_plane", (meta, planes[1], planes[2]),
                  [smem] + [hbm] * 2, [((n_plane, channels), bf16)],
                  plane_raw + [pltpu.SemaphoreType.DMA((2,))] + plane_wide, 2 * 10**9, 60)
    recv0 = lax.ppermute(send0, "ha", swap_y)
    send0, hw_late, ids_late = lax.optimization_barrier((send0, planes[0], planes[3]))
    send_hw, = call(functools.partial(pack_rows_kernel, **sizes), "pack_rows", (meta, hw_late, ids_late),
                    [smem] + [hbm] * 2, [((n_rows, channels), bf16)],
                    [hw_raw] + ids_raw + [pltpu.SemaphoreType.DMA((3,))] + hw_wide, 3 * 10**9, 12)
    recv_hw = lax.ppermute(send_hw, "ha", swap_y)
    later = lax.optimization_barrier((send_hw,) + planes)
    own_hw, own0, own1, send1, wzf0, wzf1, *shared = call(
        functools.partial(pack_own_kernel, **sizes), "pack_own",
        (meta,) + later[1:] + (wz_plane, w_in, b_in.reshape(1, hidden), w_out.T, b_out.reshape(1, classes)),
        [smem] + [hbm] * 5 + [vmem] * 4,
        [((n_rows, channels), bf16)] + [((n_plane, channels), bf16)] * 3 + [((cols_blk, ZC, channels), f32)] * 2
        + [((channels, hidden), bf16), ((hidden, channels), bf16), ((1, hidden), f32), ((CLS_PAD, hidden), bf16),
           ((CLS_PAD, hidden), bf16), ((CLS_ROWS, 128), f32)],
        [hw_raw] + plane_raw + ids_raw + [pltpu.SemaphoreType.DMA((5,))] + hw_wide + plane_wide
        + [pltpu.VMEM((cols_blk, half, channels), bf16), pltpu.SemaphoreType.DMA,
           pltpu.VMEM((CLS_PAD, hidden), f32), pltpu.VMEM((8, 128), f32)], 3 * 10**9, 16)
    send1, recv0, recv_hw = lax.optimization_barrier((send1, recv0, recv_hw))
    recv1 = lax.ppermute(send1, "ha", swap_y)

    shared = tuple(shared)
    wgt_rows = channels + 8 + CLS_ROWS
    mid = wgt_rows // 2
    buf = [pltpu.VMEM((ROWS, channels), bf16), pltpu.VMEM((ROWS, hidden), bf16),
           pltpu.VMEM((ROWS, hidden), f32), pltpu.VMEM((CLS_ROWS, ROWS), f32)]
    out_buf = [pltpu.VMEM((channels + SEL_ROWS, ROWS), bf16), pltpu.VMEM((ROWS, hidden), bf16)]
    work = [pltpu.VMEM((n_hw, channels), f32), pltpu.VMEM((2 * rows_blk, ZC, channels), f32),
            pltpu.VMEM((n_lab, 128), f32), pltpu.VMEM((n_hw, hidden), f32),
            pltpu.VMEM((channels, hidden), f32), pltpu.VMEM((CLS_PAD, hidden), f32),
            pltpu.VMEM((CLS_ROWS, 128), f32), pltpu.SMEM((8, 128), jnp.int32), pltpu.SemaphoreType.DMA]
    work += buf + buf + out_buf + out_buf
    work += [pltpu.VMEM((cols_blk, 8, channels), f32)] * 2 + [pltpu.VMEM((2 * rows_blk, 8, channels), f32)] * 2
    work += [pltpu.VMEM((8, 128), jnp.int32), pltpu.VMEM((wgt_rows, hidden), f32)]
    sums = [((cols_blk, 8, channels), f32)] * 2 + [((2 * rows_blk, 8, channels), f32)] * 2
    def decode(n, sources, outs):
        return call(
            functools.partial(decode_kernel, chunk=CHUNKS[n], first=n == 0, rows_blk=rows_blk,
                              slots=slots, pair_cols=pair_cols), "decode%d" % n,
            (meta,) + sources + (wzf0, wzf1)[n:n + 1] + shared,
            [smem] + [vmem] * (len(sources) + 8 - 1), outs, work, 22 * 10**9, 28)

    wz0a, wz0b, zh0a, zh0b, hw0, wgt0 = decode(
        0, (own_hw, recv_hw, own0, recv0), sums + [((n_hw, channels), f32), ((wgt_rows, hidden), f32)])
    recv1, wz0a, wz0b, zh0a, zh0b = lax.optimization_barrier((recv1, wz0a, wz0b, zh0a, zh0b))
    wz1a, core_send, zh1a, zh1b, hw1, w_keep = decode(
        1, (own_hw, recv_hw, own1, recv1, hw0, wgt0),
        [sums[0], ((cols_blk + mid // 4, 8, channels), f32), sums[2], sums[3],
         ((n_hw, channels), f32), ((mid // 4, 8, channels), f32)])

    def place(mine, recv):
        return call(
            functools.partial(place_kernel, slots=slots), "place", (meta, run_index, mine, recv),
            [smem, smem, vmem, vmem], [((rows_blk * cols_blk, channels), f32)], [],
            3 * 10**9, 4)[0].reshape(rows_blk, cols_blk, channels)

    zpart = half // n_zl
    moves = []
    for a in range(n_ha):
        for b in range(n_wa):
            moves.append((a * n_wa + b, ((b // n_zl) * n_q + a % n_q) * n_wa + (a // n_q) * n_zl + b % n_zl))
    barrier = lax.optimization_barrier

    if direct:
        def ha_perm(pairs):
            return [(top * n_q + a, top * n_q + b) for top in range(2) for a, b in pairs]

        def flat(value):
            return value.reshape(2 * rows_blk * 8, channels)

        n_part = rows_blk * 8
        zh0a, zh0b = flat(zh0a), flat(zh0b)
        zh1a, zh1b = flat(zh1a), flat(zh1b)
        wz0r = ppermute_xor(wz0b, "ha", n_ha, 1)
        zh0r = ppermute_xor(zh0b, "wa", n_wa, 1)
        stays = y == b1
        wz0r, zh0r, wz1a, core_send, zh1a, zh1b, hw1, w_keep = barrier(
            (wz0r, zh0r, wz1a, core_send, zh1a, zh1b, hw1, w_keep))
        def corner(value, ha_mask, wa_mask):
            pairs = [(a * n_wa + b, (a ^ ha_mask) * n_wa + (b ^ wa_mask)) for a in range(n_ha) for b in range(n_wa)]
            return lax.ppermute(value, ("ha", "wa"), pairs)

        zh1r = ppermute_xor(encode(zh1b[None]), "wa", n_wa, 1)
        core_recv = ppermute_xor(core_send, "ha", n_ha, 1)
        hw_recv = lax.ppermute(encode(hw1[None]), "ha", swap_y)
        near0 = wz0a + wz0r
        near1 = wz1a + core_recv[:cols_blk]
        outer = (my_q == 0) | (my_q == 3)
        far = ppermute_xor(encode(jnp.where(outer, near1, near0).reshape(1, cols_blk * 8, channels)), "ha", n_ha, 2)
        part0 = zh0a + zh0r
        w = w_keep + core_recv[cols_blk:]
        wr = ppermute_xor(w, "wa", n_wa, 2)
        zh1r, wr = barrier((zh1r, wr))
        both = jnp.stack([part0, zh1a + decode_half(zh1r)[0]])
        zhf = ppermute_xor(encode(both[:, n_part:]), "wa", n_wa, 2)
        w = w + wr
        wr = [ppermute_xor(w, "ha", n_ha, mask) for mask in (n_q, 2, n_q + 2)]
        zhf, wr, far, hw_recv = barrier((zhf, wr, far, hw_recv))
        zh_code = encode(both[:, :n_part] + decode_half(zhf))
        zhm = jnp.where(stays, zh_code, corner(zh_code, n_q, 2))
        w = (w + wr[0]) + (wr[1] + wr[2])
        w_mine = w + ppermute_xor(w, "wa", n_wa, 1)
        w_other = ppermute_xor(w, "ha", n_ha, 1) + corner(w, 1, 1)
        hw_grad = place(hw1, decode_half(hw_recv)[0])
        wz_grad = jnp.where(outer, near0, near1) + decode_half(far).reshape(near1.shape)
        zh_grad, w_in_grad, b_in_grad, w_out_grad, b_out_grad = call(
            functools.partial(finish_kernel, rows_blk=rows_blk), "finish", (meta, decode_half(zhm), w_mine, w_other),
            [smem] + [vmem] * 3,
            [((2 * 8, rows_blk, channels), f32), ((channels, hidden), f32), ((1, hidden), f32),
             ((classes, hidden), f32), ((1, classes), f32)], [pltpu.VMEM((wgt_rows, hidden), f32)], 10**9, 4)
        return hw_grad, zh_grad, wz_grad, w_in_grad, b_in_grad[0], w_out_grad.T, b_out_grad[0]

    wz1b = core_send[:cols_blk]
    hw_grad = place(hw1, lax.ppermute(hw1, "ha", swap_y))
    wz_all = jnp.stack([wz0a, wz1a, wz1b, wz0b])
    wz_all = wz_all.transpose(1, 0, 2, 3).reshape(cols_blk, n_q, half // n_q, channels)
    part = jnp.take(wz_all.transpose(1, 0, 2, 3), jnp.arange(n_q) ^ my_q, axis=0)
    bit = 1
    while bit < n_q:
        part = part.reshape(part.shape[0] // 2, 2, cols_blk, half // n_q, channels)
        part = part[:, 0] + ppermute_xor(part[:, 1], "ha", n_ha, bit)
        bit *= 2
    wz_grad = part[0]
    zh_all = jnp.stack([zh0a, zh1a, zh1b, zh0b], axis=1)
    zh_all = zh_all.reshape(2, rows_blk, n_zl, zpart, channels).transpose(0, 2, 1, 3, 4)
    part = jnp.take(zh_all, jnp.arange(n_zl) ^ my_zl, axis=1)
    part = jnp.take(part, jnp.arange(2) ^ b1, axis=0)
    bit = 1
    while bit < n_zl:
        part = part.reshape(2, part.shape[1] // 2, 2, rows_blk, zpart, channels)
        part = part[:, :, 0] + ppermute_xor(part[:, :, 1], "wa", n_wa, bit)
        bit *= 2
    part = part[:, 0]
    part = part[0] + ppermute_xor(part[1], "wa", n_wa, n_zl)
    zh_grad = lax.ppermute(part, ("ha", "wa"), moves).transpose(1, 0, 2)
    w = w_keep + ppermute_xor(core_send[cols_blk:], "ha", n_ha, 1)
    bit = 2
    while bit < n_ha:
        w = w + ppermute_xor(w, "ha", n_ha, bit)
        bit *= 2
    bit = 1
    while bit < n_wa:
        w = w + ppermute_xor(w, "wa", n_wa, bit)
        bit *= 2
    w_other = ppermute_xor(w, "ha", n_ha, 1)
    w, w_other = [jnp.concatenate(jnp.split(v.reshape(2 * mid, 128), 2), axis=1) for v in (w, w_other)]
    upper = ha % 2 == 1
    wgt = jnp.concatenate([jnp.where(upper, w_other, w), jnp.where(upper, w, w_other)])
    first = channels + 8
    return (hw_grad, zh_grad, wz_grad, wgt[:channels], wgt[channels],
            wgt[first:first + classes].T, wgt[channels + 1, :classes])


def solution(mesh):
    placed = (
        P("ha", "wa", None),
        P(None, "ha", None),
        P("wa", None, None),
        P(),
        P(),
        P(),
        P(),
        P(("ha", "wa"), None),
        P(("ha", "wa")),
        P(("ha", "wa"), None, None),
    )
    return jax.shard_map(
        functools.partial(local, mesh.shape["ha"], mesh.shape["wa"]),
        mesh=mesh,
        in_specs=placed,
        out_specs=(
            P("ha", "wa", None),
            P("wa", "ha", None),
            P("wa", "ha", None),
            P(),
            P(),
            P(),
            P(),
        ),
        check_vma=False,
    )
```
